128 devices in a mesh: row: 32 (over z, y, core), col: 4 (over x).
Axes of the slice: x: 4, y: 4, z: 4, core: 2. Of those that a mesh axis runs over, the one named last changes fastest.
Arguments:
- rhs: bfloat16 [8, 32, 64, 128], P(None, 'row'), may hold values from -6 to 6
- boundary: bfloat16 [512, 64, 128], P('row'), may hold values from -6 to 6
- diag_inv: bfloat16 [8, 32, 128, 128], P(None, 'row'), may hold values from -0.5 to 0.5
- off_blocks: bfloat16 [7, 32, 128, 128, 128], P(None, 'row', 'col'), may hold values from -0.09375 to 0.09375
- coupling: int32 [7, 32, 128], P(None, 'row', 'col'), may hold values from 0 to 735, as said below
- present: int32 [7, 32, 128], P(None, 'row', 'col'), may hold values 0 or 1
Outputs:
- solution: bfloat16 [8, 32, 64, 128], P(None, 'row')
The draws below stay inside these ranges and needn't reach their ends.
Inputs may be any that keep to these rules, and one draw needn't show every extreme that they name: coupling[l, q, k] is below 512 + (l + 1) * 32: it names a boundary block or a block of an earlier level; the slots of one block row name distinct blocks.
All inputs are finite; a program needn't handle non-finite values. No bound on the sum of `present` on one device may be relied on, other than what follows from the above.
Results may differ from the reference program's by a relative error of at most 0.012.
Values may be sent and summed in bfloat16 or wider, within the bound.
No kernel may reach another device: no remote copies, remote signals or barrier semaphores. Data moves between devices by JAX's collectives and lax.ppermute only.
A program may use at most 128 MiB of HBM per device.

```python
import jax
import jax.numpy as jnp
from jax import lax

BLOCK = 128
RHS_COLS = 64
LEVELS = 8
LEVEL_BLOCKS = 32
OUTER_BLOCKS = 512
COUPLINGS = 128


def draw_coupling(key, part):
    key = jax.random.fold_in(key, 11)
    total = OUTER_BLOCKS + (LEVELS - 1) * LEVEL_BLOCKS
    raw = jax.random.randint(key, (LEVELS - 1, LEVEL_BLOCKS, total), 0, 1 << 14)
    position = jnp.arange(total, dtype=jnp.int32)
    limit = OUTER_BLOCKS + (jnp.arange(LEVELS - 1, dtype=jnp.int32) + 1) * LEVEL_BLOCKS
    scores = raw * total + position[None, None, :]
    top = (1 << 14) * total
    scores = scores.at[LEVELS - 2, 0, total - 1].set(top + 1)
    scores = scores.at[0, 0, 0].set(top + 2)
    scores = jnp.where(position[None, None, :] < limit[:, None, None], scores, -1)
    values, picked = lax.top_k(scores, COUPLINGS)
    return picked.astype(jnp.int32)


def place_ends(values, stream_key, least, top_value):
    longest = values.shape.index(max(values.shape))
    spots = []
    for shift in (0, 1):
        where = [jax.random.randint(jax.random.fold_in(stream_key, axis), (), 0, length) for axis, length in enumerate(values.shape)]
        where[longest] = (where[longest] + shift) % values.shape[longest]
        spots.append(tuple(where))
    return values.at[spots[0]].set(least).at[spots[1]].set(top_value)


def levels(rng, dims, shards, low, high):
    loudness, own = 1.0, jax.random.fold_in(rng, 6)
    for dim, shards_of in shards:
        heights = jnp.exp(jax.random.uniform(jax.random.fold_in(own, dim), (shards_of,), jnp.float32, low / len(shards), high / len(shards)))
        loudness = loudness * jnp.repeat(heights, dims[dim] // shards_of).reshape([-1 if axis == dim else 1 for axis in range(len(dims))])
    return loudness


def normal_values(rng, extent, deviation, reach, pieces=(), held_as=jnp.bfloat16):
    entries = deviation * jax.random.normal(rng, extent, jnp.float32)
    if pieces:
        entries = entries * levels(rng, extent, pieces, -0.22, 0.18)
    return jnp.clip(entries, -reach, reach).astype(held_as)


def setup_inputs(seed: int = 0) -> dict:
    splits = jax.random.split(jax.random.key(seed), 7)
    return {
        "rhs": normal_values(splits[0], (LEVELS, LEVEL_BLOCKS, RHS_COLS, BLOCK), 1.0, 6.0, ((1, 32),)),
        "boundary": normal_values(splits[1], (OUTER_BLOCKS, RHS_COLS, BLOCK), 1.0, 6.0, ((0, 32),)),
        "diag_inv": normal_values(splits[2], (LEVELS, LEVEL_BLOCKS, BLOCK, BLOCK), BLOCK ** -0.5, 0.5, ((1, 32),)),
        "off_blocks": normal_values(splits[3], (LEVELS - 1, LEVEL_BLOCKS, COUPLINGS, BLOCK, BLOCK), (2 * BLOCK * COUPLINGS // 9) ** -0.5, 0.09375, ((1, 32), (2, 4))),
        "coupling": draw_coupling(jax.random.fold_in(splits[6], 71), 0),
        "present": place_ends((jax.random.randint(splits[5], (LEVELS - 1, LEVEL_BLOCKS, COUPLINGS), 0, 4) < 3).astype(jnp.int32), jax.random.fold_in(splits[5], 1), 0, 1),
    }


def reference(rhs, boundary, diag_inv, off_blocks, coupling, present):
    width = rhs.shape[1]
    outer = boundary.shape[0]
    empty = jnp.zeros((LEVELS * width, rhs.shape[2], rhs.shape[3]), jnp.bfloat16)
    solved = jnp.concatenate([boundary, empty], axis=0)
    results = []
    for level in range(LEVELS):
        target = rhs[level].astype(jnp.float32)
        if level > 0:
            current = solved

            def row_term(args):
                blocks, index, keep = args
                picked = jnp.take(current, index, axis=0).astype(jnp.float32)
                picked = picked * keep.astype(jnp.float32)[:, None, None]
                return jnp.einsum("kab,krb->ra", blocks.astype(jnp.float32), picked, precision=lax.Precision.HIGHEST)

            target = target - lax.map(row_term, (off_blocks[level - 1], coupling[level - 1], present[level - 1]))
        reduced = target.astype(jnp.bfloat16)
        fresh = jnp.einsum("irb,iab->ira", reduced.astype(jnp.float32), diag_inv[level].astype(jnp.float32), precision=lax.Precision.HIGHEST).astype(jnp.bfloat16)
        solved = solved.at[outer + level * width:outer + (level + 1) * width].set(fresh)
        results.append(fresh)
    return jnp.stack(results)
```

```python
import jax
import jax.numpy as jnp
from jax import lax
from jax.experimental import pallas as pl
from jax.experimental.pallas import tpu as pltpu
from jax.sharding import Mesh, PartitionSpec as P

ROWS = ("z", "y", "core")
VMEM_LIMIT = 48 * 1024 * 1024


def xor_pairs(n, k):
    return [(i, i ^ k) for i in range(n)]


def shift_pairs(n, k):
    return [(i, (i + k) % n) for i in range(n)]


def swap_cores(v):
    return lax.ppermute(v, "core", xor_pairs(2, 1))


def direct_gather(v, axis):
    return jnp.concatenate([v] + [lax.ppermute(v, axis, xor_pairs(4, k)) for k in (1, 2, 3)])


def ring_gather(v, axis):
    before = lax.ppermute(v, axis, shift_pairs(4, 1))
    after = lax.ppermute(v, axis, shift_pairs(4, 3))
    half = v.shape[0] // 2
    far_a = lax.ppermute(before[:half], axis, shift_pairs(4, 1))
    far_b = lax.ppermute(after[half:], axis, shift_pairs(4, 3))
    return jnp.concatenate([v, before, after, far_a, far_b])


def nt_dot(x, a):
    return lax.dot_general(x, a, (((1,), (1,)), ((), ())), preferred_element_type=jnp.float32)


GROUP = 8


def old_kernel(code_ref, *refs):
    sources, (own_ref, other_ref, out_ref, picked, sem) = refs[:-5], refs[-5:]
    slots = code_ref.shape[0]

    for k in range(slots):
        code = jnp.maximum(code_ref[k], 0)
        which, place = code // 1024, code % 1024
        if len(sources) == 1:
            pltpu.make_async_copy(sources[0].at[place], picked.at[k], sem).start()
        else:
            for s, source in enumerate(sources):

                @pl.when(which == s)
                def _(source=source, k=k, place=place):
                    pltpu.make_async_copy(source.at[place], picked.at[k], sem).start()

    pltpu.make_async_copy(sources[0].at[pl.ds(0, slots)], picked, sem).wait()
    per_row = slots // 2
    for r, a_ref in enumerate((own_ref, other_ref)):
        total = None
        for g in range(0, per_row, GROUP):
            xs, blocks = [], []
            for k in range(g, g + GROUP):
                kept = (code_ref[r * per_row + k] >= 0).astype(jnp.float32)
                xs.append((picked[r * per_row + k].astype(jnp.float32) * kept).astype(jnp.bfloat16))
                blocks.append(a_ref[0, 0, k])
            part = nt_dot(jnp.concatenate(xs, axis=1), jnp.concatenate(blocks, axis=1))
            total = part if total is None else total + part
        out_ref[r] = total


def old_sum(level, code, sources, own, other):
    slots, (rhs_cols, block) = code.shape[0], sources[0].shape[1:]
    per_row = slots // 2
    a_spec = pl.BlockSpec((1, 1, per_row, block, block), lambda i: (level - 1, 0, 0, 0, 0))
    return pl.pallas_call(
        old_kernel,
        grid=(1,),
        out_shape=jax.ShapeDtypeStruct((2, rhs_cols, block), jnp.float32),
        in_specs=[pl.BlockSpec(memory_space=pltpu.SMEM)]
        + [pl.BlockSpec(memory_space=pl.ANY)] * len(sources)
        + [a_spec, a_spec],
        out_specs=pl.BlockSpec((2, rhs_cols, block), lambda i: (0, 0, 0)),
        scratch_shapes=[pltpu.VMEM((slots, rhs_cols, block), jnp.bfloat16), pltpu.SemaphoreType.DMA],
        compiler_params=pltpu.CompilerParams(vmem_limit_bytes=VMEM_LIMIT),
        cost_estimate=pl.CostEstimate(
            flops=2 * slots * rhs_cols * block * block,
            bytes_accessed=slots * block * (block + 2 * rhs_cols) * 4,
            transcendentals=0,
        ),
        name="old_sum",
    )(code, *sources, own, other)


def fresh_kernel(code_ref, x_ref, old_ref, own_ref, other_ref, out_ref):
    per_row = code_ref.shape[0] // 2
    for r, a_ref in enumerate((own_ref, other_ref)):
        out_ref[r] = old_ref[r]

        def add(k, carry, r=r, a_ref=a_ref):
            code = code_ref[r * per_row + k]

            @pl.when(code >= 0)
            def _():
                out_ref[r] += nt_dot(x_ref[code], a_ref[0, 0, k])

            return carry

        lax.fori_loop(0, per_row, add, 0)


def fresh_sum(level, code, solved, old, own, other):
    slots, (rhs_cols, block) = code.shape[0], solved.shape[1:]
    per_row = slots // 2
    a_spec = pl.BlockSpec((1, 1, per_row, block, block), lambda i: (level - 1, 0, 0, 0, 0))
    whole = lambda shape: pl.BlockSpec(shape, lambda i: (0,) * len(shape))
    return pl.pallas_call(
        fresh_kernel,
        grid=(1,),
        out_shape=jax.ShapeDtypeStruct(old.shape, jnp.float32),
        in_specs=[pl.BlockSpec(memory_space=pltpu.SMEM), whole(solved.shape), whole(old.shape), a_spec, a_spec],
        out_specs=whole(old.shape),
        compiler_params=pltpu.CompilerParams(vmem_limit_bytes=VMEM_LIMIT),
        cost_estimate=pl.CostEstimate(
            flops=2 * 8 * rhs_cols * block * block, bytes_accessed=slots * block * block * 2, transcendentals=0
        ),
        name="fresh_sum",
    )(code, solved, old, own, other)


def solve_kernel(core_ref, p0, p1, p2, p3, rhs_ref, own_d_ref, other_d_ref, out_ref, all_ref):
    core = core_ref[0]
    for r, d_ref in enumerate((own_d_ref, other_d_ref)):
        coupled = (p0[r] + p1[r]) + (p2[r] + p3[r])
        reduced = (rhs_ref[0, r].astype(jnp.float32) - coupled).astype(jnp.bfloat16)
        solved = nt_dot(reduced, d_ref[0, 0]).astype(jnp.bfloat16)
        out_ref[r] = solved
        if all_ref is not None:
            row = core ^ r
            for i in range(all_ref.shape[0]):
                all_ref[i, row] = solved


def solve_level(level, core, partials, rhs, own_d, other_d, copies):
    _, rhs_cols, block = partials[0].shape
    whole = lambda shape: pl.BlockSpec(shape, lambda i: (0,) * len(shape))
    d_spec = pl.BlockSpec((1, 1, block, block), lambda i: (level, 0, 0, 0))
    d2_spec = pl.BlockSpec((1, 1, block, block), lambda i: (level, 0, 0, 0))
    out_shape = [jax.ShapeDtypeStruct((2, rhs_cols, block), jnp.bfloat16)]
    if copies:
        out_shape.append(jax.ShapeDtypeStruct((copies, 2, rhs_cols, block), jnp.bfloat16))
        body = solve_kernel
    else:
        body = lambda *refs: solve_kernel(*refs, None)
    return pl.pallas_call(
        body,
        grid=(1,),
        out_shape=out_shape,
        in_specs=[pl.BlockSpec(memory_space=pltpu.SMEM)]
        + [whole(partials[0].shape)] * 4
        + [pl.BlockSpec((1, 2, rhs_cols, block), lambda i: (level, 0, 0, 0)), d_spec, d2_spec],
        out_specs=[whole(s.shape) for s in out_shape],
        compiler_params=pltpu.CompilerParams(vmem_limit_bytes=VMEM_LIMIT),
        name="solve_level",
    )(core, *partials, rhs, own_d, other_d)


def on_device(rhs, boundary, diag_inv, off_blocks, coupling, present):
    levels, _, rhs_cols, block = rhs.shape
    outer_each = boundary.shape[0]
    outer = outer_each * 32
    half = rhs_cols // 2
    z, y, core = lax.axis_index("z"), lax.axis_index("y"), lax.axis_index("core")

    def my_half(v, axis):
        return lax.dynamic_slice_in_dim(v, core * half, half, axis)

    def their_half(v, axis):
        return lax.dynamic_slice_in_dim(v, (1 - core) * half, half, axis)

    first = jnp.einsum("rb,ab->ra", rhs[0, 0], diag_inv[0, 0], preferred_element_type=jnp.float32).astype(jnp.bfloat16)
    known = jnp.concatenate([boundary, first[None]])
    known_own = my_half(known, 1)
    known_other = swap_cores(their_half(known, 1))
    color_a = ring_gather(direct_gather(known_own, "z"), "y")
    color_b = ring_gather(direct_gather(known_other, "y"), "z")
    store = jnp.concatenate([color_a, color_b])

    code_own = (coupling + 1024 * present)[:, 0]
    code_both = jnp.stack([code_own, swap_cores(code_own)], axis=1)
    rhs_both = jnp.concatenate([my_half(rhs, 2), swap_cores(their_half(rhs, 2))], axis=1)
    diag_other = swap_cores(diag_inv)
    off_other = swap_cores(off_blocks)

    keep, index = code_both >= 1024, code_both % 1024
    in_outer = index < outer
    row = jnp.where(in_outer, index // outer_each, index - outer)
    member = jnp.where(in_outer, index % outer_each, outer_each)
    src_z, src_y, src_core = row // 8, (row // 2) % 4, row % 2
    each = outer_each + 1
    ring_place = lambda d: jnp.where(d == 3, 1, jnp.where(d == 1, 2, jnp.where(d == 2, 3, 0)))
    place_a = ring_place((src_y - y) % 4) * 4 + (src_z ^ z)
    place_b = 16 + ring_place((src_z - z) % 4) * 4 + (src_y ^ y)
    place_known = jnp.where(src_core == core, place_a, place_b) * each + member
    level_of = jnp.maximum(index - outer, 0) // 32
    code = jnp.where(level_of == 0, place_known, level_of * 1024 + (index - outer) % 32)
    this = jnp.arange(levels - 1)[:, None, None]
    is_fresh = (level_of == this) & (level_of > 0)
    old_code = jnp.where(keep & ~is_fresh, code, -1).reshape(levels - 1, -1)
    fresh_code = jnp.where(keep & is_fresh, code % 1024, -1).reshape(levels - 1, -1)

    core_arr = jnp.reshape(core, (1,)).astype(jnp.int32)
    sources = [store]
    own_rows, other_rows = [], []
    value = old_sum(1, old_code[0], sources, off_blocks, off_other)
    for level in range(1, levels):
        partials = [value] + [lax.ppermute(value, "x", xor_pairs(4, k)) for k in (1, 2, 3)]
        last = level == levels - 1
        if not last:
            next_code, value = lax.optimization_barrier((old_code[level], value))
            old = old_sum(level + 1, next_code, sources, off_blocks, off_other)
        outs = solve_level(level, core_arr, partials, rhs_both, diag_inv, diag_other, 0 if last else 16)
        own_rows.append(outs[0][0])
        other_rows.append(outs[0][1])
        if not last:
            solved = lax.all_to_all(outs[1], ("z", "y"), 0, 0).reshape(32, half, block)
            value = fresh_sum(level + 1, fresh_code[level], solved, old, off_blocks, off_other)
            sources = sources + [solved]

    mine = jnp.stack(own_rows)
    theirs = swap_cores(jnp.stack(other_rows))
    low = jnp.where(core == 0, mine, theirs)
    high = jnp.where(core == 0, theirs, mine)
    rest = jnp.concatenate([low, high], axis=1)
    return jnp.concatenate([first[None], rest])[:, None]


def solution(mesh):
    split = Mesh(mesh.devices.reshape(4, 4, 2, 4), ("z", "y", "core", "x"))
    in_specs = (
        P(None, ROWS, None, None),
        P(ROWS, None, None),
        P(None, ROWS, None, None),
        P(None, ROWS, "x", None, None),
        P(None, ROWS, "x"),
        P(None, ROWS, "x"),
    )
    return jax.shard_map(
        on_device, mesh=split, in_specs=in_specs, out_specs=P(None, ROWS, None, None), check_vma=False
    )
```

```python
import jax
import jax.numpy as jnp
from jax import lax
from jax.experimental import pallas as pl
from jax.experimental.pallas import tpu as pltpu
from jax.sharding import Mesh, PartitionSpec as P

ROWS = ("z", "y", "core")
VMEM_LIMIT = 48 * 1024 * 1024


def xor_pairs(n, k):
    return [(i, i ^ k) for i in range(n)]


def shift_pairs(n, k):
    return [(i, (i + k) % n) for i in range(n)]


def swap_cores(v):
    return lax.ppermute(v, "core", xor_pairs(2, 1))


def direct_gather(v, axis):
    return jnp.concatenate([v] + [lax.ppermute(v, axis, xor_pairs(4, k)) for k in (1, 2, 3)])


def ring_gather(v, axis):
    before = lax.ppermute(v, axis, shift_pairs(4, 1))
    after = lax.ppermute(v, axis, shift_pairs(4, 3))
    half = v.shape[0] // 2
    far_a = lax.ppermute(before[:half], axis, shift_pairs(4, 1))
    far_b = lax.ppermute(after[half:], axis, shift_pairs(4, 3))
    return [v, before, after, far_a, far_b]


def nt_dot(x, a):
    return lax.dot_general(x, a, (((1,), (1,)), ((), ())), preferred_element_type=jnp.float32)


GROUP = 8


def pick(sources, first, which, place, target, sem):
    if len(sources) == 1:
        pltpu.make_async_copy(sources[0].at[place], target, sem).start()
        return
    middle = len(sources) // 2

    @pl.when(which < first + middle)
    def _():
        pick(sources[:middle], first, which, place, target, sem)

    @pl.when(which >= first + middle)
    def _():
        pick(sources[middle:], first + middle, which, place, target, sem)


def old_kernel(code_ref, *refs):
    sources, (own_ref, other_ref, out_ref, picked, sem) = refs[:-5], refs[-5:]
    slots = code_ref.shape[0]

    for k in range(slots):
        code = jnp.maximum(code_ref[k], 0)
        which, place = code // 1024, code % 1024
        pick(sources, 0, which, place, picked.at[k], sem)

    pltpu.make_async_copy(sources[0].at[pl.ds(0, slots)], picked, sem).wait()
    per_row = slots // 2
    for r, a_ref in enumerate((own_ref, other_ref)):
        total = None
        for g in range(0, per_row, GROUP):
            xs, blocks = [], []
            for k in range(g, g + GROUP):
                kept = (code_ref[r * per_row + k] >= 0).astype(jnp.float32)
                xs.append((picked[r * per_row + k].astype(jnp.float32) * kept).astype(jnp.bfloat16))
                blocks.append(a_ref[0, 0, k])
            part = nt_dot(jnp.concatenate(xs, axis=1), jnp.concatenate(blocks, axis=1))
            total = part if total is None else total + part
        out_ref[r] = total


def old_sum(level, code, sources, own, other):
    slots, (rhs_cols, block) = code.shape[0], sources[0].shape[1:]
    per_row = slots // 2
    a_spec = pl.BlockSpec((1, 1, per_row, block, block), lambda i: (level - 1, 0, 0, 0, 0))
    return pl.pallas_call(
        old_kernel,
        grid=(1,),
        out_shape=jax.ShapeDtypeStruct((2, rhs_cols, block), jnp.float32),
        in_specs=[pl.BlockSpec(memory_space=pltpu.SMEM)]
        + [pl.BlockSpec(memory_space=pl.ANY)] * len(sources)
        + [a_spec, a_spec],
        out_specs=pl.BlockSpec((2, rhs_cols, block), lambda i: (0, 0, 0)),
        scratch_shapes=[pltpu.VMEM((slots, rhs_cols, block), jnp.bfloat16), pltpu.SemaphoreType.DMA],
        compiler_params=pltpu.CompilerParams(vmem_limit_bytes=VMEM_LIMIT),
        cost_estimate=pl.CostEstimate(
            flops=2 * slots * rhs_cols * block * block,
            bytes_accessed=slots * block * (block + 2 * rhs_cols) * 4,
            transcendentals=0,
        ),
        name="old_sum",
    )(code, *sources, own, other)


def fresh_kernel(code_ref, x_ref, old_ref, own_ref, other_ref, out_ref):
    per_row = code_ref.shape[0] // 2
    for r, a_ref in enumerate((own_ref, other_ref)):
        out_ref[r] = old_ref[r]

        def add(k, carry, r=r, a_ref=a_ref):
            code = code_ref[r * per_row + k]

            @pl.when(code >= 0)
            def _():
                out_ref[r] += nt_dot(x_ref[code], a_ref[0, 0, k])

            return carry

        lax.fori_loop(0, per_row, add, 0)


def fresh_sum(level, code, solved, old, own, other):
    slots, (rhs_cols, block) = code.shape[0], solved.shape[1:]
    per_row = slots // 2
    a_spec = pl.BlockSpec((1, 1, per_row, block, block), lambda i: (level - 1, 0, 0, 0, 0))
    whole = lambda shape: pl.BlockSpec(shape, lambda i: (0,) * len(shape))
    return pl.pallas_call(
        fresh_kernel,
        grid=(1,),
        out_shape=jax.ShapeDtypeStruct(old.shape, jnp.float32),
        in_specs=[pl.BlockSpec(memory_space=pltpu.SMEM), whole(solved.shape), whole(old.shape), a_spec, a_spec],
        out_specs=whole(old.shape),
        compiler_params=pltpu.CompilerParams(vmem_limit_bytes=VMEM_LIMIT),
        cost_estimate=pl.CostEstimate(
            flops=2 * 8 * rhs_cols * block * block, bytes_accessed=slots * block * block * 2, transcendentals=0
        ),
        name="fresh_sum",
    )(code, solved, old, own, other)


def solve_kernel(core_ref, p0, p1, p2, p3, rhs_ref, own_d_ref, other_d_ref, out_ref, all_ref):
    core = core_ref[0]
    for r, d_ref in enumerate((own_d_ref, other_d_ref)):
        coupled = (p0[r] + p1[r]) + (p2[r] + p3[r])
        reduced = (rhs_ref[0, r].astype(jnp.float32) - coupled).astype(jnp.bfloat16)
        solved = nt_dot(reduced, d_ref[0, 0]).astype(jnp.bfloat16)
        out_ref[r] = solved
        if all_ref is not None:
            row = core ^ r
            for i in range(all_ref.shape[0]):
                all_ref[i, row] = solved


def solve_level(level, core, partials, rhs, own_d, other_d, copies):
    _, rhs_cols, block = partials[0].shape
    whole = lambda shape: pl.BlockSpec(shape, lambda i: (0,) * len(shape))
    d_spec = pl.BlockSpec((1, 1, block, block), lambda i: (level, 0, 0, 0))
    d2_spec = pl.BlockSpec((1, 1, block, block), lambda i: (level, 0, 0, 0))
    out_shape = [jax.ShapeDtypeStruct((2, rhs_cols, block), jnp.bfloat16)]
    if copies:
        out_shape.append(jax.ShapeDtypeStruct((copies, 2, rhs_cols, block), jnp.bfloat16))
        body = solve_kernel
    else:
        body = lambda *refs: solve_kernel(*refs, None)
    return pl.pallas_call(
        body,
        grid=(1,),
        out_shape=out_shape,
        in_specs=[pl.BlockSpec(memory_space=pltpu.SMEM)]
        + [whole(partials[0].shape)] * 4
        + [pl.BlockSpec((1, 2, rhs_cols, block), lambda i: (level, 0, 0, 0)), d_spec, d2_spec],
        out_specs=[whole(s.shape) for s in out_shape],
        compiler_params=pltpu.CompilerParams(vmem_limit_bytes=VMEM_LIMIT),
        name="solve_level",
    )(core, *partials, rhs, own_d, other_d)


def on_device(rhs, boundary, diag_inv, off_blocks, coupling, present):
    levels, _, rhs_cols, block = rhs.shape
    outer_each = boundary.shape[0]
    outer = outer_each * 32
    half = rhs_cols // 2
    z, y, core = lax.axis_index("z"), lax.axis_index("y"), lax.axis_index("core")

    def my_half(v, axis):
        return lax.dynamic_slice_in_dim(v, core * half, half, axis)

    def their_half(v, axis):
        return lax.dynamic_slice_in_dim(v, (1 - core) * half, half, axis)

    first = jnp.einsum("rb,ab->ra", rhs[0, 0], diag_inv[0, 0], preferred_element_type=jnp.float32).astype(jnp.bfloat16)
    known = jnp.concatenate([boundary, first[None]])
    known_own = my_half(known, 1)
    known_own, known_other = lax.optimization_barrier((known_own, swap_cores(their_half(known, 1))))
    color_a = ring_gather(direct_gather(known_own, "z"), "y")
    color_b = ring_gather(direct_gather(known_other, "y"), "z")

    code_own = (coupling + 1024 * present)[:, 0]
    code_both = jnp.stack([code_own, swap_cores(code_own)], axis=1)
    rhs_both = jnp.concatenate([my_half(rhs, 2), swap_cores(their_half(rhs, 2))], axis=1)
    diag_other = swap_cores(diag_inv)
    off_other = swap_cores(off_blocks)

    keep, index = code_both >= 1024, code_both % 1024
    in_outer = index < outer
    row = jnp.where(in_outer, index // outer_each, index - outer)
    member = jnp.where(in_outer, index % outer_each, outer_each)
    src_z, src_y, src_core = row // 8, (row // 2) % 4, row % 2
    each = outer_each + 1
    mine_too = src_core == core
    away = jnp.where(mine_too, src_y - y, src_z - z) % 4
    place = jnp.where(mine_too, src_z ^ z, src_y ^ y) * each + member
    far_half = (away == 2) & (place >= 2 * each)
    piece = jnp.where(away == 3, 1, jnp.where(away == 1, 2, jnp.where(away == 2, 3, 0))) + far_half
    place = jnp.where(far_half, place - 2 * each, place)
    code_known = (piece + jnp.where(mine_too, 0, 5)) * 1024 + place
    level_of = jnp.maximum(index - outer, 0) // 32
    code = jnp.where(level_of == 0, code_known, (9 + level_of) * 1024 + (index - outer) % 32)
    this = jnp.arange(levels - 1)[:, None, None]
    is_fresh = (level_of == this) & (level_of > 0)
    old_code = jnp.where(keep & ~is_fresh, code, -1).reshape(levels - 1, -1)
    fresh_code = jnp.where(keep & is_fresh, code % 1024, -1).reshape(levels - 1, -1)

    core_arr = jnp.reshape(core, (1,)).astype(jnp.int32)
    sources = color_a + color_b
    own_rows, other_rows = [], []
    value = old_sum(1, old_code[0], sources, off_blocks, off_other)
    for level in range(1, levels):
        partials = [value] + [lax.ppermute(value, "x", xor_pairs(4, k)) for k in (1, 2, 3)]
        last = level == levels - 1
        if not last:
            next_code, value = lax.optimization_barrier((old_code[level], value))
            old = old_sum(level + 1, next_code, sources, off_blocks, off_other)
        outs = solve_level(level, core_arr, partials, rhs_both, diag_inv, diag_other, 0 if last else 16)
        own_rows.append(outs[0][0])
        other_rows.append(outs[0][1])
        if not last:
            solved = lax.all_to_all(outs[1], ("z", "y"), 0, 0).reshape(32, half, block)
            value = fresh_sum(level + 1, fresh_code[level], solved, old, off_blocks, off_other)
            sources = sources + [solved]

    mine = jnp.stack(own_rows)
    theirs = swap_cores(jnp.stack(other_rows))
    low = jnp.where(core == 0, mine, theirs)
    high = jnp.where(core == 0, theirs, mine)
    rest = jnp.concatenate([low, high], axis=1)
    return jnp.concatenate([first[None], rest])[:, None]


def solution(mesh):
    split = Mesh(mesh.devices.reshape(4, 4, 2, 4), ("z", "y", "core", "x"))
    in_specs = (
        P(None, ROWS, None, None),
        P(ROWS, None, None),
        P(None, ROWS, None, None),
        P(None, ROWS, "x", None, None),
        P(None, ROWS, "x"),
        P(None, ROWS, "x"),
    )
    return jax.shard_map(
        on_device, mesh=split, in_specs=in_specs, out_specs=P(None, ROWS, None, None), check_vma=False
    )
```

```python
import jax
import jax.numpy as jnp
from jax import lax
from jax.experimental import pallas as pl
from jax.experimental.pallas import tpu as pltpu
from jax.sharding import Mesh, PartitionSpec as P

ROWS = ("z", "y", "core")
VMEM_LIMIT = 16 * 1024 * 1024


def xor_pairs(n, k):
    return [(i, i ^ k) for i in range(n)]


def shift_pairs(n, k):
    return [(i, (i + k) % n) for i in range(n)]


def swap_cores(v):
    return lax.ppermute(v, "core", xor_pairs(2, 1))


def direct_gather(v, axis):
    return jnp.concatenate([v] + [lax.ppermute(v, axis, xor_pairs(4, k)) for k in (1, 2, 3)])


def ring_gather(v, axis):
    before = lax.ppermute(v, axis, shift_pairs(4, 1))
    after = lax.ppermute(v, axis, shift_pairs(4, 3))
    half = v.shape[0] // 2
    far_a = lax.ppermute(before[:half], axis, shift_pairs(4, 1))
    far_b = lax.ppermute(after[half:], axis, shift_pairs(4, 3))
    return [v, before, after, far_a, far_b]


def nt_dot(x, a):
    return lax.dot_general(x, a, (((1,), (1,)), ((), ())), preferred_element_type=jnp.float32)


GROUP = 8


def pick(sources, first, which, place, target, sem):
    if len(sources) == 1:
        pltpu.make_async_copy(sources[0].at[place], target, sem).start()
        return
    middle = len(sources) // 2

    @pl.when(which < first + middle)
    def _():
        pick(sources[:middle], first, which, place, target, sem)

    @pl.when(which >= first + middle)
    def _():
        pick(sources[middle:], first + middle, which, place, target, sem)


def old_kernel(code_ref, *refs):
    sources, (own_ref, other_ref, out_ref, picked, sem) = refs[:-5], refs[-5:]
    slots = code_ref.shape[0]

    for k in range(slots):
        code = jnp.maximum(code_ref[k], 0)
        which, place = code >> 10, code & 1023
        pick(sources, 0, which, place, picked.at[k], sem)

    pltpu.make_async_copy(sources[0].at[pl.ds(0, slots)], picked, sem).wait()
    per_row = slots // 2
    for r, a_ref in enumerate((own_ref, other_ref)):
        total = None
        for g in range(0, per_row, GROUP):
            xs, blocks = [], []
            for k in range(g, g + GROUP):
                kept = (code_ref[r * per_row + k] >= 0).astype(jnp.float32)
                xs.append((picked[r * per_row + k].astype(jnp.float32) * kept).astype(jnp.bfloat16))
                blocks.append(a_ref[0, 0, k])
            part = nt_dot(jnp.concatenate(xs, axis=1), jnp.concatenate(blocks, axis=1))
            total = part if total is None else total + part
        out_ref[r] = total


def old_sum(level, code, sources, own, other):
    slots, (rhs_cols, block) = code.shape[0], sources[0].shape[1:]
    per_row = slots // 2
    a_spec = pl.BlockSpec((1, 1, per_row, block, block), lambda i: (level - 1, 0, 0, 0, 0))
    return pl.pallas_call(
        old_kernel,
        grid=(1,),
        out_shape=jax.ShapeDtypeStruct((2, rhs_cols, block), jnp.float32),
        in_specs=[pl.BlockSpec(memory_space=pltpu.SMEM)]
        + [pl.BlockSpec(memory_space=pl.ANY)] * len(sources)
        + [a_spec, a_spec],
        out_specs=pl.BlockSpec((2, rhs_cols, block), lambda i: (0, 0, 0)),
        scratch_shapes=[pltpu.VMEM((slots, rhs_cols, block), jnp.bfloat16), pltpu.SemaphoreType.DMA],
        compiler_params=pltpu.CompilerParams(vmem_limit_bytes=VMEM_LIMIT),
        cost_estimate=pl.CostEstimate(
            flops=2 * slots * rhs_cols * block * block,
            bytes_accessed=slots * block * (block + 2 * rhs_cols) * 4,
            transcendentals=0,
        ),
        name="old_sum",
    )(code, *sources, own, other)


def fresh_kernel(code_ref, x_ref, old_ref, own_ref, other_ref, out_ref):
    per_row = code_ref.shape[0] // 2
    for r, a_ref in enumerate((own_ref, other_ref)):
        out_ref[r] = old_ref[r]

        def add(k, carry, r=r, a_ref=a_ref):
            code = code_ref[r * per_row + k]

            @pl.when(code >= 0)
            def _():
                out_ref[r] += nt_dot(x_ref[code], a_ref[0, 0, k])

            return carry

        lax.fori_loop(0, per_row, add, 0)


def fresh_sum(level, code, solved, old, own, other):
    slots, (rhs_cols, block) = code.shape[0], solved.shape[1:]
    per_row = slots // 2
    a_spec = pl.BlockSpec((1, 1, per_row, block, block), lambda i: (level - 1, 0, 0, 0, 0))
    whole = lambda shape: pl.BlockSpec(shape, lambda i: (0,) * len(shape))
    return pl.pallas_call(
        fresh_kernel,
        grid=(1,),
        out_shape=jax.ShapeDtypeStruct(old.shape, jnp.float32),
        in_specs=[pl.BlockSpec(memory_space=pltpu.SMEM), whole(solved.shape), whole(old.shape), a_spec, a_spec],
        out_specs=whole(old.shape),
        compiler_params=pltpu.CompilerParams(vmem_limit_bytes=VMEM_LIMIT),
        cost_estimate=pl.CostEstimate(
            flops=2 * 8 * rhs_cols * block * block, bytes_accessed=slots * block * block * 2, transcendentals=0
        ),
        name="fresh_sum",
    )(code, solved, old, own, other)


def solve_kernel(core_ref, p0, p1, p2, p3, rhs_ref, own_d_ref, other_d_ref, out_ref, all_ref):
    core = core_ref[0]
    for r, d_ref in enumerate((own_d_ref, other_d_ref)):
        coupled = (p0[r] + p1[r]) + (p2[r] + p3[r])
        reduced = (rhs_ref[0, r].astype(jnp.float32) - coupled).astype(jnp.bfloat16)
        solved = nt_dot(reduced, d_ref[0, 0]).astype(jnp.bfloat16)
        out_ref[r] = solved
        if all_ref is not None:
            row = core ^ r
            for i in range(all_ref.shape[0]):
                all_ref[i, row] = solved


def solve_level(level, core, partials, rhs, own_d, other_d, copies):
    _, rhs_cols, block = partials[0].shape
    whole = lambda shape: pl.BlockSpec(shape, lambda i: (0,) * len(shape))
    d_spec = pl.BlockSpec((1, 1, block, block), lambda i: (level, 0, 0, 0))
    d2_spec = pl.BlockSpec((1, 1, block, block), lambda i: (level, 0, 0, 0))
    out_shape = [jax.ShapeDtypeStruct((2, rhs_cols, block), jnp.bfloat16)]
    if copies:
        out_shape.append(jax.ShapeDtypeStruct((copies, 2, rhs_cols, block), jnp.bfloat16))
        body = solve_kernel
    else:
        body = lambda *refs: solve_kernel(*refs, None)
    return pl.pallas_call(
        body,
        grid=(1,),
        out_shape=out_shape,
        in_specs=[pl.BlockSpec(memory_space=pltpu.SMEM)]
        + [whole(partials[0].shape)] * 4
        + [pl.BlockSpec((1, 2, rhs_cols, block), lambda i: (level, 0, 0, 0)), d_spec, d2_spec],
        out_specs=[whole(s.shape) for s in out_shape],
        compiler_params=pltpu.CompilerParams(vmem_limit_bytes=VMEM_LIMIT),
        name="solve_level",
    )(core, *partials, rhs, own_d, other_d)


def on_device(rhs, boundary, diag_inv, off_blocks, coupling, present):
    levels, _, rhs_cols, block = rhs.shape
    outer_each = boundary.shape[0]
    outer = outer_each * 32
    half = rhs_cols // 2
    z, y, core = lax.axis_index("z"), lax.axis_index("y"), lax.axis_index("core")

    def my_half(v, axis):
        return lax.dynamic_slice_in_dim(v, core * half, half, axis)

    def their_half(v, axis):
        return lax.dynamic_slice_in_dim(v, (1 - core) * half, half, axis)

    first = jnp.einsum("rb,ab->ra", rhs[0, 0], diag_inv[0, 0], preferred_element_type=jnp.float32).astype(jnp.bfloat16)
    known = jnp.concatenate([boundary, first[None]])
    known_own = my_half(known, 1)
    known_own, known_other = lax.optimization_barrier((known_own, swap_cores(their_half(known, 1))))
    code_own = (coupling + 1024 * present)[:, 0]
    code_both = jnp.stack([code_own, swap_cores(code_own)], axis=1)
    rhs_both = jnp.concatenate([my_half(rhs, 2), swap_cores(their_half(rhs, 2))], axis=1)
    diag_other = swap_cores(diag_inv)
    off_sent, known_own = lax.optimization_barrier((off_blocks, known_own))
    off_other = swap_cores(off_sent)

    color_a = ring_gather(direct_gather(known_own, "z"), "y")
    color_b = ring_gather(direct_gather(known_other, "y"), "z")

    keep, index = code_both >= 1024, code_both % 1024
    in_outer = index < outer
    row = jnp.where(in_outer, index // outer_each, index - outer)
    member = jnp.where(in_outer, index % outer_each, outer_each)
    src_z, src_y, src_core = row // 8, (row // 2) % 4, row % 2
    each = outer_each + 1
    mine_too = src_core == core
    away = jnp.where(mine_too, src_y - y, src_z - z) % 4
    place = jnp.where(mine_too, src_z ^ z, src_y ^ y) * each + member
    far_half = (away == 2) & (place >= 2 * each)
    piece = jnp.where(away == 3, 1, jnp.where(away == 1, 2, jnp.where(away == 2, 3, 0))) + far_half
    place = jnp.where(far_half, place - 2 * each, place)
    code_known = (piece + jnp.where(mine_too, 0, 5)) * 1024 + place
    level_of = jnp.maximum(index - outer, 0) // 32
    code = jnp.where(level_of == 0, code_known, (9 + level_of) * 1024 + (index - outer) % 32)
    this = jnp.arange(levels - 1)[:, None, None]
    is_fresh = (level_of == this) & (level_of > 0)
    old_code = jnp.where(keep & ~is_fresh, code, -1).reshape(levels - 1, -1)
    fresh_code = jnp.where(keep & is_fresh, code % 1024, -1).reshape(levels - 1, -1)

    core_arr = jnp.reshape(core, (1,)).astype(jnp.int32)
    sources = color_a + color_b
    own_rows, other_rows = [], []
    value = old_sum(1, old_code[0], sources, off_blocks, off_other)
    for level in range(1, levels):
        partials = [value] + [lax.ppermute(value, "x", xor_pairs(4, k)) for k in (1, 2, 3)]
        last = level == levels - 1
        outs = solve_level(level, core_arr, partials, rhs_both, diag_inv, diag_other, 0 if last else 16)
        own_rows.append(outs[0][0])
        other_rows.append(outs[0][1])
        if not last:
            next_code, sent = lax.optimization_barrier((old_code[level], outs[1]))
            solved = lax.all_to_all(sent, ("z", "y"), 0, 0).reshape(32, half, block)
            old = old_sum(level + 1, next_code, sources, off_blocks, off_other)
            value = fresh_sum(level + 1, fresh_code[level], solved, old, off_blocks, off_other)
            sources = sources + [solved]

    mine = jnp.stack(own_rows)
    theirs = swap_cores(jnp.stack(other_rows))
    low = jnp.where(core == 0, mine, theirs)
    high = jnp.where(core == 0, theirs, mine)
    rest = jnp.concatenate([low, high], axis=1)
    return jnp.concatenate([first[None], rest])[:, None]


def solution(mesh):
    split = Mesh(mesh.devices.reshape(4, 4, 2, 4), ("z", "y", "core", "x"))
    in_specs = (
        P(None, ROWS, None, None),
        P(ROWS, None, None),
        P(None, ROWS, None, None),
        P(None, ROWS, "x", None, None),
        P(None, ROWS, "x"),
        P(None, ROWS, "x"),
    )
    return jax.shard_map(
        on_device, mesh=split, in_specs=in_specs, out_specs=P(None, ROWS, None, None), check_vma=False
    )
```

```python
import functools

import jax
import jax.numpy as jnp
from jax import lax
from jax.experimental import pallas as pl
from jax.experimental.pallas import tpu as pltpu
from jax.sharding import Mesh, PartitionSpec as P

ROWS = ("z", "y", "core")
VMEM_LIMIT = 24 * 1024 * 1024


def xor_pairs(n, k):
    return [(i, i ^ k) for i in range(n)]


def shift_pairs(n, k):
    return [(i, (i + k) % n) for i in range(n)]


def swap_cores(v):
    return lax.ppermute(v, "core", xor_pairs(2, 1))


def direct_gather(v, axis):
    return jnp.concatenate([v] + [lax.ppermute(v, axis, xor_pairs(4, k)) for k in (1, 2, 3)])


def ring_gather(v, axis):
    before = lax.ppermute(v, axis, shift_pairs(4, 1))
    after = lax.ppermute(v, axis, shift_pairs(4, 3))
    half = v.shape[0] // 2
    far_a = lax.ppermute(before[:half], axis, shift_pairs(4, 1))
    far_b = lax.ppermute(after[half:], axis, shift_pairs(4, 3))
    return [v, before, after, far_a, far_b]


def nt_dot(x, a):
    return lax.dot_general(x, a, (((1,), (1,)), ((), ())), preferred_element_type=jnp.float32)


GROUP = 8


def pick(sources, first, which, place, target, sem):
    if len(sources) == 1:
        pltpu.make_async_copy(sources[0].at[place], target, sem).start()
        return
    middle = len(sources) // 2

    @pl.when(which < first + middle)
    def _():
        pick(sources[:middle], first, which, place, target, sem)

    @pl.when(which >= first + middle)
    def _():
        pick(sources[middle:], first + middle, which, place, target, sem)


def old_kernel(level, code_ref, *refs):
    sources, (own_ref, other_ref, out_ref, picked, blocks, sem, block_sems) = refs[:-7], refs[-7:]
    slots = code_ref.shape[0]
    per_row = slots // 2
    loads = [
        pltpu.make_async_copy(a_ref.at[level - 1, 0], blocks.at[pl.ds(r * per_row, per_row)], block_sems.at[r])
        for r, a_ref in enumerate((own_ref, other_ref))
    ]
    for load in loads:
        load.start()

    def fetch(k, carry):
        code = jnp.maximum(code_ref[k], 0)
        pick(sources, 0, code >> 10, code & 1023, picked.at[k], sem)
        return carry

    lax.fori_loop(0, slots, fetch, 0)
    pltpu.make_async_copy(sources[0].at[pl.ds(0, slots)], picked, sem).wait()
    for r in range(2):
        loads[r].wait()
        total = None
        for g in range(r * per_row, (r + 1) * per_row, GROUP):
            xs, group = [], []
            for k in range(g, g + GROUP):
                kept = (code_ref[k] >= 0).astype(jnp.float32)
                xs.append((picked[k].astype(jnp.float32) * kept).astype(jnp.bfloat16))
                group.append(blocks[k])
            part = nt_dot(jnp.concatenate(xs, axis=1), jnp.concatenate(group, axis=1))
            total = part if total is None else total + part
        out_ref[r] = total


def old_sum(level, code, sources, own, other):
    slots, (rhs_cols, block) = code.shape[0], sources[0].shape[1:]
    return pl.pallas_call(
        functools.partial(old_kernel, level),
        out_shape=jax.ShapeDtypeStruct((2, rhs_cols, block), jnp.float32),
        in_specs=[pl.BlockSpec(memory_space=pltpu.SMEM)]
        + [pl.BlockSpec(memory_space=pl.ANY)] * len(sources)
        + [pl.BlockSpec(memory_space=pltpu.HBM)] * 2,
        out_specs=pl.BlockSpec(memory_space=pltpu.VMEM),
        scratch_shapes=[
            pltpu.VMEM((slots, rhs_cols, block), jnp.bfloat16),
            pltpu.VMEM((slots, block, block), jnp.bfloat16),
            pltpu.SemaphoreType.DMA,
            pltpu.SemaphoreType.DMA((2,)),
        ],
        compiler_params=pltpu.CompilerParams(vmem_limit_bytes=VMEM_LIMIT),
        cost_estimate=pl.CostEstimate(
            flops=2 * slots * rhs_cols * block * block,
            bytes_accessed=slots * block * (block + 2 * rhs_cols) * 4,
            transcendentals=0,
        ),
        name="old_sum",
    )(code, *sources, own, other)


def fresh_kernel(level, code_ref, old_ref, x_ref, own_ref, other_ref, out_ref, which, near_x, near_a, x_sems, a_sems):
    slots = code_ref.shape[0]
    per_row = slots // 2

    def fetch(slot, count):
        code = code_ref[slot]

        @pl.when(code >= 0)
        def _():
            which[count] = slot
            pltpu.make_async_copy(x_ref.at[code], near_x.at[count], x_sems.at[count]).start()

            @pl.when(slot < per_row)
            def _():
                pltpu.make_async_copy(own_ref.at[level - 1, 0, slot], near_a.at[count], a_sems.at[count]).start()

            @pl.when(slot >= per_row)
            def _():
                pltpu.make_async_copy(other_ref.at[level - 1, 0, slot - per_row], near_a.at[count], a_sems.at[count]).start()

        return count + (code >= 0).astype(jnp.int32)

    count = lax.fori_loop(0, slots, fetch, jnp.int32(0))
    out_ref[...] = old_ref[...]

    def add(n, carry):
        slot = which[n]
        pltpu.make_async_copy(x_ref.at[0], near_x.at[n], x_sems.at[n]).wait()
        pltpu.make_async_copy(own_ref.at[level - 1, 0, 0], near_a.at[n], a_sems.at[n]).wait()
        out_ref[(slot >= per_row).astype(jnp.int32)] += nt_dot(near_x[n], near_a[n])
        return carry

    lax.fori_loop(0, count, add, 0)


def fresh_sum(level, code, solved, old, own, other):
    slots, (rhs_cols, block) = code.shape[0], solved.shape[1:]
    return pl.pallas_call(
        functools.partial(fresh_kernel, level),
        out_shape=jax.ShapeDtypeStruct(old.shape, jnp.float32),
        in_specs=[
            pl.BlockSpec(memory_space=pltpu.SMEM),
            pl.BlockSpec(memory_space=pltpu.VMEM),
            pl.BlockSpec(memory_space=pl.ANY),
            pl.BlockSpec(memory_space=pltpu.HBM),
            pl.BlockSpec(memory_space=pltpu.HBM),
        ],
        out_specs=pl.BlockSpec(memory_space=pltpu.VMEM),
        scratch_shapes=[
            pltpu.SMEM((slots,), jnp.int32),
            pltpu.VMEM((slots, rhs_cols, block), jnp.bfloat16),
            pltpu.VMEM((slots, block, block), jnp.bfloat16),
            pltpu.SemaphoreType.DMA((slots,)),
            pltpu.SemaphoreType.DMA((slots,)),
        ],
        compiler_params=pltpu.CompilerParams(vmem_limit_bytes=VMEM_LIMIT),
        cost_estimate=pl.CostEstimate(
            flops=2 * 8 * rhs_cols * block * block, bytes_accessed=slots * block * block * 2, transcendentals=0
        ),
        name="fresh_sum",
    )(code, old, solved, own, other)


def solve_kernel(core_ref, p0, p1, p2, p3, rhs_ref, own_d_ref, other_d_ref, out_ref, *refs):
    for r, d_ref in enumerate((own_d_ref, other_d_ref)):
        coupled = (p0[r] + p1[r]) + (p2[r] + p3[r])
        reduced = (rhs_ref[r].astype(jnp.float32) - coupled).astype(jnp.bfloat16)
        solved = nt_dot(reduced, d_ref[...]).astype(jnp.bfloat16)
        out_ref[r] = solved
        if refs:
            refs[1][core_ref[0] ^ r] = solved
    if refs:
        all_ref, both, sems = refs
        sends = [pltpu.make_async_copy(both, all_ref.at[i], sems.at[i]) for i in range(all_ref.shape[0])]
        for send in sends:
            send.start()
        for send in sends:
            send.wait()


def solve_level(level, core, partials, rhs, own_d, other_d, copies):
    _, rhs_cols, block = partials[0].shape
    vmem = pl.BlockSpec(memory_space=pltpu.VMEM)
    out_shape, out_specs, scratch = [jax.ShapeDtypeStruct((2, rhs_cols, block), jnp.bfloat16)], [vmem], []
    if copies:
        out_shape.append(jax.ShapeDtypeStruct((copies, 2, rhs_cols, block), jnp.bfloat16))
        out_specs.append(pl.BlockSpec(memory_space=pltpu.HBM))
        scratch = [pltpu.VMEM((2, rhs_cols, block), jnp.bfloat16), pltpu.SemaphoreType.DMA((copies,))]
    return pl.pallas_call(
        solve_kernel,
        out_shape=out_shape,
        in_specs=[pl.BlockSpec(memory_space=pltpu.SMEM)] + [vmem] * 7,
        out_specs=out_specs,
        scratch_shapes=scratch,
        compiler_params=pltpu.CompilerParams(vmem_limit_bytes=VMEM_LIMIT),
        name="solve_level",
    )(core, *partials, rhs[level], own_d[level, 0], other_d[level, 0])


def on_device(rhs, boundary, diag_inv, off_blocks, coupling, present):
    levels, _, rhs_cols, block = rhs.shape
    outer_each = boundary.shape[0]
    outer = outer_each * 32
    half = rhs_cols // 2
    z, y, core = lax.axis_index("z"), lax.axis_index("y"), lax.axis_index("core")

    def my_half(v, axis):
        return lax.dynamic_slice_in_dim(v, core * half, half, axis)

    def their_half(v, axis):
        return lax.dynamic_slice_in_dim(v, (1 - core) * half, half, axis)

    first = jnp.einsum("rb,ab->ra", rhs[0, 0], diag_inv[0, 0], preferred_element_type=jnp.float32).astype(jnp.bfloat16)
    known = jnp.concatenate([boundary, first[None]])
    known_own = my_half(known, 1)
    known_own, known_other = lax.optimization_barrier((known_own, swap_cores(their_half(known, 1))))
    code_own = (coupling + 1024 * present)[:, 0]
    code_both = jnp.stack([code_own, swap_cores(code_own)], axis=1)
    rhs_both = jnp.concatenate([my_half(rhs, 2), swap_cores(their_half(rhs, 2))], axis=1)
    diag_other = swap_cores(diag_inv)
    off_sent, known_own = lax.optimization_barrier((off_blocks, known_own))
    off_other = swap_cores(off_sent)

    color_a = ring_gather(direct_gather(known_own, "z"), "y")
    color_b = ring_gather(direct_gather(known_other, "y"), "z")

    keep, index = code_both >= 1024, code_both % 1024
    in_outer = index < outer
    row = jnp.where(in_outer, index // outer_each, index - outer)
    member = jnp.where(in_outer, index % outer_each, outer_each)
    src_z, src_y, src_core = row // 8, (row // 2) % 4, row % 2
    each = outer_each + 1
    mine_too = src_core == core
    away = jnp.where(mine_too, src_y - y, src_z - z) % 4
    place = jnp.where(mine_too, src_z ^ z, src_y ^ y) * each + member
    far_half = (away == 2) & (place >= 2 * each)
    piece = jnp.where(away == 3, 1, jnp.where(away == 1, 2, jnp.where(away == 2, 3, 0))) + far_half
    place = jnp.where(far_half, place - 2 * each, place)
    code_known = (piece + jnp.where(mine_too, 0, 5)) * 1024 + place
    level_of = jnp.maximum(index - outer, 0) // 32
    code = jnp.where(level_of == 0, code_known, (9 + level_of) * 1024 + (index - outer) % 32)
    this = jnp.arange(levels - 1)[:, None, None]
    is_fresh = (level_of == this) & (level_of > 0)
    old_code = jnp.where(keep & ~is_fresh, code, -1).reshape(levels - 1, -1)
    fresh_code = jnp.where(keep & is_fresh, code % 1024, -1).reshape(levels - 1, -1)

    core_arr = jnp.reshape(core, (1,)).astype(jnp.int32)
    sources = color_a + color_b
    own_rows, other_rows = [], []
    value = old_sum(1, old_code[0], sources, off_blocks, off_other)
    for level in range(1, levels):
        partials = [value] + [lax.ppermute(value, "x", xor_pairs(4, k)) for k in (1, 2, 3)]
        last = level == levels - 1
        outs = solve_level(level, core_arr, partials, rhs_both, diag_inv, diag_other, 0 if last else 16)
        own_rows.append(outs[0][0])
        other_rows.append(outs[0][1])
        if not last:
            next_code, sent = lax.optimization_barrier((old_code[level], outs[1]))
            solved = lax.all_to_all(sent, ("z", "y"), 0, 0).reshape(32, half, block)
            old = old_sum(level + 1, next_code, sources, off_blocks, off_other)
            value = fresh_sum(level + 1, fresh_code[level], solved, old, off_blocks, off_other)
            sources = sources + [solved]

    mine = jnp.stack(own_rows)
    theirs = swap_cores(jnp.stack(other_rows))
    low = jnp.where(core == 0, mine, theirs)
    high = jnp.where(core == 0, theirs, mine)
    rest = jnp.concatenate([low, high], axis=1)
    return jnp.concatenate([first[None], rest])[:, None]


def solution(mesh):
    split = Mesh(mesh.devices.reshape(4, 4, 2, 4), ("z", "y", "core", "x"))
    in_specs = (
        P(None, ROWS, None, None),
        P(ROWS, None, None),
        P(None, ROWS, None, None),
        P(None, ROWS, "x", None, None),
        P(None, ROWS, "x"),
        P(None, ROWS, "x"),
    )
    return jax.shard_map(
        on_device, mesh=split, in_specs=in_specs, out_specs=P(None, ROWS, None, None), check_vma=False
    )
```

```python
import functools

import jax
import jax.numpy as jnp
from jax import lax
from jax.experimental import pallas as pl
from jax.experimental.pallas import tpu as pltpu
from jax.sharding import Mesh, PartitionSpec as P

ROWS = ("z", "y", "core")
VMEM_LIMIT = 48 * 1024 * 1024


def xor_pairs(n, k):
    return [(i, i ^ k) for i in range(n)]


def shift_pairs(n, k):
    return [(i, (i + k) % n) for i in range(n)]


def swap_cores(v):
    return lax.ppermute(v, "core", xor_pairs(2, 1))


def direct_gather(v, axis):
    return jnp.concatenate([v] + [lax.ppermute(v, axis, xor_pairs(4, k)) for k in (1, 2, 3)])


def ring_gather(v, axis):
    before = lax.ppermute(v, axis, shift_pairs(4, 1))
    after = lax.ppermute(v, axis, shift_pairs(4, 3))
    half = v.shape[0] // 2
    far_a = lax.ppermute(before[:half], axis, shift_pairs(4, 1))
    far_b = lax.ppermute(after[half:], axis, shift_pairs(4, 3))
    return [v, before, after, far_a, far_b]


def nt_dot(x, a):
    return lax.dot_general(x, a, (((1,), (1,)), ((), ())), preferred_element_type=jnp.float32)


GROUP = 8
NEAR = 16


def pick(sources, first, which, place, target, sem):
    if len(sources) == 1:
        pltpu.make_async_copy(sources[0].at[place], target, sem).start()
        return
    middle = len(sources) // 2

    @pl.when(which < first + middle)
    def _():
        pick(sources[:middle], first, which, place, target, sem)

    @pl.when(which >= first + middle)
    def _():
        pick(sources[middle:], first + middle, which, place, target, sem)


def gather_sum(level, code_ref, sources, own_ref, other_ref, out_ref, picked, blocks, sem, block_sems, between=None):
    slots = code_ref.shape[1]
    per_row = slots // 2
    loads = [
        pltpu.make_async_copy(a_ref.at[level - 1, 0], blocks.at[pl.ds(r * per_row, per_row)], block_sems.at[r])
        for r, a_ref in enumerate((own_ref, other_ref))
    ]
    for load in loads:
        load.start()

    def fetch(k, carry):
        code = jnp.maximum(code_ref[level - 1, k], 0)
        pick(sources, 0, code >> 10, code & 1023, picked.at[k], sem)
        return carry

    lax.fori_loop(0, slots, fetch, 0)
    if between is not None:
        between()
    pltpu.make_async_copy(sources[0].at[pl.ds(0, slots)], picked, sem).wait()
    for r in range(2):
        loads[r].wait()
        total = None
        for g in range(r * per_row, (r + 1) * per_row, GROUP):
            xs, group = [], []
            for k in range(g, g + GROUP):
                kept = (code_ref[level - 1, k] >= 0).astype(jnp.float32)
                xs.append((picked[k].astype(jnp.float32) * kept).astype(jnp.bfloat16))
                group.append(blocks[k])
            part = nt_dot(jnp.concatenate(xs, axis=1), jnp.concatenate(group, axis=1))
            total = part if total is None else total + part
        out_ref[r] = total


def first_kernel(code_ref, *refs):
    sources, refs = refs[:-9], refs[-9:]
    own_ref, other_ref, out_ref, store_ref, picked, blocks, sem, block_sems, pack_sems = refs
    packs, start = [], 0
    for i, source in enumerate(sources):
        packs.append(pltpu.make_async_copy(source, store_ref.at[pl.ds(start, source.shape[0])], pack_sems.at[i]))
        start += source.shape[0]

    def between():
        for pack in packs:
            pack.start()

    gather_sum(1, code_ref, sources, own_ref, other_ref, out_ref, picked, blocks, sem, block_sems, between)
    for pack in packs:
        pack.wait()


def old_kernel(level, code_ref, fresh_ref, *refs):
    sources, refs = refs[:-9], refs[-9:]
    own_ref, other_ref, out_ref, list_ref, near_ref, picked, blocks, sem, block_sems = refs
    gather_sum(level, code_ref, sources, own_ref, other_ref, out_ref, picked, blocks, sem, block_sems)

    def note(slot, count):
        code = fresh_ref[level - 1, slot]

        @pl.when(code >= 0)
        def _():
            list_ref[1 + count] = code * 1024 + slot

        @pl.when((code >= 0) & (count < NEAR))
        def _():
            near_ref[count] = blocks[slot]

        return count + (code >= 0).astype(jnp.int32)

    list_ref[0] = lax.fori_loop(0, fresh_ref.shape[1], note, jnp.int32(0))


def sum_call(kernel, codes, sources, own, other, outs, out_spaces, extra, name):
    slots, (rhs_cols, block) = codes[0].shape[1], sources[0].shape[1:]
    return pl.pallas_call(
        kernel,
        out_shape=[jax.ShapeDtypeStruct((2, rhs_cols, block), jnp.float32)] + outs,
        in_specs=[pl.BlockSpec(memory_space=pltpu.SMEM)] * len(codes)
        + [pl.BlockSpec(memory_space=pl.ANY)] * len(sources)
        + [pl.BlockSpec(memory_space=pltpu.HBM)] * 2,
        out_specs=[pl.BlockSpec(memory_space=space) for space in [pltpu.VMEM] + out_spaces],
        scratch_shapes=[
            pltpu.VMEM((slots, rhs_cols, block), jnp.bfloat16),
            pltpu.VMEM((slots, block, block), jnp.bfloat16),
            pltpu.SemaphoreType.DMA,
            pltpu.SemaphoreType.DMA((2,)),
        ]
        + extra,
        compiler_params=pltpu.CompilerParams(vmem_limit_bytes=VMEM_LIMIT),
        cost_estimate=pl.CostEstimate(
            flops=2 * slots * rhs_cols * block * block,
            bytes_accessed=slots * block * (block + 2 * rhs_cols) * 4,
            transcendentals=0,
        ),
        name=name,
    )(*codes, *sources, own, other)


def first_sum(code, sources, own, other):
    store = jax.ShapeDtypeStruct((sum(s.shape[0] for s in sources),) + sources[0].shape[1:], jnp.bfloat16)
    extra = [pltpu.SemaphoreType.DMA((len(sources),))]
    return sum_call(first_kernel, [code], sources, own, other, [store], [pltpu.HBM], extra, "first_sum")


def old_sum(level, code, fresh, sources, own, other):
    block = sources[0].shape[-1]
    outs = [
        jax.ShapeDtypeStruct((code.shape[1] + 1,), jnp.int32),
        jax.ShapeDtypeStruct((NEAR, block, block), jnp.bfloat16),
    ]
    kernel = functools.partial(old_kernel, level)
    return sum_call(kernel, [code, fresh], sources, own, other, outs, [pltpu.SMEM, pltpu.VMEM], [], "old_sum")


def fresh_kernel(level, list_ref, old_ref, x_ref, near_ref, own_ref, other_ref, out_ref, far, sem):
    per_row = own_ref.shape[2]
    out_ref[...] = old_ref[...]
    count = list_ref[0]

    def add(block, entry):
        row = ((entry & 1023) >= per_row).astype(jnp.int32)
        out_ref[row] += nt_dot(x_ref[entry >> 10], block)

    def add_near(n, carry):
        add(near_ref[n], list_ref[1 + n])
        return carry

    def add_far(n, carry):
        slot = list_ref[1 + n] & 1023

        @pl.when(slot < per_row)
        def _():
            pltpu.make_async_copy(own_ref.at[level - 1, 0, slot], far, sem).start()

        @pl.when(slot >= per_row)
        def _():
            pltpu.make_async_copy(other_ref.at[level - 1, 0, slot - per_row], far, sem).start()

        pltpu.make_async_copy(own_ref.at[level - 1, 0, 0], far, sem).wait()
        add(far[...], list_ref[1 + n])
        return carry

    lax.fori_loop(0, jnp.minimum(count, NEAR), add_near, 0)
    lax.fori_loop(NEAR, count, add_far, 0)


def fresh_sum(level, listed, solved, old, near, own, other):
    block = solved.shape[-1]
    vmem = pl.BlockSpec(memory_space=pltpu.VMEM)
    return pl.pallas_call(
        functools.partial(fresh_kernel, level),
        out_shape=jax.ShapeDtypeStruct(old.shape, jnp.float32),
        in_specs=[pl.BlockSpec(memory_space=pltpu.SMEM), vmem, vmem, vmem] + [pl.BlockSpec(memory_space=pltpu.HBM)] * 2,
        out_specs=vmem,
        scratch_shapes=[pltpu.VMEM((block, block), jnp.bfloat16), pltpu.SemaphoreType.DMA],
        compiler_params=pltpu.CompilerParams(vmem_limit_bytes=VMEM_LIMIT),
        name="fresh_sum",
    )(listed, old, solved, near, own, other)


def solve_kernel(level, p0, p1, p2, p3, rhs_ref, own_d_ref, other_d_ref, out_ref, *refs):
    core = lax.axis_index("core")
    for r, d_ref in enumerate((own_d_ref, other_d_ref)):
        coupled = (p0[r] + p1[r]) + (p2[r] + p3[r])
        reduced = (rhs_ref[level, r].astype(jnp.float32) - coupled).astype(jnp.bfloat16)
        solved = nt_dot(reduced, d_ref[level, 0]).astype(jnp.bfloat16)
        out_ref[r] = solved
        if refs:
            refs[1][core ^ r] = solved
    if refs:
        all_ref, both, sems = refs
        sends = [pltpu.make_async_copy(both, all_ref.at[i], sems.at[i]) for i in range(all_ref.shape[0])]
        for send in sends:
            send.start()
        for send in sends:
            send.wait()


def solve_level(level, partials, rhs, own_d, other_d, copies):
    _, rhs_cols, block = partials[0].shape
    vmem = pl.BlockSpec(memory_space=pltpu.VMEM)
    out_shape, out_specs, scratch = [jax.ShapeDtypeStruct((2, rhs_cols, block), jnp.bfloat16)], [vmem], []
    if copies:
        out_shape.append(jax.ShapeDtypeStruct((copies, 2, rhs_cols, block), jnp.bfloat16))
        out_specs.append(pl.BlockSpec(memory_space=pltpu.HBM))
        scratch = [pltpu.VMEM((2, rhs_cols, block), jnp.bfloat16), pltpu.SemaphoreType.DMA((copies,))]
    return pl.pallas_call(
        functools.partial(solve_kernel, level),
        out_shape=out_shape,
        in_specs=[vmem] * 7,
        out_specs=out_specs,
        scratch_shapes=scratch,
        compiler_params=pltpu.CompilerParams(vmem_limit_bytes=VMEM_LIMIT),
        name="solve_level",
    )(*partials, rhs, own_d, other_d)


def on_device(rhs, boundary, diag_inv, off_blocks, coupling, present):
    levels, _, rhs_cols, block = rhs.shape
    outer_each = boundary.shape[0]
    outer = outer_each * 32
    half = rhs_cols // 2
    z, y, core = lax.axis_index("z"), lax.axis_index("y"), lax.axis_index("core")

    def my_half(v, axis):
        return lax.dynamic_slice_in_dim(v, core * half, half, axis)

    def their_half(v, axis):
        return lax.dynamic_slice_in_dim(v, (1 - core) * half, half, axis)

    first = jnp.einsum("rb,ab->ra", rhs[0, 0], diag_inv[0, 0], preferred_element_type=jnp.float32).astype(jnp.bfloat16)
    known = jnp.concatenate([boundary, first[None]])
    known_own = my_half(known, 1)
    known_own, known_other = lax.optimization_barrier((known_own, swap_cores(their_half(known, 1))))
    code_own = (coupling + 1024 * present)[:, 0]
    code_both = jnp.stack([code_own, swap_cores(code_own)], axis=1)
    rhs_both = jnp.concatenate([my_half(rhs, 2), swap_cores(their_half(rhs, 2))], axis=1)
    diag_other = swap_cores(diag_inv)
    off_sent, known_own = lax.optimization_barrier((off_blocks, known_own))
    off_other = swap_cores(off_sent)

    color_a = ring_gather(direct_gather(known_own, "z"), "y")
    color_b = ring_gather(direct_gather(known_other, "y"), "z")

    keep, index = code_both >= 1024, code_both % 1024
    in_outer = index < outer
    row = jnp.where(in_outer, index // outer_each, index - outer)
    member = jnp.where(in_outer, index % outer_each, outer_each)
    src_z, src_y, src_core = row // 8, (row // 2) % 4, row % 2
    each = outer_each + 1
    mine_too = src_core == core
    away = jnp.where(mine_too, src_y - y, src_z - z) % 4
    place = jnp.where(mine_too, src_z ^ z, src_y ^ y) * each + member
    far_half = (away == 2) & (place >= 2 * each)
    piece = jnp.where(away == 3, 1, jnp.where(away == 1, 2, jnp.where(away == 2, 3, 0))) + far_half
    place = jnp.where(far_half, place - 2 * each, place)
    piece_code = (piece + jnp.where(mine_too, 0, 5)) * 1024 + place
    store_code = jnp.where(mine_too, 0, 16 * each) + piece * (4 * each) - jnp.where(piece == 4, 2 * each, 0) + place
    level_of = jnp.maximum(index - outer, 0) // 32
    this = jnp.arange(levels - 1)[:, None, None]
    is_fresh = (level_of == this) & (level_of > 0)
    place_level = (index - outer) % 32
    old_code = jnp.where(level_of == 0, jnp.where(this == 0, piece_code, store_code), level_of * 1024 + place_level)
    old_code = jnp.where(keep & ~is_fresh, old_code, -1).reshape(levels - 1, -1)
    fresh_code = jnp.where(keep & is_fresh, place_level, -1).reshape(levels - 1, -1)

    own_rows, other_rows = [], []
    value, store = first_sum(old_code, color_a + color_b, off_blocks, off_other)
    sources = [store]
    for level in range(1, levels):
        partials = [value] + [lax.ppermute(value, "x", xor_pairs(4, k)) for k in (1, 2, 3)]
        last = level == levels - 1
        outs = solve_level(level, partials, rhs_both, diag_inv, diag_other, 0 if last else 16)
        own_rows.append(outs[0][0])
        other_rows.append(outs[0][1])
        if not last:
            next_fresh, sent = lax.optimization_barrier((fresh_code, outs[1]))
            solved = lax.all_to_all(sent, ("z", "y"), 0, 0).reshape(32, half, block)
            old, listed, near = old_sum(level + 1, old_code, next_fresh, sources, off_blocks, off_other)
            value = fresh_sum(level + 1, listed, solved, old, near, off_blocks, off_other)
            sources = sources + [solved]

    mine = jnp.stack(own_rows)
    theirs = swap_cores(jnp.stack(other_rows))
    low = jnp.where(core == 0, mine, theirs)
    high = jnp.where(core == 0, theirs, mine)
    rest = jnp.concatenate([low, high], axis=1)
    return jnp.concatenate([first[None], rest])[:, None]


def solution(mesh):
    split = Mesh(mesh.devices.reshape(4, 4, 2, 4), ("z", "y", "core", "x"))
    in_specs = (
        P(None, ROWS, None, None),
        P(ROWS, None, None),
        P(None, ROWS, None, None),
        P(None, ROWS, "x", None, None),
        P(None, ROWS, "x"),
        P(None, ROWS, "x"),
    )
    return jax.shard_map(
        on_device, mesh=split, in_specs=in_specs, out_specs=P(None, ROWS, None, None), check_vma=False
    )
```

```python
import functools

import jax
import jax.numpy as jnp
from jax import lax
from jax.experimental import pallas as pl
from jax.experimental.pallas import tpu as pltpu
from jax.sharding import Mesh, PartitionSpec as P

ROWS = ("z", "y", "core")
VMEM_LIMIT = 48 * 1024 * 1024


def xor_pairs(n, k):
    return [(i, i ^ k) for i in range(n)]


def shift_pairs(n, k):
    return [(i, (i + k) % n) for i in range(n)]


def swap_cores(v):
    return lax.ppermute(v, "core", xor_pairs(2, 1))


def direct_gather(v, axis):
    return jnp.concatenate([v] + [lax.ppermute(v, axis, xor_pairs(4, k)) for k in (1, 2, 3)])


def ring_gather(v, axis):
    before = lax.ppermute(v, axis, shift_pairs(4, 1))
    after = lax.ppermute(v, axis, shift_pairs(4, 3))
    half = v.shape[0] // 2
    far_a = lax.ppermute(before[:half], axis, shift_pairs(4, 1))
    far_b = lax.ppermute(after[half:], axis, shift_pairs(4, 3))
    return [v, before, after, far_a, far_b]


def nt_dot(x, a):
    return lax.dot_general(x, a, (((1,), (1,)), ((), ())), preferred_element_type=jnp.float32)


GROUP = 8
NEAR = 16


def gather_sum(level, code_ref, store_ref, solved_ref, own_ref, other_ref, out_ref, blocks, block_sems, between=None):
    slots = code_ref.shape[1]
    known = store_ref.shape[0]
    per_row = slots // 2
    loads = [
        pltpu.make_async_copy(a_ref.at[level - 1, 0], blocks.at[pl.ds(r * per_row, per_row)], block_sems.at[r])
        for r, a_ref in enumerate((own_ref, other_ref))
    ]
    for load in loads:
        load.start()
    if between is not None:
        between()
    for r in range(2):
        loads[r].wait()
        total = None
        for g in range(r * per_row, (r + 1) * per_row, GROUP):
            xs, group = [], []
            for k in range(g, g + GROUP):
                code = code_ref[level - 1, k]
                kept = (code >= 0).astype(jnp.float32)
                picked = store_ref[jnp.clip(code, 0, known - 1)]
                if solved_ref is not None:
                    picked = jnp.where(code >= known, solved_ref[jnp.maximum(code - known, 0)], picked)
                xs.append((picked.astype(jnp.float32) * kept).astype(jnp.bfloat16))
                group.append(blocks[k])
            part = nt_dot(jnp.concatenate(xs, axis=1), jnp.concatenate(group, axis=1))
            total = part if total is None else total + part
        out_ref[r] = total


def first_kernel(code_ref, *refs):
    sources, refs = refs[:-7], refs[-7:]
    own_ref, other_ref, out_ref, store_ref, blocks, block_sems, pack_sems = refs
    packs, start = [], 0
    for i, source in enumerate(sources):
        packs.append(pltpu.make_async_copy(source, store_ref.at[pl.ds(start, source.shape[0])], pack_sems.at[i]))
        start += source.shape[0]

    def between():
        for pack in packs:
            pack.start()
        for pack in packs:
            pack.wait()

    gather_sum(1, code_ref, store_ref, None, own_ref, other_ref, out_ref, blocks, block_sems, between)


def old_kernel(level, code_ref, fresh_ref, store_ref, *refs):
    solved, refs = refs[: level - 2], refs[level - 2 :]
    own_ref, other_ref, out_ref, list_ref, near_ref, blocks, block_sems = refs[:7]
    solved_ref = refs[7] if solved else None

    def between():
        for i, one in enumerate(solved):
            solved_ref[i * one.shape[0] : (i + 1) * one.shape[0]] = one[...]

    gather_sum(level, code_ref, store_ref, solved_ref, own_ref, other_ref, out_ref, blocks, block_sems, between)

    def note(slot, count):
        code = fresh_ref[level - 1, slot]

        @pl.when(code >= 0)
        def _():
            list_ref[1 + count] = code * 1024 + slot

        @pl.when((code >= 0) & (count < NEAR))
        def _():
            near_ref[count] = blocks[slot]

        return count + (code >= 0).astype(jnp.int32)

    list_ref[0] = lax.fori_loop(0, fresh_ref.shape[1], note, jnp.int32(0))


def sum_call(kernel, codes, sources, source_space, own, other, outs, out_spaces, extra, name):
    slots, (rhs_cols, block) = codes[0].shape[1], sources[0].shape[1:]
    return pl.pallas_call(
        kernel,
        out_shape=[jax.ShapeDtypeStruct((2, rhs_cols, block), jnp.float32)] + outs,
        in_specs=[pl.BlockSpec(memory_space=pltpu.SMEM)] * len(codes)
        + [pl.BlockSpec(memory_space=source_space)] * len(sources)
        + [pl.BlockSpec(memory_space=pltpu.HBM)] * 2,
        out_specs=[pl.BlockSpec(memory_space=space) for space in [pltpu.VMEM] + out_spaces],
        scratch_shapes=[pltpu.VMEM((slots, block, block), jnp.bfloat16), pltpu.SemaphoreType.DMA((2,))] + extra,
        compiler_params=pltpu.CompilerParams(vmem_limit_bytes=VMEM_LIMIT),
        cost_estimate=pl.CostEstimate(
            flops=2 * slots * rhs_cols * block * block,
            bytes_accessed=slots * block * (block + 2 * rhs_cols) * 4,
            transcendentals=0,
        ),
        name=name,
    )(*codes, *sources, own, other)


def first_sum(code, sources, own, other):
    store = jax.ShapeDtypeStruct((sum(v.shape[0] for v in sources),) + sources[0].shape[1:], jnp.bfloat16)
    extra = [pltpu.SemaphoreType.DMA((len(sources),))]
    return sum_call(first_kernel, [code], sources, pl.ANY, own, other, [store], [pltpu.VMEM], extra, "first_sum")


def old_sum(level, code, fresh, store, solved, own, other):
    block = store.shape[-1]
    outs = [
        jax.ShapeDtypeStruct((code.shape[1] + 1,), jnp.int32),
        jax.ShapeDtypeStruct((NEAR, block, block), jnp.bfloat16),
    ]
    kernel = functools.partial(old_kernel, level)
    spaces = [pltpu.SMEM, pltpu.VMEM]
    extra = [pltpu.VMEM((sum(v.shape[0] for v in solved),) + store.shape[1:], jnp.bfloat16)] if solved else []
    return sum_call(kernel, [code, fresh], [store] + solved, pltpu.VMEM, own, other, outs, spaces, extra, "old_sum")


def fresh_kernel(level, list_ref, old_ref, x_ref, near_ref, own_ref, other_ref, out_ref, far, sem):
    per_row = own_ref.shape[2]
    out_ref[...] = old_ref[...]
    count = list_ref[0]

    def add(block, entry):
        row = ((entry & 1023) >= per_row).astype(jnp.int32)
        out_ref[row] += nt_dot(x_ref[entry >> 10], block)

    def add_near(n, carry):
        add(near_ref[n], list_ref[1 + n])
        return carry

    def add_far(n, carry):
        slot = list_ref[1 + n] & 1023

        @pl.when(slot < per_row)
        def _():
            pltpu.make_async_copy(own_ref.at[level - 1, 0, slot], far, sem).start()

        @pl.when(slot >= per_row)
        def _():
            pltpu.make_async_copy(other_ref.at[level - 1, 0, slot - per_row], far, sem).start()

        pltpu.make_async_copy(own_ref.at[level - 1, 0, 0], far, sem).wait()
        add(far[...], list_ref[1 + n])
        return carry

    lax.fori_loop(0, jnp.minimum(count, NEAR), add_near, 0)
    lax.fori_loop(NEAR, count, add_far, 0)


def fresh_sum(level, listed, solved, old, near, own, other):
    block = solved.shape[-1]
    vmem = pl.BlockSpec(memory_space=pltpu.VMEM)
    return pl.pallas_call(
        functools.partial(fresh_kernel, level),
        out_shape=jax.ShapeDtypeStruct(old.shape, jnp.float32),
        in_specs=[pl.BlockSpec(memory_space=pltpu.SMEM)] + [vmem] * 3 + [pl.BlockSpec(memory_space=pltpu.HBM)] * 2,
        out_specs=vmem,
        scratch_shapes=[pltpu.VMEM((block, block), jnp.bfloat16), pltpu.SemaphoreType.DMA],
        compiler_params=pltpu.CompilerParams(vmem_limit_bytes=VMEM_LIMIT),
        name="fresh_sum",
    )(listed, old, solved, near, own, other)


def solve_kernel(level, p0, p1, p2, p3, rhs_ref, own_d_ref, other_d_ref, out_ref, *refs):
    core = lax.axis_index("core")
    for r, d_ref in enumerate((own_d_ref, other_d_ref)):
        coupled = (p0[r] + p1[r]) + (p2[r] + p3[r])
        reduced = (rhs_ref[level, r].astype(jnp.float32) - coupled).astype(jnp.bfloat16)
        solved = nt_dot(reduced, d_ref[level, 0]).astype(jnp.bfloat16)
        out_ref[r] = solved
        if refs:
            refs[1][core ^ r] = solved
    if refs:
        all_ref, both, sems = refs
        sends = [pltpu.make_async_copy(both, all_ref.at[i], sems.at[i]) for i in range(all_ref.shape[0])]
        for send in sends:
            send.start()
        for send in sends:
            send.wait()


def solve_level(level, partials, rhs, own_d, other_d, copies):
    _, rhs_cols, block = partials[0].shape
    vmem = pl.BlockSpec(memory_space=pltpu.VMEM)
    out_shape, out_specs, scratch = [jax.ShapeDtypeStruct((2, rhs_cols, block), jnp.bfloat16)], [vmem], []
    if copies:
        out_shape.append(jax.ShapeDtypeStruct((copies, 2, rhs_cols, block), jnp.bfloat16))
        out_specs.append(pl.BlockSpec(memory_space=pltpu.HBM))
        scratch = [pltpu.VMEM((2, rhs_cols, block), jnp.bfloat16), pltpu.SemaphoreType.DMA((copies,))]
    return pl.pallas_call(
        functools.partial(solve_kernel, level),
        out_shape=out_shape,
        in_specs=[vmem] * 7,
        out_specs=out_specs,
        scratch_shapes=scratch,
        compiler_params=pltpu.CompilerParams(vmem_limit_bytes=VMEM_LIMIT),
        name="solve_level",
    )(*partials, rhs, own_d, other_d)


def on_device(rhs, boundary, diag_inv, off_blocks, coupling, present):
    levels, _, rhs_cols, block = rhs.shape
    outer_each = boundary.shape[0]
    outer = outer_each * 32
    half = rhs_cols // 2
    z, y, core = lax.axis_index("z"), lax.axis_index("y"), lax.axis_index("core")

    def my_half(v, axis):
        return lax.dynamic_slice_in_dim(v, core * half, half, axis)

    def their_half(v, axis):
        return lax.dynamic_slice_in_dim(v, (1 - core) * half, half, axis)

    first = jnp.einsum("rb,ab->ra", rhs[0, 0], diag_inv[0, 0], preferred_element_type=jnp.float32).astype(jnp.bfloat16)
    known = jnp.concatenate([boundary, first[None]])
    known_own = my_half(known, 1)
    known_own, known_other = lax.optimization_barrier((known_own, swap_cores(their_half(known, 1))))
    code_own = (coupling + 1024 * present)[:, 0]
    code_both = jnp.stack([code_own, swap_cores(code_own)], axis=1)
    rhs_both = jnp.concatenate([my_half(rhs, 2), swap_cores(their_half(rhs, 2))], axis=1)
    diag_other = swap_cores(diag_inv)
    off_sent, known_own = lax.optimization_barrier((off_blocks, known_own))
    off_other = swap_cores(off_sent)

    color_a = ring_gather(direct_gather(known_own, "z"), "y")
    color_b = ring_gather(direct_gather(known_other, "y"), "z")

    keep, index = code_both >= 1024, code_both % 1024
    in_outer = index < outer
    row = jnp.where(in_outer, index // outer_each, index - outer)
    member = jnp.where(in_outer, index % outer_each, outer_each)
    src_z, src_y, src_core = row // 8, (row // 2) % 4, row % 2
    each = outer_each + 1
    mine_too = src_core == core
    away = jnp.where(mine_too, src_y - y, src_z - z) % 4
    place = jnp.where(mine_too, src_z ^ z, src_y ^ y) * each + member
    far_half = (away == 2) & (place >= 2 * each)
    piece = jnp.where(away == 3, 1, jnp.where(away == 1, 2, jnp.where(away == 2, 3, 0))) + far_half
    place = jnp.where(far_half, place - 2 * each, place)
    known_place = jnp.where(mine_too, 0, 16 * each) + piece * (4 * each) - jnp.where(piece == 4, 2 * each, 0) + place
    level_of = jnp.maximum(index - outer, 0) // 32
    this = jnp.arange(levels - 1)[:, None, None]
    is_fresh = (level_of == this) & (level_of > 0)
    place_level = (index - outer) % 32
    old_code = jnp.where(level_of == 0, known_place, 32 * each + (level_of - 1) * 32 + place_level)
    old_code = jnp.where(keep & ~is_fresh, old_code, -1).reshape(levels - 1, -1)
    fresh_code = jnp.where(keep & is_fresh, place_level, -1).reshape(levels - 1, -1)

    own_rows, other_rows = [], []
    value, store = first_sum(old_code, color_a + color_b, off_blocks, off_other)
    solved_levels = []
    for level in range(1, levels):
        partials = [value] + [lax.ppermute(value, "x", xor_pairs(4, k)) for k in (1, 2, 3)]
        last = level == levels - 1
        outs = solve_level(level, partials, rhs_both, diag_inv, diag_other, 0 if last else 16)
        own_rows.append(outs[0][0])
        other_rows.append(outs[0][1])
        if not last:
            next_fresh, sent = lax.optimization_barrier((fresh_code, outs[1]))
            solved = lax.all_to_all(sent, ("z", "y"), 0, 0).reshape(32, half, block)
            old, listed, near = old_sum(level + 1, old_code, next_fresh, store, solved_levels, off_blocks, off_other)
            value = fresh_sum(level + 1, listed, solved, old, near, off_blocks, off_other)
            solved_levels = solved_levels + [solved]

    mine = jnp.stack(own_rows)
    theirs = swap_cores(jnp.stack(other_rows))
    low = jnp.where(core == 0, mine, theirs)
    high = jnp.where(core == 0, theirs, mine)
    rest = jnp.concatenate([low, high], axis=1)
    return jnp.concatenate([first[None], rest])[:, None]


def solution(mesh):
    split = Mesh(mesh.devices.reshape(4, 4, 2, 4), ("z", "y", "core", "x"))
    in_specs = (
        P(None, ROWS, None, None),
        P(ROWS, None, None),
        P(None, ROWS, None, None),
        P(None, ROWS, "x", None, None),
        P(None, ROWS, "x"),
        P(None, ROWS, "x"),
    )
    return jax.shard_map(
        on_device, mesh=split, in_specs=in_specs, out_specs=P(None, ROWS, None, None), check_vma=False
    )
```

```python
import functools

import jax
import jax.numpy as jnp
from jax import lax
from jax.experimental import pallas as pl
from jax.experimental.pallas import tpu as pltpu
from jax.sharding import Mesh, PartitionSpec as P

ROWS = ("z", "y", "core")
VMEM_LIMIT = 48 * 1024 * 1024


def xor_pairs(n, k):
    return [(i, i ^ k) for i in range(n)]


def shift_pairs(n, k):
    return [(i, (i + k) % n) for i in range(n)]


def swap_cores(v):
    return lax.ppermute(v, "core", xor_pairs(2, 1))


def direct_gather(v, axis):
    return jnp.concatenate([v] + [lax.ppermute(v, axis, xor_pairs(4, k)) for k in (1, 2, 3)])


def ring_gather(v, axis):
    before = lax.ppermute(v, axis, shift_pairs(4, 1))
    after = lax.ppermute(v, axis, shift_pairs(4, 3))
    half = v.shape[0] // 2
    far_a = lax.ppermute(before[:half], axis, shift_pairs(4, 1))
    far_b = lax.ppermute(after[half:], axis, shift_pairs(4, 3))
    return [v, before, after, far_a, far_b]


def nt_dot(x, a):
    return lax.dot_general(x, a, (((1,), (1,)), ((), ())), preferred_element_type=jnp.float32)


GROUP = 8
NEAR = 16


def gather_sum(level, code_ref, picks, known, solved_ref, own_ref, other_ref, out_ref, blocks, block_sems, between):
    slots = code_ref.shape[1]
    per_row = slots // 2
    loads = [
        pltpu.make_async_copy(a_ref.at[level - 1, 0], blocks.at[pl.ds(r * per_row, per_row)], block_sems.at[r])
        for r, a_ref in enumerate((own_ref, other_ref))
    ]
    for load in loads:
        load.start()
    between()
    for r in range(2):
        loads[r].wait()
        total = None
        for g in range(r * per_row, (r + 1) * per_row, GROUP):
            xs, group = [], []
            for k in range(g, g + GROUP):
                code = code_ref[level - 1, k]
                kept = (code >= 0).astype(jnp.float32)
                picked = picks(k, jnp.clip(code, 0, known - 1))
                if solved_ref is not None:
                    picked = jnp.where(code >= known, solved_ref[jnp.maximum(code - known, 0)], picked)
                xs.append((picked.astype(jnp.float32) * kept).astype(jnp.bfloat16))
                group.append(blocks[k])
            part = nt_dot(jnp.concatenate(xs, axis=1), jnp.concatenate(group, axis=1))
            total = part if total is None else total + part
        out_ref[r] = total


def first_kernel(code_ref, *refs):
    sources, refs = refs[:-9], refs[-9:]
    own_ref, other_ref, out_ref, store_ref, blocks, block_sems, pack_sems, packed, store_sem = refs
    packs, start = [], 0
    for i, source in enumerate(sources):
        packs.append(pltpu.make_async_copy(source, packed.at[pl.ds(start, source.shape[0])], pack_sems.at[i]))
        start += source.shape[0]
    keep = pltpu.make_async_copy(packed, store_ref.at[pl.ds(0, start)], store_sem)

    def between():
        for pack in packs:
            pack.start()
        for pack in packs:
            pack.wait()
        keep.start()

    picks = lambda k, code: packed[code]
    gather_sum(1, code_ref, picks, start, None, own_ref, other_ref, out_ref, blocks, block_sems, between)
    keep.wait()


def old_kernel(level, known, code_ref, fresh_ref, store_ref, *refs):
    solved, refs = refs[: level - 2], refs[level - 2 :]
    own_ref, other_ref, out_ref, list_ref, near_ref, blocks, block_sems, picked, pick_sem = refs[:9]
    solved_ref = refs[9] if solved else None
    slots = code_ref.shape[1]

    def between():
        for k in range(slots):
            place = jnp.clip(code_ref[level - 1, k], 0, known - 1)
            pltpu.make_async_copy(store_ref.at[place], picked.at[k], pick_sem).start()
        for i, one in enumerate(solved):
            solved_ref[i * one.shape[0] : (i + 1) * one.shape[0]] = one[...]
        pltpu.make_async_copy(store_ref.at[pl.ds(0, slots)], picked, pick_sem).wait()

    picks = lambda k, code: picked[k]
    gather_sum(level, code_ref, picks, known, solved_ref, own_ref, other_ref, out_ref, blocks, block_sems, between)

    def note(slot, count):
        code = fresh_ref[level - 1, slot]

        @pl.when(code >= 0)
        def _():
            list_ref[1 + count] = code * 1024 + slot

        @pl.when((code >= 0) & (count < NEAR))
        def _():
            near_ref[count] = blocks[slot]

        return count + (code >= 0).astype(jnp.int32)

    list_ref[0] = lax.fori_loop(0, fresh_ref.shape[1], note, jnp.int32(0))


def sum_call(kernel, codes, sources, source_spaces, own, other, outs, out_spaces, extra, name):
    slots, (rhs_cols, block) = codes[0].shape[1], sources[0].shape[1:]
    return pl.pallas_call(
        kernel,
        out_shape=[jax.ShapeDtypeStruct((2, rhs_cols, block), jnp.float32)] + outs,
        in_specs=[pl.BlockSpec(memory_space=pltpu.SMEM)] * len(codes)
        + [pl.BlockSpec(memory_space=space) for space in source_spaces]
        + [pl.BlockSpec(memory_space=pltpu.HBM)] * 2,
        out_specs=[pl.BlockSpec(memory_space=space) for space in [pltpu.VMEM] + out_spaces],
        scratch_shapes=[pltpu.VMEM((slots, block, block), jnp.bfloat16), pltpu.SemaphoreType.DMA((2,))] + extra,
        compiler_params=pltpu.CompilerParams(vmem_limit_bytes=VMEM_LIMIT),
        cost_estimate=pl.CostEstimate(
            flops=2 * slots * rhs_cols * block * block,
            bytes_accessed=slots * block * (block + 2 * rhs_cols) * 4,
            transcendentals=0,
        ),
        name=name,
    )(*codes, *sources, own, other)


def first_sum(code, sources, own, other):
    one = sources[0].shape[1:]
    known = sum(v.shape[0] for v in sources)
    store = jax.ShapeDtypeStruct((2048,) + one, jnp.bfloat16)
    extra = [
        pltpu.SemaphoreType.DMA((len(sources),)),
        pltpu.VMEM((known,) + one, jnp.bfloat16),
        pltpu.SemaphoreType.DMA,
    ]
    spaces = [pl.ANY] * len(sources)
    return sum_call(first_kernel, [code], sources, spaces, own, other, [store], [pltpu.HBM], extra, "first_sum")


def old_sum(level, known, code, fresh, store, solved, own, other):
    one = store.shape[1:]
    outs = [
        jax.ShapeDtypeStruct((code.shape[1] + 1,), jnp.int32),
        jax.ShapeDtypeStruct((NEAR, one[1], one[1]), jnp.bfloat16),
    ]
    kernel = functools.partial(old_kernel, level, known)
    extra = [pltpu.VMEM((code.shape[1],) + one, jnp.bfloat16), pltpu.SemaphoreType.DMA]
    if solved:
        extra.append(pltpu.VMEM((sum(v.shape[0] for v in solved),) + one, jnp.bfloat16))
    spaces = [pl.ANY] + [pltpu.VMEM] * len(solved)
    out_spaces = [pltpu.SMEM, pltpu.VMEM]
    return sum_call(kernel, [code, fresh], [store] + solved, spaces, own, other, outs, out_spaces, extra, "old_sum")


def fresh_kernel(level, list_ref, old_ref, x_ref, near_ref, own_ref, other_ref, out_ref, far, sem):
    per_row = own_ref.shape[2]
    out_ref[...] = old_ref[...]
    count = list_ref[0]

    def add(block, entry):
        row = ((entry & 1023) >= per_row).astype(jnp.int32)
        out_ref[row] += nt_dot(x_ref[entry >> 10], block)

    def add_near(n, carry):
        add(near_ref[n], list_ref[1 + n])
        return carry

    def add_far(n, carry):
        slot = list_ref[1 + n] & 1023

        @pl.when(slot < per_row)
        def _():
            pltpu.make_async_copy(own_ref.at[level - 1, 0, slot], far, sem).start()

        @pl.when(slot >= per_row)
        def _():
            pltpu.make_async_copy(other_ref.at[level - 1, 0, slot - per_row], far, sem).start()

        pltpu.make_async_copy(own_ref.at[level - 1, 0, 0], far, sem).wait()
        add(far[...], list_ref[1 + n])
        return carry

    lax.fori_loop(0, jnp.minimum(count, NEAR), add_near, 0)
    lax.fori_loop(NEAR, count, add_far, 0)


def fresh_sum(level, listed, solved, old, near, own, other):
    block = solved.shape[-1]
    vmem = pl.BlockSpec(memory_space=pltpu.VMEM)
    return pl.pallas_call(
        functools.partial(fresh_kernel, level),
        out_shape=jax.ShapeDtypeStruct(old.shape, jnp.float32),
        in_specs=[pl.BlockSpec(memory_space=pltpu.SMEM)] + [vmem] * 3 + [pl.BlockSpec(memory_space=pltpu.HBM)] * 2,
        out_specs=vmem,
        scratch_shapes=[pltpu.VMEM((block, block), jnp.bfloat16), pltpu.SemaphoreType.DMA],
        compiler_params=pltpu.CompilerParams(vmem_limit_bytes=VMEM_LIMIT),
        name="fresh_sum",
    )(listed, old, solved, near, own, other)


def solve_kernel(level, p0, p1, p2, p3, rhs_ref, own_d_ref, other_d_ref, out_ref, *refs):
    core = lax.axis_index("core")
    for r, d_ref in enumerate((own_d_ref, other_d_ref)):
        coupled = (p0[r] + p1[r]) + (p2[r] + p3[r])
        reduced = (rhs_ref[level, r].astype(jnp.float32) - coupled).astype(jnp.bfloat16)
        solved = nt_dot(reduced, d_ref[level, 0]).astype(jnp.bfloat16)
        out_ref[r] = solved
        if refs:
            refs[1][core ^ r] = solved
    if refs:
        all_ref, both, sems = refs
        sends = [pltpu.make_async_copy(both, all_ref.at[i], sems.at[i]) for i in range(all_ref.shape[0])]
        for send in sends:
            send.start()
        for send in sends:
            send.wait()


def solve_level(level, partials, rhs, own_d, other_d, copies):
    _, rhs_cols, block = partials[0].shape
    vmem = pl.BlockSpec(memory_space=pltpu.VMEM)
    out_shape, out_specs, scratch = [jax.ShapeDtypeStruct((2, rhs_cols, block), jnp.bfloat16)], [vmem], []
    if copies:
        out_shape.append(jax.ShapeDtypeStruct((copies, 2, rhs_cols, block), jnp.bfloat16))
        out_specs.append(pl.BlockSpec(memory_space=pltpu.HBM))
        scratch = [pltpu.VMEM((2, rhs_cols, block), jnp.bfloat16), pltpu.SemaphoreType.DMA((copies,))]
    return pl.pallas_call(
        functools.partial(solve_kernel, level),
        out_shape=out_shape,
        in_specs=[vmem] * 7,
        out_specs=out_specs,
        scratch_shapes=scratch,
        compiler_params=pltpu.CompilerParams(vmem_limit_bytes=VMEM_LIMIT),
        name="solve_level",
    )(*partials, rhs, own_d, other_d)


def on_device(rhs, boundary, diag_inv, off_blocks, coupling, present):
    levels, _, rhs_cols, block = rhs.shape
    outer_each = boundary.shape[0]
    outer = outer_each * 32
    half = rhs_cols // 2
    z, y, core = lax.axis_index("z"), lax.axis_index("y"), lax.axis_index("core")

    def my_half(v, axis):
        return lax.dynamic_slice_in_dim(v, core * half, half, axis)

    def their_half(v, axis):
        return lax.dynamic_slice_in_dim(v, (1 - core) * half, half, axis)

    first = jnp.einsum("rb,ab->ra", rhs[0, 0], diag_inv[0, 0], preferred_element_type=jnp.float32).astype(jnp.bfloat16)
    known = jnp.concatenate([boundary, first[None]])
    known_own = my_half(known, 1)
    known_own, known_other = lax.optimization_barrier((known_own, swap_cores(their_half(known, 1))))
    code_own = (coupling + 1024 * present)[:, 0]
    code_both = jnp.stack([code_own, swap_cores(code_own)], axis=1)
    rhs_both = jnp.concatenate([my_half(rhs, 2), swap_cores(their_half(rhs, 2))], axis=1)
    diag_other = swap_cores(diag_inv)
    off_sent, known_own = lax.optimization_barrier((off_blocks, known_own))
    off_other = swap_cores(off_sent)

    color_a = ring_gather(direct_gather(known_own, "z"), "y")
    color_b = ring_gather(direct_gather(known_other, "y"), "z")

    keep, index = code_both >= 1024, code_both % 1024
    in_outer = index < outer
    row = jnp.where(in_outer, index // outer_each, index - outer)
    member = jnp.where(in_outer, index % outer_each, outer_each)
    src_z, src_y, src_core = row // 8, (row // 2) % 4, row % 2
    each = outer_each + 1
    mine_too = src_core == core
    away = jnp.where(mine_too, src_y - y, src_z - z) % 4
    place = jnp.where(mine_too, src_z ^ z, src_y ^ y) * each + member
    far_half = (away == 2) & (place >= 2 * each)
    piece = jnp.where(away == 3, 1, jnp.where(away == 1, 2, jnp.where(away == 2, 3, 0))) + far_half
    place = jnp.where(far_half, place - 2 * each, place)
    known_place = jnp.where(mine_too, 0, 16 * each) + piece * (4 * each) - jnp.where(piece == 4, 2 * each, 0) + place
    level_of = jnp.maximum(index - outer, 0) // 32
    this = jnp.arange(levels - 1)[:, None, None]
    is_fresh = (level_of == this) & (level_of > 0)
    place_level = (index - outer) % 32
    old_code = jnp.where(level_of == 0, known_place, 32 * each + (level_of - 1) * 32 + place_level)
    old_code = jnp.where(keep & ~is_fresh, old_code, -1).reshape(levels - 1, -1)
    fresh_code = jnp.where(keep & is_fresh, place_level, -1).reshape(levels - 1, -1)

    own_rows, other_rows = [], []
    value, store = first_sum(old_code, color_a + color_b, off_blocks, off_other)
    solved_levels = []
    for level in range(1, levels):
        partials = [value] + [lax.ppermute(value, "x", xor_pairs(4, k)) for k in (1, 2, 3)]
        last = level == levels - 1
        outs = solve_level(level, partials, rhs_both, diag_inv, diag_other, 0 if last else 16)
        own_rows.append(outs[0][0])
        other_rows.append(outs[0][1])
        if not last:
            next_fresh, sent = lax.optimization_barrier((fresh_code, outs[1]))
            solved = lax.all_to_all(sent, ("z", "y"), 0, 0).reshape(32, half, block)
            old, listed, near = old_sum(
                level + 1, 32 * each, old_code, next_fresh, store, solved_levels, off_blocks, off_other
            )
            value = fresh_sum(level + 1, listed, solved, old, near, off_blocks, off_other)
            solved_levels = solved_levels + [solved]

    mine = jnp.stack(own_rows)
    theirs = swap_cores(jnp.stack(other_rows))
    low = jnp.where(core == 0, mine, theirs)
    high = jnp.where(core == 0, theirs, mine)
    rest = jnp.concatenate([low, high], axis=1)
    return jnp.concatenate([first[None], rest])[:, None]


def solution(mesh):
    split = Mesh(mesh.devices.reshape(4, 4, 2, 4), ("z", "y", "core", "x"))
    in_specs = (
        P(None, ROWS, None, None),
        P(ROWS, None, None),
        P(None, ROWS, None, None),
        P(None, ROWS, "x", None, None),
        P(None, ROWS, "x"),
        P(None, ROWS, "x"),
    )
    return jax.shard_map(
        on_device, mesh=split, in_specs=in_specs, out_specs=P(None, ROWS, None, None), check_vma=False
    )
```

```python
import functools

import jax
import jax.numpy as jnp
from jax import lax
from jax.experimental import pallas as pl
from jax.experimental.pallas import tpu as pltpu
from jax.sharding import Mesh, PartitionSpec as P

ROWS = ("z", "y", "core")
VMEM_LIMIT = 48 * 1024 * 1024


def xor_pairs(n, k):
    return [(i, i ^ k) for i in range(n)]


def shift_pairs(n, k):
    return [(i, (i + k) % n) for i in range(n)]


def swap_cores(v):
    return lax.ppermute(v, "core", xor_pairs(2, 1))


def direct_gather(v, axis):
    return jnp.concatenate([v] + [lax.ppermute(v, axis, xor_pairs(4, k)) for k in (1, 2, 3)])


def ring_gather(v, axis):
    before = lax.ppermute(v, axis, shift_pairs(4, 1))
    after = lax.ppermute(v, axis, shift_pairs(4, 3))
    half = v.shape[0] // 2
    far_a = lax.ppermute(before[:half], axis, shift_pairs(4, 1))
    far_b = lax.ppermute(after[half:], axis, shift_pairs(4, 3))
    return [v, before, after, far_a, far_b]


def nt_dot(x, a):
    return lax.dot_general(x, a, (((1,), (1,)), ((), ())), preferred_element_type=jnp.float32)


GROUP = 8
UNROLL = 4
CAPACITY = (12, 14, 16, 18, 19, 20)
FRESH_CAPACITY = 24
MIDDLE_CAPACITY = 52
CHUNKS = ((2, 3), (4, 5), (6,), (7,))


def chunk_of(level):
    for n, chunk in enumerate(CHUNKS):
        if level in chunk:
            before = sum(CAPACITY[one - 2] for one in chunk if one < level)
            return n, before, sum(CAPACITY[one - 2] for one in chunk)


def call(kernel, name, operands, in_spaces, outs, out_spaces, scratch, flops=0, bytes_accessed=0):
    return pl.pallas_call(
        kernel,
        out_shape=outs,
        in_specs=[pl.BlockSpec(memory_space=space) for space in in_spaces],
        out_specs=[pl.BlockSpec(memory_space=space) for space in out_spaces],
        scratch_shapes=scratch,
        compiler_params=pltpu.CompilerParams(vmem_limit_bytes=VMEM_LIMIT),
        cost_estimate=pl.CostEstimate(flops=flops, bytes_accessed=bytes_accessed, transcendentals=0),
        name=name,
    )(*operands)


def gather_sum(level, code_ref, picks, own_ref, other_ref, out_ref, blocks, block_sems):
    slots = code_ref.shape[1]
    per_row = slots // 2
    loads = [
        pltpu.make_async_copy(a_ref.at[level - 1, 0], blocks.at[pl.ds(r * per_row, per_row)], block_sems.at[r])
        for r, a_ref in enumerate((own_ref, other_ref))
    ]
    for r in range(2):
        loads[r].wait()
        total = None
        for g in range(r * per_row, (r + 1) * per_row, GROUP):
            xs, group = [], []
            for k in range(g, g + GROUP):
                code = code_ref[level - 1, k]
                kept = (code >= 0).astype(jnp.float32)
                xs.append((picks(k, jnp.maximum(code, 0)).astype(jnp.float32) * kept).astype(jnp.bfloat16))
                group.append(blocks[k])
            part = nt_dot(jnp.concatenate(xs, axis=1), jnp.concatenate(group, axis=1))
            total = part if total is None else total + part
        out_ref[r] = total


def start_blocks(levels, own_ref, other_ref, blocks, block_sems):
    per_row = blocks.shape[1] // 2
    for n, level in enumerate(levels):
        for r, a_ref in enumerate((own_ref, other_ref)):
            target = blocks.at[n, pl.ds(r * per_row, per_row)]
            pltpu.make_async_copy(a_ref.at[level - 1, 0], target, block_sems.at[n, r]).start()


def first_kernel(levels, code_ref, flag_ref, *refs):
    sources, refs = refs[:-9], refs[-9:]
    own_ref, other_ref, out_ref, store_ref, blocks, block_sems, pack_sems, packed, store_sem = refs
    start_blocks(levels, own_ref, other_ref, blocks, block_sems)
    packs, start = [], 0
    for i, source in enumerate(sources):
        packs.append(pltpu.make_async_copy(source, packed.at[pl.ds(start, source.shape[0])], pack_sems.at[i]))
        start += source.shape[0]
    for pack in packs:
        pack.start()
    for pack in packs:
        pack.wait()
    keep = pltpu.make_async_copy(packed, store_ref.at[pl.ds(0, start)], store_sem)
    keep.start()
    for n, level in enumerate(levels):
        gather_sum(
            level, code_ref, lambda k, code: packed[code], own_ref, other_ref, out_ref.at[n], blocks.at[n], block_sems.at[n]
        )
    out_ref[0] = out_ref[0] + jnp.where(flag_ref[0] > 0, jnp.float32(jnp.nan), jnp.float32(0.0))
    keep.wait()


def known_kernel(levels, code_ref, store_ref, own_ref, other_ref, out_ref, blocks, block_sems, picked, pick_sem):
    slots = code_ref.shape[1]
    start_blocks(levels, own_ref, other_ref, blocks, block_sems)
    for n, level in enumerate(levels):

        def fetch(k, carry, n=n, level=level):
            place = jnp.maximum(code_ref[level - 1, k], 0)
            pltpu.make_async_copy(store_ref.at[place], picked.at[n * slots + k], pick_sem).start()
            return carry

        lax.fori_loop(0, slots, fetch, 0)
    pltpu.make_async_copy(store_ref.at[pl.ds(0, slots * len(levels))], picked, pick_sem).wait()
    for n, level in enumerate(levels):
        picks = lambda k, code, n=n: picked[n * slots + k]
        gather_sum(level, code_ref, picks, own_ref, other_ref, out_ref.at[n], blocks.at[n], block_sems.at[n])


def known_sums(levels, code, flag, sources, own, other):
    slots, one, some = code.shape[1], sources[0].shape[1:], len(levels)
    sums = jax.ShapeDtypeStruct((some, 2) + one, jnp.float32)
    scratch = [pltpu.VMEM((some, slots, one[1], one[1]), jnp.bfloat16), pltpu.SemaphoreType.DMA((some, 2))]
    cost = dict(
        flops=2 * some * slots * one[0] * one[1] * one[1], bytes_accessed=some * slots * one[1] * (one[1] + 2 * one[0]) * 4
    )
    spaces = [pl.ANY] * len(sources) + [pltpu.HBM] * 2
    if flag is None:
        scratch += [pltpu.VMEM((some * slots,) + one, jnp.bfloat16), pltpu.SemaphoreType.DMA]
        kernel = functools.partial(known_kernel, levels)
        operands = (code, *sources, own, other)
        return call(kernel, "known_sums", operands, [pltpu.SMEM] + spaces, [sums], [pltpu.VMEM], scratch, **cost)[0]
    known = sum(v.shape[0] for v in sources)
    scratch += [
        pltpu.SemaphoreType.DMA((len(sources),)),
        pltpu.VMEM((known,) + one, jnp.bfloat16),
        pltpu.SemaphoreType.DMA,
    ]
    store = jax.ShapeDtypeStruct((2048,) + one, jnp.bfloat16)
    kernel = functools.partial(first_kernel, levels)
    operands = (code, flag, *sources, own, other)
    spaces = [pltpu.SMEM] * 2 + spaces
    return call(kernel, "first_sums", operands, spaces, [sums, store], [pltpu.VMEM, pltpu.HBM], scratch, **cost)


def near_kernel(rank_ref, off_ref, *refs):
    outs, (blocks, sem, out_sems) = refs[: len(CHUNKS)], refs[len(CHUNKS) :]
    slots = rank_ref.shape[1]
    places = []
    for level in range(2, 2 + len(CAPACITY)):
        n, before, _ = chunk_of(level)
        places.append(sum(sum(CAPACITY[one - 2] for one in chunk) for chunk in CHUNKS[:n]) + before)
        if before == 0:
            blocks[places[-1]] = jnp.zeros(blocks.shape[1:], blocks.dtype)

    for level, place in zip(range(2, 2 + len(CAPACITY)), places):

        def copy_of(k, level=level, place=place):
            target = place + rank_ref[level - 1, k]
            return pltpu.make_async_copy(off_ref.at[level - 1, 0, k], blocks.at[target], sem.at[target])

        def load(k, carry, level=level, copy_of=copy_of):
            @pl.when(rank_ref[level - 1, k] >= 0)
            def _():
                copy_of(k).start()

            return carry

        lax.fori_loop(0, slots, load, 0)

    for level, place in zip(range(2, 2 + len(CAPACITY)), places):

        def wait(k, carry, level=level, place=place):
            @pl.when(rank_ref[level - 1, k] >= 0)
            def _():
                target = place + rank_ref[level - 1, k]
                pltpu.make_async_copy(off_ref.at[level - 1, 0, k], blocks.at[target], sem.at[target]).wait()

            return carry

        lax.fori_loop(0, slots, wait, 0)
    start, stores = 0, []
    for n, out in enumerate(outs):
        stores.append(pltpu.make_async_copy(blocks.at[pl.ds(start, out.shape[0])], out, out_sems.at[n]))
        stores[-1].start()
        start += out.shape[0]
    for store in stores:
        store.wait()


def near_blocks(rank, off):
    block = off.shape[-1]
    sizes = [sum(CAPACITY[one - 2] for one in chunk) for chunk in CHUNKS]
    outs = [jax.ShapeDtypeStruct((size, block, block), jnp.bfloat16) for size in sizes]
    scratch = [
        pltpu.VMEM((sum(sizes), block, block), jnp.bfloat16),
        pltpu.SemaphoreType.DMA((sum(sizes),)),
        pltpu.SemaphoreType.DMA((len(sizes),)),
    ]
    return call(
        near_kernel, "near_blocks", (rank, off), [pltpu.SMEM, pltpu.HBM], outs, [pltpu.HBM] * len(sizes), scratch
    )


def add_listed(total, count, entry_of, block_of, solved_of, ready=None):
    def step(j, total):
        xs, blocks = [], []
        for t in range(UNROLL):
            i = j * UNROLL + t
            entry = entry_of(i)
            if ready is not None:
                ready(i)
            kept = ((entry >> 8) & 1).astype(jnp.float32)
            xs.append((solved_of(entry & 255).astype(jnp.float32) * kept).astype(jnp.bfloat16))
            blocks.append(block_of(i))
        return total + nt_dot(jnp.concatenate(xs, axis=1), jnp.concatenate(blocks, axis=1))

    return lax.fori_loop(0, (count + UNROLL - 1) // UNROLL, step, total)


def middle_kernel(level, counts_ref, fresh_ref, middle_ref, *refs):
    solved, refs = refs[: level - 2], refs[level - 2 :]
    own_ref, other_ref, out_ref, near_ref, blocks, sems, near_sems = refs[:7]
    fresh_max, middle_max = fresh_ref.shape[1], middle_ref.shape[1]
    at = 2 * (level - 1)
    rounded = lambda n: (n + UNROLL - 1) // UNROLL * UNROLL

    def copies(r, source):
        fresh = lambda i: pltpu.make_async_copy(
            source.at[fresh_ref[at + r, i] >> 9], near_ref.at[r * fresh_max + i], near_sems.at[r * fresh_max + i]
        )
        middle = lambda i: pltpu.make_async_copy(
            source.at[middle_ref[at + r, i] >> 9], blocks.at[r * middle_max + i], sems.at[r * middle_max + i]
        )
        return fresh, middle

    def each(count, do):
        def body(i, carry):
            do(i)
            return carry

        lax.fori_loop(0, rounded(count), body, 0)

    for r, source in enumerate((own_ref, other_ref)):
        fresh, middle = copies(r, source)
        if solved:
            each(counts_ref[1, at + r], lambda i: middle(i).start())
        each(counts_ref[0, at + r], lambda i: fresh(i).start())
    if solved:
        solved_ref = refs[7]
        for i, one in enumerate(solved):
            solved_ref[i * one.shape[0] : (i + 1) * one.shape[0]] = one[...]
    for r, source in enumerate((own_ref, other_ref)):
        _, middle = copies(r, source)
        total = jnp.zeros(out_ref.shape[1:], jnp.float32)
        if solved:
            total = add_listed(
                total,
                counts_ref[1, at + r],
                lambda i: middle_ref[at + r, i],
                lambda i: blocks[r * middle_max + i],
                lambda place: solved_ref[place],
                lambda i: middle(i).wait(),
            )
        out_ref[r] = total
    for r, source in enumerate((own_ref, other_ref)):
        fresh, _ = copies(r, source)
        each(counts_ref[0, at + r], lambda i: fresh(i).wait())


def middle_sum(level, counts, fresh, middle, solved, own, other, rhs_cols):
    block = own.shape[-1]
    one = (rhs_cols, block)
    outs = [
        jax.ShapeDtypeStruct((2,) + one, jnp.float32),
        jax.ShapeDtypeStruct((2 * fresh.shape[1], block, block), jnp.bfloat16),
    ]
    scratch = [
        pltpu.VMEM((2 * middle.shape[1], block, block), jnp.bfloat16),
        pltpu.SemaphoreType.DMA((2 * middle.shape[1],)),
        pltpu.SemaphoreType.DMA((2 * fresh.shape[1],)),
    ]
    if solved:
        scratch.append(pltpu.VMEM((sum(v.shape[0] for v in solved),) + one, jnp.bfloat16))
    spaces = [pltpu.SMEM] * 3 + [pltpu.VMEM] * len(solved) + [pltpu.HBM] * 2
    operands = (counts, fresh, middle, *solved, own, other)
    kernel = functools.partial(middle_kernel, level)
    return call(
        kernel, "middle_sum", operands, spaces, outs, [pltpu.VMEM] * 2, scratch, 2 * 40 * rhs_cols * block**2, 8 << 20
    )


def solve_kernel(level, at, last, *refs):
    near = level > 1
    if near:
        (counts_ref, fresh_ref, middle_ref, near_ref, solved_ref), refs = refs[:5], refs[5:]
    p0, p1, p2, p3, rhs_ref, own_d_ref, other_d_ref, out_ref = refs[:8]
    for r, d_ref in enumerate((own_d_ref, other_d_ref)):
        coupled = (p0[at, r] + p1[at, r]) + (p2[at, r] + p3[at, r])
        if near:
            row = 2 * (level - 1) + r
            first = level - 2
            place = first * 32
            fresh_max = fresh_ref.shape[1]
            coupled = add_listed(
                coupled + middle_ref[r],
                counts_ref[0, row],
                lambda i: fresh_ref[row, i],
                lambda i: near_ref[r * fresh_max + i],
                lambda code: solved_ref[jnp.maximum(code - place, 0)],
            )
        reduced = (rhs_ref[level, r].astype(jnp.float32) - coupled).astype(jnp.bfloat16)
        solved = nt_dot(reduced, d_ref[level, 0]).astype(jnp.bfloat16)
        out_ref[r] = solved
        if not last:
            refs[9][lax.axis_index("core") ^ r] = solved
    if not last:
        all_ref, both, sems = refs[8:]
        sends = [pltpu.make_async_copy(both, all_ref.at[i], sems.at[i]) for i in range(all_ref.shape[0])]
        for send in sends:
            send.start()
        for send in sends:
            send.wait()


def solve_level(level, at, near, partials, rhs, own_d, other_d, copies):
    one = partials[0].shape[2:]
    outs, spaces, scratch = [jax.ShapeDtypeStruct((2,) + one, jnp.bfloat16)], [pltpu.VMEM], []
    if copies:
        outs.append(jax.ShapeDtypeStruct((copies, 2) + one, jnp.bfloat16))
        spaces.append(pltpu.HBM)
        scratch = [pltpu.VMEM((2,) + one, jnp.bfloat16), pltpu.SemaphoreType.DMA((copies,))]
    in_spaces = ([pltpu.SMEM] * 2 + [pltpu.VMEM] * 3 if near else []) + [pltpu.VMEM] * 7
    kernel = functools.partial(solve_kernel, level, at, not copies)
    return call(
        kernel, "solve_level", (*near, *partials, rhs, own_d, other_d), in_spaces, outs, spaces, scratch
    )


def plain(rhs, boundary, diag_inv, off_blocks, coupling, present):
    levels, _, rhs_cols, block = rhs.shape
    outer_all = lax.all_gather(boundary, ROWS, axis=0, tiled=True)
    outer, width = outer_all.shape[0], 32
    empty = jnp.zeros((levels * width, rhs_cols, block), jnp.bfloat16)
    solved = jnp.concatenate([outer_all, empty], axis=0)
    results = []
    for level in range(levels):
        target = rhs[level, 0].astype(jnp.float32)
        if level > 0:
            picked = jnp.take(solved, coupling[level - 1, 0], axis=0)
            picked = picked * present[level - 1, 0].astype(jnp.bfloat16)[:, None, None]
            partial_value = jnp.einsum(
                "kab,krb->ra", off_blocks[level - 1, 0], picked, preferred_element_type=jnp.float32
            )
            target = target - lax.psum(partial_value, "x")
        own = jnp.einsum(
            "rb,ab->ra", target.astype(jnp.bfloat16), diag_inv[level, 0], preferred_element_type=jnp.float32
        ).astype(jnp.bfloat16)
        fresh = lax.all_gather(own[None], ROWS, axis=0, tiled=True)
        solved = solved.at[outer + level * width : outer + (level + 1) * width].set(fresh)
        results.append(own)
    return jnp.stack(results)[:, None]


def tied(value, to):
    return lax.optimization_barrier((value, to))


def on_device(rhs, boundary, diag_inv, off_blocks, coupling, present):
    levels, _, rhs_cols, block = rhs.shape
    outer_each = boundary.shape[0]
    outer = outer_each * 32
    half = rhs_cols // 2
    z, y, core, x = (lax.axis_index(a) for a in ("z", "y", "core", "x"))

    def my_half(v, axis):
        return lax.dynamic_slice_in_dim(v, core * half, half, axis)

    def their_half(v, axis):
        return lax.dynamic_slice_in_dim(v, (1 - core) * half, half, axis)

    first = jnp.einsum("rb,ab->ra", rhs[0, 0], diag_inv[0, 0], preferred_element_type=jnp.float32).astype(jnp.bfloat16)
    known = jnp.concatenate([boundary, first[None]])
    known_own, known_other = tied(my_half(known, 1), swap_cores(their_half(known, 1)))

    code_own = (coupling + 1024 * present)[:, 0]
    inside = lambda code: (code >= 1024 + outer + 32) & (jnp.arange(levels - 1) > 0)[:, None]
    own_inside = inside(code_own)
    limits = jnp.array((0,) + CAPACITY, jnp.int32)[:, None]
    own_rank = jnp.cumsum(own_inside.astype(jnp.int32), axis=1) - 1
    own_rank = jnp.where(own_inside & (own_rank < limits), own_rank, -1)
    nears = near_blocks(own_rank, off_blocks)
    near_own = [lax.all_gather(v, "x", axis=0, tiled=True) for v in nears]
    near_other = [swap_cores(v) for v in near_own]

    code_both = jnp.stack([code_own, swap_cores(code_own)], axis=1)
    rhs_both = jnp.concatenate([my_half(rhs, 2), swap_cores(their_half(rhs, 2))], axis=1)
    diag_other = swap_cores(diag_inv)
    off_sent, known_own = tied(off_blocks, known_own)
    off_other = swap_cores(off_sent)

    color_a = ring_gather(direct_gather(known_own, "z"), "y")
    color_b = ring_gather(direct_gather(known_other, "y"), "z")

    keep, index = code_both >= 1024, code_both % 1024
    in_outer = index < outer
    row = jnp.where(in_outer, index // outer_each, index - outer)
    member = jnp.where(in_outer, index % outer_each, outer_each)
    src_z, src_y, src_core = row // 8, (row // 2) % 4, row % 2
    each = outer_each + 1
    mine_too = src_core == core
    away = jnp.where(mine_too, src_y - y, src_z - z) % 4
    place = jnp.where(mine_too, src_z ^ z, src_y ^ y) * each + member
    slot_of = jnp.where(away == 3, 1, jnp.where(away == 1, 2, jnp.where(away == 2, 3, 0)))
    known_place = jnp.where(mine_too, 0, 16 * each) + slot_of * (4 * each) + place
    known_code = jnp.where(keep & (index < outer + 32), known_place, -1).reshape(levels - 1, -1)

    every = jnp.stack([code_both] + [lax.ppermute(code_both, "x", xor_pairs(4, k)) for k in (1, 2, 3)], axis=2)
    this = jnp.arange(levels - 1)[:, None, None, None]
    every_inside = (every >= 1024 + outer + 32) & (this > 0)
    rank = jnp.cumsum(every_inside.astype(jnp.int32), axis=3) - 1
    solved_place = every - (1024 + outer + 32)
    at_x = (x ^ jnp.arange(4))[:, None]
    chunk_size = jnp.array([0] + [chunk_of(level)[2] for level in range(2, levels)], jnp.int32)[:, None, None, None]
    chunk_start = jnp.array([0] + [chunk_of(level)[1] for level in range(2, levels)], jnp.int32)[:, None, None, None]
    entry = (at_x * chunk_size + chunk_start + rank) * 512 + 256 + solved_place
    is_fresh = every_inside & (solved_place >= (this - 1) * 32)
    is_middle = every_inside & ~is_fresh

    def listed(chosen, capacity):
        entries = jnp.where(chosen, entry, 0).reshape(2 * (levels - 1), -1)
        return -lax.sort(-entries, dimension=1)[:, :capacity], jnp.sum(chosen, axis=(2, 3), dtype=jnp.int32).reshape(-1)

    fresh_list, fresh_count = listed(is_fresh, FRESH_CAPACITY)
    middle_list, middle_count = listed(is_middle, MIDDLE_CAPACITY)
    inside_count = jnp.sum(every_inside, axis=3, dtype=jnp.int32)
    over = jnp.any(inside_count > limits[:, :, None]) | jnp.any(fresh_count > FRESH_CAPACITY)
    over = over | jnp.any(middle_count > MIDDLE_CAPACITY)
    flag = over.astype(jnp.int32).reshape(1)
    counts = jnp.stack([jnp.minimum(fresh_count, FRESH_CAPACITY), jnp.minimum(middle_count, MIDDLE_CAPACITY)])
    in_reach = lambda entries: jnp.minimum(entries, (4 * jnp.repeat(chunk_size.reshape(-1), 2)[:, None] - 1) * 512 + 511)
    fresh_list, middle_list = in_reach(fresh_list), in_reach(middle_list)
    fresh_list, middle_list = jnp.maximum(fresh_list, 0), jnp.maximum(middle_list, 0)

    def over_x(value):
        return [value] + [lax.ppermute(value, "x", xor_pairs(4, k)) for k in (1, 2, 3)]

    batches = ((1, 2), (3, 4), (5, 6), (7,))
    value, store = known_sums(batches[0], known_code, flag, color_a + color_b, off_blocks, off_other)
    sums = {level: (over_x_value, n) for over_x_value in [over_x(value)] for n, level in enumerate(batches[0])}
    own_rows, other_rows, solved_levels, pending = [], [], [], None
    near = ()
    for level in range(1, levels):
        last = level == levels - 1
        partials, at = sums[level]
        outs = solve_level(level, at, near, partials, rhs_both, diag_inv, diag_other, 0 if last else 16)
        own_rows.append(outs[0][0])
        other_rows.append(outs[0][1])
        if last:
            break
        tie, sent = tied(counts, outs[1])
        solved = lax.all_to_all(sent, ("z", "y"), 0, 0).reshape(32, half, block)
        if pending is not None:
            batch, value = pending
            value, _ = tied(value, sent)
            spread = over_x(value)
            sums.update({one: (spread, n) for n, one in enumerate(batch)})
            pending = None
        if level < len(batches):
            code, _ = tied(known_code, sent)
            pending = (batches[level], known_sums(batches[level], code, None, [store], off_blocks, off_other))
        n = chunk_of(level + 1)[0]
        middle, near_now = middle_sum(
            level + 1, tie, fresh_list, middle_list, solved_levels, near_own[n], near_other[n], half
        )
        near = (counts, fresh_list, middle, near_now, solved)
        solved_levels = solved_levels + [solved]

    given_up = jnp.any(solved_levels[0] != solved_levels[0])
    mine = jnp.stack(own_rows)
    theirs = swap_cores(jnp.stack(other_rows))
    low = jnp.where(core == 0, mine, theirs)
    high = jnp.where(core == 0, theirs, mine)
    rest = jnp.concatenate([low, high], axis=1)
    fast = jnp.concatenate([first[None], rest])[:, None]
    arguments = (rhs, boundary, diag_inv, off_blocks, coupling, present)
    return lax.cond(given_up, lambda fast, *arguments: plain(*arguments), lambda fast, *arguments: fast, fast, *arguments)


def solution(mesh):
    split = Mesh(mesh.devices.reshape(4, 4, 2, 4), ("z", "y", "core", "x"))
    in_specs = (
        P(None, ROWS, None, None),
        P(ROWS, None, None),
        P(None, ROWS, None, None),
        P(None, ROWS, "x", None, None),
        P(None, ROWS, "x"),
        P(None, ROWS, "x"),
    )
    return jax.shard_map(
        on_device, mesh=split, in_specs=in_specs, out_specs=P(None, ROWS, None, None), check_vma=False
    )
```

```python
import functools

import jax
import jax.numpy as jnp
from jax import lax
from jax.experimental import pallas as pl
from jax.experimental.pallas import tpu as pltpu
from jax.sharding import Mesh, PartitionSpec as P

ROWS = ("z", "y", "core")
VMEM_LIMIT = 48 * 1024 * 1024


def xor_pairs(n, k):
    return [(i, i ^ k) for i in range(n)]


def shift_pairs(n, k):
    return [(i, (i + k) % n) for i in range(n)]


def swap_cores(v):
    return lax.ppermute(v, "core", xor_pairs(2, 1))


def direct_gather(v, axis):
    return jnp.concatenate([v] + [lax.ppermute(v, axis, xor_pairs(4, k)) for k in (1, 2, 3)])


def ring_gather(v, axis):
    before = lax.ppermute(v, axis, shift_pairs(4, 1))
    after = lax.ppermute(v, axis, shift_pairs(4, 3))
    half = v.shape[0] // 2
    far_a = lax.ppermute(before[:half], axis, shift_pairs(4, 1))
    far_b = lax.ppermute(after[half:], axis, shift_pairs(4, 3))
    return [v, before, after, far_a, far_b]


def nt_dot(x, a):
    return lax.dot_general(x, a, (((1,), (1,)), ((), ())), preferred_element_type=jnp.float32)


GROUP = 8
UNROLL = 4
LATE_LIMIT = 60 * 1024 * 1024
CAPACITY = (10, 12, 14, 16, 17, 18)
FRESH_CAPACITY = 24
MIDDLE_CAPACITY = 52
CHUNKS = ((2, 3), (4, 5), (6,), (7,))


def chunk_of(level):
    for n, chunk in enumerate(CHUNKS):
        if level in chunk:
            before = sum(CAPACITY[one - 2] for one in chunk if one < level)
            return n, before, sum(CAPACITY[one - 2] for one in chunk)


def call(kernel, name, operands, in_spaces, outs, out_spaces, scratch, flops=0, bytes_accessed=0, limit=VMEM_LIMIT):
    return pl.pallas_call(
        kernel,
        out_shape=outs,
        in_specs=[pl.BlockSpec(memory_space=space) for space in in_spaces],
        out_specs=[pl.BlockSpec(memory_space=space) for space in out_spaces],
        scratch_shapes=scratch,
        compiler_params=pltpu.CompilerParams(vmem_limit_bytes=limit),
        cost_estimate=pl.CostEstimate(flops=flops, bytes_accessed=bytes_accessed, transcendentals=0),
        name=name,
    )(*operands)


def gather_sum(level, code_ref, picks, own_ref, other_ref, out_ref, blocks, block_sems):
    slots = code_ref.shape[1]
    per_row = slots // 2
    loads = [
        pltpu.make_async_copy(a_ref.at[level - 1, 0], blocks.at[pl.ds(r * per_row, per_row)], block_sems.at[r])
        for r, a_ref in enumerate((own_ref, other_ref))
    ]
    for r in range(2):
        loads[r].wait()
        total = None
        for g in range(r * per_row, (r + 1) * per_row, GROUP):
            xs, group = [], []
            for k in range(g, g + GROUP):
                code = code_ref[level - 1, k]
                kept = (code >= 0).astype(jnp.float32)
                xs.append((picks(k, jnp.maximum(code, 0)).astype(jnp.float32) * kept).astype(jnp.bfloat16))
                group.append(blocks[k])
            part = nt_dot(jnp.concatenate(xs, axis=1), jnp.concatenate(group, axis=1))
            total = part if total is None else total + part
        out_ref[r] = total


def start_blocks(levels, own_ref, other_ref, blocks, block_sems):
    per_row = blocks.shape[1] // 2
    for n, level in enumerate(levels):
        for r, a_ref in enumerate((own_ref, other_ref)):
            target = blocks.at[n, pl.ds(r * per_row, per_row)]
            pltpu.make_async_copy(a_ref.at[level - 1, 0], target, block_sems.at[n, r]).start()


def send_copies(source, copies_ref, sems):
    sends = [pltpu.make_async_copy(source, copies_ref.at[i], sems.at[i]) for i in range(copies_ref.shape[0])]
    for send in sends:
        send.start()
    for send in sends:
        send.wait()


def first_kernel(levels, code_ref, flag_ref, *refs):
    sources, refs = refs[:-11], refs[-11:]
    own_ref, other_ref, copies_ref, store_ref, blocks, block_sems, out_ref, copy_sems, pack_sems, packed, store_sem = refs
    start_blocks(levels, own_ref, other_ref, blocks, block_sems)
    packs, start = [], 0
    for i, source in enumerate(sources):
        packs.append(pltpu.make_async_copy(source, packed.at[pl.ds(start, source.shape[0])], pack_sems.at[i]))
        start += source.shape[0]
    for pack in packs:
        pack.start()
    for pack in packs:
        pack.wait()
    keep = pltpu.make_async_copy(packed, store_ref.at[pl.ds(0, start)], store_sem)
    keep.start()
    for n, level in enumerate(levels):
        gather_sum(
            level, code_ref, lambda k, code: packed[code], own_ref, other_ref, out_ref.at[n], blocks.at[n], block_sems.at[n]
        )
    out_ref[0] = out_ref[0] + jnp.where(flag_ref[0] > 0, jnp.float32(jnp.nan), jnp.float32(0.0))
    send_copies(out_ref, copies_ref, copy_sems)
    keep.wait()


def known_kernel(
    levels, code_ref, store_ref, own_ref, other_ref, copies_ref, blocks, block_sems, out_ref, copy_sems, picked, pick_sem
):
    slots = code_ref.shape[1]
    start_blocks(levels, own_ref, other_ref, blocks, block_sems)
    for n, level in enumerate(levels):

        def fetch(k, carry, n=n, level=level):
            place = jnp.maximum(code_ref[level - 1, k], 0)
            pltpu.make_async_copy(store_ref.at[place], picked.at[n * slots + k], pick_sem).start()
            return carry

        lax.fori_loop(0, slots, fetch, 0)
    pltpu.make_async_copy(store_ref.at[pl.ds(0, slots * len(levels))], picked, pick_sem).wait()
    for n, level in enumerate(levels):
        picks = lambda k, code, n=n: picked[n * slots + k]
        gather_sum(level, code_ref, picks, own_ref, other_ref, out_ref.at[n], blocks.at[n], block_sems.at[n])
    send_copies(out_ref, copies_ref, copy_sems)


def known_sums(levels, code, flag, sources, own, other):
    slots, one, some = code.shape[1], sources[0].shape[1:], len(levels)
    sums = jax.ShapeDtypeStruct((4, some, 2) + one, jnp.float32)
    scratch = [
        pltpu.VMEM((some, slots, one[1], one[1]), jnp.bfloat16),
        pltpu.SemaphoreType.DMA((some, 2)),
        pltpu.VMEM((some, 2) + one, jnp.float32),
        pltpu.SemaphoreType.DMA((4,)),
    ]
    cost = dict(
        flops=2 * some * slots * one[0] * one[1] * one[1], bytes_accessed=some * slots * one[1] * (one[1] + 2 * one[0]) * 4
    )
    spaces = [pl.ANY] * len(sources) + [pltpu.HBM] * 2
    if flag is None:
        scratch += [pltpu.VMEM((some * slots,) + one, jnp.bfloat16), pltpu.SemaphoreType.DMA]
        kernel = functools.partial(known_kernel, levels)
        operands = (code, *sources, own, other)
        return call(kernel, "known_sums", operands, [pltpu.SMEM] + spaces, [sums], [pltpu.HBM], scratch, limit=LATE_LIMIT, **cost)[0]
    known = sum(v.shape[0] for v in sources)
    scratch += [
        pltpu.SemaphoreType.DMA((len(sources),)),
        pltpu.VMEM((known,) + one, jnp.bfloat16),
        pltpu.SemaphoreType.DMA,
    ]
    store = jax.ShapeDtypeStruct((2048,) + one, jnp.bfloat16)
    kernel = functools.partial(first_kernel, levels)
    operands = (code, flag, *sources, own, other)
    spaces = [pltpu.SMEM] * 2 + spaces
    return call(kernel, "first_sums", operands, spaces, [sums, store], [pltpu.HBM, pltpu.HBM], scratch, **cost)


def near_kernel(levels, rank_ref, off_ref, out_ref, blocks, sem, out_sem):
    slots = rank_ref.shape[1]
    blocks[0] = jnp.zeros(blocks.shape[1:], blocks.dtype)

    def each(do):
        for level in levels:
            place = chunk_of(level)[1]

            def body(k, carry, level=level, place=place):
                @pl.when(rank_ref[level - 1, k] >= 0)
                def _():
                    target = place + rank_ref[level - 1, k]
                    do(pltpu.make_async_copy(off_ref.at[level - 1, 0, k], blocks.at[target], sem.at[target]))

                return carry

            lax.fori_loop(0, slots, body, 0)

    each(lambda copy: copy.start())
    each(lambda copy: copy.wait())
    store = pltpu.make_async_copy(blocks, out_ref, out_sem)
    store.start()
    store.wait()


def near_blocks(chunk, rank, off):
    block = off.shape[-1]
    size = sum(CAPACITY[one - 2] for one in chunk)
    out = jax.ShapeDtypeStruct((size, block, block), jnp.bfloat16)
    scratch = [
        pltpu.VMEM((size, block, block), jnp.bfloat16),
        pltpu.SemaphoreType.DMA((size,)),
        pltpu.SemaphoreType.DMA,
    ]
    kernel = functools.partial(near_kernel, chunk)
    return call(kernel, "near_blocks", (rank, off), [pltpu.SMEM, pltpu.HBM], [out], [pltpu.HBM], scratch)[0]


def add_listed(total, count, entry_of, block_of, solved_of, ready=None):
    def step(j, total):
        xs, blocks = [], []
        for t in range(UNROLL):
            i = j * UNROLL + t
            entry = entry_of(i)
            if ready is not None:
                ready(i)
            kept = ((entry >> 8) & 1).astype(jnp.float32)
            xs.append((solved_of(entry & 255).astype(jnp.float32) * kept).astype(jnp.bfloat16))
            blocks.append(block_of(i))
        return total + nt_dot(jnp.concatenate(xs, axis=1), jnp.concatenate(blocks, axis=1))

    return lax.fori_loop(0, (count + UNROLL - 1) // UNROLL, step, total)


def middle_kernel(level, counts_ref, fresh_ref, middle_ref, *refs):
    solved, refs = refs[: level - 2], refs[level - 2 :]
    own_ref, other_ref, out_ref, near_ref, blocks, sems, near_sems = refs[:7]
    fresh_max, middle_max = fresh_ref.shape[1], middle_ref.shape[1]
    at = 2 * (level - 1)
    rounded = lambda n: (n + UNROLL - 1) // UNROLL * UNROLL

    def copies(r, source):
        fresh = lambda i: pltpu.make_async_copy(
            source.at[fresh_ref[at + r, i] >> 9], near_ref.at[r * fresh_max + i], near_sems.at[r * fresh_max + i]
        )
        middle = lambda i: pltpu.make_async_copy(
            source.at[middle_ref[at + r, i] >> 9], blocks.at[r * middle_max + i], sems.at[r * middle_max + i]
        )
        return fresh, middle

    def each(count, do):
        def body(i, carry):
            do(i)
            return carry

        lax.fori_loop(0, rounded(count), body, 0)

    for r, source in enumerate((own_ref, other_ref)):
        fresh, middle = copies(r, source)
        if solved:
            each(counts_ref[1, at + r], lambda i: middle(i).start())
        each(counts_ref[0, at + r], lambda i: fresh(i).start())
    if solved:
        solved_ref = refs[7]
        for i, one in enumerate(solved):
            solved_ref[i * one.shape[0] : (i + 1) * one.shape[0]] = one[...]
    for r, source in enumerate((own_ref, other_ref)):
        _, middle = copies(r, source)
        total = jnp.zeros(out_ref.shape[1:], jnp.float32)
        if solved:
            total = add_listed(
                total,
                counts_ref[1, at + r],
                lambda i: middle_ref[at + r, i],
                lambda i: blocks[r * middle_max + i],
                lambda place: solved_ref[place],
                lambda i: middle(i).wait(),
            )
        out_ref[r] = total
    for r, source in enumerate((own_ref, other_ref)):
        fresh, _ = copies(r, source)
        each(counts_ref[0, at + r], lambda i: fresh(i).wait())


def middle_sum(level, counts, fresh, middle, solved, own, other, rhs_cols):
    block = own.shape[-1]
    one = (rhs_cols, block)
    outs = [
        jax.ShapeDtypeStruct((2,) + one, jnp.float32),
        jax.ShapeDtypeStruct((2 * fresh.shape[1], block, block), jnp.bfloat16),
    ]
    scratch = [
        pltpu.VMEM((2 * middle.shape[1], block, block), jnp.bfloat16),
        pltpu.SemaphoreType.DMA((2 * middle.shape[1],)),
        pltpu.SemaphoreType.DMA((2 * fresh.shape[1],)),
    ]
    if solved:
        scratch.append(pltpu.VMEM((sum(v.shape[0] for v in solved),) + one, jnp.bfloat16))
    spaces = [pltpu.SMEM] * 3 + [pltpu.VMEM] * len(solved) + [pltpu.HBM] * 2
    operands = (counts, fresh, middle, *solved, own, other)
    kernel = functools.partial(middle_kernel, level)
    return call(
        kernel, "middle_sum", operands, spaces, outs, [pltpu.VMEM] * 2, scratch, 2 * 40 * rhs_cols * block**2, 8 << 20, LATE_LIMIT
    )


def solve_kernel(level, at, last, *refs):
    near = level > 1
    if near:
        (counts_ref, fresh_ref, middle_ref, near_ref, solved_ref), refs = refs[:5], refs[5:]
    sums, rhs_ref, own_d_ref, other_d_ref, out_ref = refs[:5]
    for r, d_ref in enumerate((own_d_ref, other_d_ref)):
        coupled = (sums[0, at, r] + sums[1, at, r]) + (sums[2, at, r] + sums[3, at, r])
        if near:
            row = 2 * (level - 1) + r
            first = level - 2
            place = first * 32
            fresh_max = fresh_ref.shape[1]
            coupled = add_listed(
                coupled + middle_ref[r],
                counts_ref[0, row],
                lambda i: fresh_ref[row, i],
                lambda i: near_ref[r * fresh_max + i],
                lambda code: solved_ref[jnp.maximum(code - place, 0)],
            )
        reduced = (rhs_ref[level, r].astype(jnp.float32) - coupled).astype(jnp.bfloat16)
        solved = nt_dot(reduced, d_ref[level, 0]).astype(jnp.bfloat16)
        out_ref[r] = solved
        if not last:
            refs[6][lax.axis_index("core") ^ r] = solved
    if not last:
        all_ref, both, sems = refs[5:]
        send_copies(both, all_ref, sems)


def solve_level(level, at, near, sums, rhs, own_d, other_d, copies):
    one = sums.shape[3:]
    outs, spaces, scratch = [jax.ShapeDtypeStruct((2,) + one, jnp.bfloat16)], [pltpu.VMEM], []
    if copies:
        outs.append(jax.ShapeDtypeStruct((copies, 2) + one, jnp.bfloat16))
        spaces.append(pltpu.HBM)
        scratch = [pltpu.VMEM((2,) + one, jnp.bfloat16), pltpu.SemaphoreType.DMA((copies,))]
    in_spaces = ([pltpu.SMEM] * 2 + [pltpu.VMEM] * 3 if near else []) + [pltpu.VMEM] * 4
    kernel = functools.partial(solve_kernel, level, at, not copies)
    return call(
        kernel, "solve_level", (*near, sums, rhs, own_d, other_d), in_spaces, outs, spaces, scratch, limit=LATE_LIMIT
    )


def plain(rhs, boundary, diag_inv, off_blocks, coupling, present):
    levels, _, rhs_cols, block = rhs.shape
    outer_all = lax.all_gather(boundary, ROWS, axis=0, tiled=True)
    outer, width = outer_all.shape[0], 32
    empty = jnp.zeros((levels * width, rhs_cols, block), jnp.bfloat16)
    solved = jnp.concatenate([outer_all, empty], axis=0)
    results = []
    for level in range(levels):
        target = rhs[level, 0].astype(jnp.float32)
        if level > 0:
            picked = jnp.take(solved, coupling[level - 1, 0], axis=0)
            picked = picked * present[level - 1, 0].astype(jnp.bfloat16)[:, None, None]
            partial_value = jnp.einsum(
                "kab,krb->ra", off_blocks[level - 1, 0], picked, preferred_element_type=jnp.float32
            )
            target = target - lax.psum(partial_value, "x")
        own = jnp.einsum(
            "rb,ab->ra", target.astype(jnp.bfloat16), diag_inv[level, 0], preferred_element_type=jnp.float32
        ).astype(jnp.bfloat16)
        fresh = lax.all_gather(own[None], ROWS, axis=0, tiled=True)
        solved = solved.at[outer + level * width : outer + (level + 1) * width].set(fresh)
        results.append(own)
    return jnp.stack(results)[:, None]


def tied(value, to):
    return lax.optimization_barrier((value, to))


def on_device(rhs, boundary, diag_inv, off_blocks, coupling, present):
    levels, _, rhs_cols, block = rhs.shape
    outer_each = boundary.shape[0]
    outer = outer_each * 32
    half = rhs_cols // 2
    z, y, core, x = (lax.axis_index(a) for a in ("z", "y", "core", "x"))

    def my_half(v, axis):
        return lax.dynamic_slice_in_dim(v, core * half, half, axis)

    def their_half(v, axis):
        return lax.dynamic_slice_in_dim(v, (1 - core) * half, half, axis)

    first = jnp.einsum("rb,ab->ra", rhs[0, 0], diag_inv[0, 0], preferred_element_type=jnp.float32).astype(jnp.bfloat16)
    known = jnp.concatenate([boundary, first[None]])
    known_own, known_other = tied(my_half(known, 1), swap_cores(their_half(known, 1)))

    code_own = (coupling + 1024 * present)[:, 0]
    inside = lambda code: (code >= 1024 + outer + 32) & (jnp.arange(levels - 1) > 0)[:, None]
    own_inside = inside(code_own)
    limits = jnp.array((0,) + CAPACITY, jnp.int32)[:, None]
    own_rank = jnp.cumsum(own_inside.astype(jnp.int32), axis=1) - 1
    own_rank = jnp.where(own_inside & (own_rank < limits), own_rank, -1)
    own_rank, known_own = tied(own_rank, known_own)
    nears = [near_blocks(chunk, own_rank, off_blocks) for chunk in CHUNKS]
    near_own = [lax.all_gather(v, "x", axis=0, tiled=True) for v in nears]
    near_other = {}

    def swap_chunk(n, after):
        near_other[n] = swap_cores(tied(near_own[n], after)[0])

    code_both = jnp.stack([code_own, swap_cores(code_own)], axis=1)
    rhs_both = jnp.concatenate([my_half(rhs, 2), swap_cores(their_half(rhs, 2))], axis=1)
    diag_other = swap_cores(diag_inv)
    off_sent, known_own = tied(off_blocks, known_own)
    off_other = swap_cores(off_sent)

    color_a = ring_gather(direct_gather(known_own, "z"), "y")
    color_b = ring_gather(direct_gather(known_other, "y"), "z")

    keep, index = code_both >= 1024, code_both % 1024
    in_outer = index < outer
    row = jnp.where(in_outer, index // outer_each, index - outer)
    member = jnp.where(in_outer, index % outer_each, outer_each)
    src_z, src_y, src_core = row // 8, (row // 2) % 4, row % 2
    each = outer_each + 1
    mine_too = src_core == core
    away = jnp.where(mine_too, src_y - y, src_z - z) % 4
    place = jnp.where(mine_too, src_z ^ z, src_y ^ y) * each + member
    slot_of = jnp.where(away == 3, 1, jnp.where(away == 1, 2, jnp.where(away == 2, 3, 0)))
    known_place = jnp.where(mine_too, 0, 16 * each) + slot_of * (4 * each) + place
    known_code = jnp.where(keep & (index < outer + 32), known_place, -1).reshape(levels - 1, -1)
    known_code, _ = tied(known_code, nears)

    code_late, _ = tied(code_both, color_a[1])
    every = jnp.stack([code_both] + [lax.ppermute(code_late, "x", xor_pairs(4, k)) for k in (1, 2, 3)], axis=2)
    this = jnp.arange(levels - 1)[:, None, None, None]
    every_inside = (every >= 1024 + outer + 32) & (this > 0)
    rank = jnp.cumsum(every_inside.astype(jnp.int32), axis=3) - 1
    solved_place = every - (1024 + outer + 32)
    at_x = (x ^ jnp.arange(4))[:, None]
    chunk_size = jnp.array([0] + [chunk_of(level)[2] for level in range(2, levels)], jnp.int32)[:, None, None, None]
    chunk_start = jnp.array([0] + [chunk_of(level)[1] for level in range(2, levels)], jnp.int32)[:, None, None, None]
    entry = (at_x * chunk_size + chunk_start + rank) * 512 + 256 + solved_place
    is_fresh = every_inside & (solved_place >= (this - 1) * 32)
    is_middle = every_inside & ~is_fresh

    def listed(chosen, capacity):
        entries = jnp.where(chosen, entry, 0).reshape(2 * (levels - 1), -1)
        return -lax.sort(-entries, dimension=1)[:, :capacity], jnp.sum(chosen, axis=(2, 3), dtype=jnp.int32).reshape(-1)

    fresh_list, fresh_count = listed(is_fresh, FRESH_CAPACITY)
    middle_list, middle_count = listed(is_middle, MIDDLE_CAPACITY)
    inside_count = jnp.sum(every_inside, axis=3, dtype=jnp.int32)
    over = jnp.any(inside_count > limits[:, :, None]) | jnp.any(fresh_count > FRESH_CAPACITY)
    over = over | jnp.any(middle_count > MIDDLE_CAPACITY)
    flag = over.astype(jnp.int32).reshape(1)
    counts = jnp.stack([jnp.minimum(fresh_count, FRESH_CAPACITY), jnp.minimum(middle_count, MIDDLE_CAPACITY)])
    in_reach = lambda entries: jnp.minimum(entries, (4 * jnp.repeat(chunk_size.reshape(-1), 2)[:, None] - 1) * 512 + 511)
    fresh_list, middle_list = in_reach(fresh_list), in_reach(middle_list)
    fresh_list, middle_list = jnp.maximum(fresh_list, 0), jnp.maximum(middle_list, 0)

    def over_x(value):
        return lax.all_to_all(value, "x", 0, 0)

    batches = ((1, 2), (3, 4), (5, 6), (7,))
    value, store = known_sums(batches[0], known_code, flag, color_a + color_b, off_blocks, off_other)
    swap_chunk(0, value)
    spread = over_x(value)
    sums = {level: (spread, n) for n, level in enumerate(batches[0])}
    own_rows, other_rows, solved_levels, near = [], [], [], ()
    for level in range(1, levels):
        last = level == levels - 1
        spread, at = sums[level]
        outs = solve_level(level, at, near, spread, rhs_both, diag_inv, diag_other, 0 if last else 16)
        own_rows.append(outs[0][0])
        other_rows.append(outs[0][1])
        if last:
            break
        counts_now, sent = tied(counts, outs[1])
        solved = lax.all_to_all(sent, ("z", "y"), 0, 0).reshape(32, half, block)
        if level % 2 == 1 and level // 2 + 1 < len(batches):
            batch = batches[level // 2 + 1]
            value = known_sums(batch, tied(known_code, sent)[0], None, [store], off_blocks, off_other)
            solved, value = tied(solved, value)
        elif level % 2 == 0:
            spread = over_x(tied(value, sent)[0])
            sums.update({one: (spread, n) for n, one in enumerate(batch)})
        for n, chunk in enumerate(CHUNKS):
            if n > 0 and chunk[0] == level + 2:
                swap_chunk(n, sent)
        n = chunk_of(level + 1)[0]
        middle, near_now = middle_sum(
            level + 1, counts_now, fresh_list, middle_list, solved_levels, near_own[n], near_other[n], half
        )
        near = (counts, fresh_list, middle, near_now, solved)
        solved_levels = solved_levels + [solved]

    given_up = jnp.any(solved_levels[0] != solved_levels[0])
    mine = jnp.stack(own_rows)
    theirs = swap_cores(jnp.stack(other_rows))
    low = jnp.where(core == 0, mine, theirs)
    high = jnp.where(core == 0, theirs, mine)
    rest = jnp.concatenate([low, high], axis=1)
    fast = jnp.concatenate([first[None], rest])[:, None]
    arguments = (rhs, boundary, diag_inv, off_blocks, coupling, present)
    return lax.cond(given_up, lambda fast, *arguments: plain(*arguments), lambda fast, *arguments: fast, fast, *arguments)


def solution(mesh):
    split = Mesh(mesh.devices.reshape(4, 4, 2, 4), ("z", "y", "core", "x"))
    in_specs = (
        P(None, ROWS, None, None),
        P(ROWS, None, None),
        P(None, ROWS, None, None),
        P(None, ROWS, "x", None, None),
        P(None, ROWS, "x"),
        P(None, ROWS, "x"),
    )
    return jax.shard_map(
        on_device, mesh=split, in_specs=in_specs, out_specs=P(None, ROWS, None, None), check_vma=False
    )
```

```python
import functools

import jax
import jax.numpy as jnp
from jax import lax
from jax.experimental import pallas as pl
from jax.experimental.pallas import tpu as pltpu
from jax.sharding import Mesh, PartitionSpec as P

ROWS = ("z", "y", "core")
VMEM_LIMIT = 48 * 1024 * 1024


def xor_pairs(n, k):
    return [(i, i ^ k) for i in range(n)]


def shift_pairs(n, k):
    return [(i, (i + k) % n) for i in range(n)]


def swap_cores(v):
    return lax.ppermute(v, "core", xor_pairs(2, 1))


def pairs(stage, move):
    result = []
    for z in range(4):
        for y in range(4):
            for core in range(2):
                to_z, to_y = (move(z), y) if core + 1 == stage else (z, move(y))
                result.append(((z * 4 + y) * 2 + core, (to_z * 4 + to_y) * 2 + core))
    return result


def direct_gather(v):
    return jnp.stack([v] + [lax.ppermute(v, ROWS, pairs(1, lambda i, k=k: i ^ k)) for k in (1, 2, 3)])


def ring_gather(v):
    up, down = pairs(2, lambda i: (i + 1) % 4), pairs(2, lambda i: (i + 3) % 4)
    before, after = lax.ppermute(v, ROWS, up), lax.ppermute(v, ROWS, down)
    half = v.shape[0] // 2
    return [v, before, after, lax.ppermute(before[:half], ROWS, up), lax.ppermute(after[half:], ROWS, down)]


def nt_dot(x, a):
    return lax.dot_general(x, a, (((1,), (1,)), ((), ())), preferred_element_type=jnp.float32)


GROUP = 8
NEAR = 16


def gather_sum(level, code_ref, picks, known, solved_ref, own_ref, other_ref, out_ref, blocks, block_sems, between):
    slots = code_ref.shape[1]
    per_row = slots // 2
    loads = [
        pltpu.make_async_copy(a_ref.at[level - 1, 0], blocks.at[pl.ds(r * per_row, per_row)], block_sems.at[r])
        for r, a_ref in enumerate((own_ref, other_ref))
    ]
    for load in loads:
        load.start()
    between()
    for r in range(2):
        loads[r].wait()
        total = None
        for g in range(r * per_row, (r + 1) * per_row, GROUP):
            xs, group = [], []
            for k in range(g, g + GROUP):
                code = code_ref[level - 1, k]
                kept = (code >= 0).astype(jnp.float32)
                picked = picks(k, jnp.clip(code, 0, known - 1))
                if solved_ref is not None:
                    picked = jnp.where(code >= known, solved_ref[jnp.maximum(code - known, 0)], picked)
                xs.append((picked.astype(jnp.float32) * kept).astype(jnp.bfloat16))
                group.append(blocks[k])
            part = nt_dot(jnp.concatenate(xs, axis=1), jnp.concatenate(group, axis=1))
            total = part if total is None else total + part
        out_ref[r] = total


def first_kernel(code_ref, *refs):
    sources, refs = refs[:-9], refs[-9:]
    own_ref, other_ref, out_ref, store_ref, blocks, block_sems, pack_sems, packed, store_sem = refs
    packs, start = [], 0
    for i, source in enumerate(sources):
        which = 0 if i < len(sources) // 2 else 1
        for part in range(source.shape[0]):
            target = packed.at[pl.ds(start, source.shape[2])]
            packs.append(pltpu.make_async_copy(source.at[part, which], target, pack_sems.at[len(packs)]))
            start += source.shape[2]
    keep = pltpu.make_async_copy(packed, store_ref.at[pl.ds(0, start)], store_sem)

    def between():
        for pack in packs:
            pack.start()
        for pack in packs:
            pack.wait()
        keep.start()

    picks = lambda k, code: packed[code]
    gather_sum(1, code_ref, picks, start, None, own_ref, other_ref, out_ref, blocks, block_sems, between)
    keep.wait()


def old_kernel(level, known, code_ref, fresh_ref, store_ref, *refs):
    solved, refs = refs[: level - 2], refs[level - 2 :]
    own_ref, other_ref, out_ref, list_ref, near_ref, blocks, block_sems, picked, pick_sem = refs[:9]
    solved_ref = refs[9] if solved else None
    slots = code_ref.shape[1]

    def between():
        for k in range(slots):
            place = jnp.clip(code_ref[level - 1, k], 0, known - 1)
            pltpu.make_async_copy(store_ref.at[place], picked.at[k], pick_sem).start()
        for i, one in enumerate(solved):
            solved_ref[i * one.shape[0] : (i + 1) * one.shape[0]] = one[...]
        pltpu.make_async_copy(store_ref.at[pl.ds(0, slots)], picked, pick_sem).wait()

    picks = lambda k, code: picked[k]
    gather_sum(level, code_ref, picks, known, solved_ref, own_ref, other_ref, out_ref, blocks, block_sems, between)

    def note(slot, count):
        code = fresh_ref[level - 1, slot]

        @pl.when(code >= 0)
        def _():
            list_ref[1 + count] = code * 1024 + slot

        @pl.when((code >= 0) & (count < NEAR))
        def _():
            near_ref[count] = blocks[slot]

        return count + (code >= 0).astype(jnp.int32)

    list_ref[0] = lax.fori_loop(0, fresh_ref.shape[1], note, jnp.int32(0))


def sum_call(kernel, codes, sources, source_spaces, own, other, outs, out_spaces, extra, name):
    slots, (rhs_cols, block) = codes[0].shape[1], sources[0].shape[-2:]
    return pl.pallas_call(
        kernel,
        out_shape=[jax.ShapeDtypeStruct((2, rhs_cols, block), jnp.float32)] + outs,
        in_specs=[pl.BlockSpec(memory_space=pltpu.SMEM)] * len(codes)
        + [pl.BlockSpec(memory_space=space) for space in source_spaces]
        + [pl.BlockSpec(memory_space=pltpu.HBM)] * 2,
        out_specs=[pl.BlockSpec(memory_space=space) for space in [pltpu.VMEM] + out_spaces],
        scratch_shapes=[pltpu.VMEM((slots, block, block), jnp.bfloat16), pltpu.SemaphoreType.DMA((2,))] + extra,
        compiler_params=pltpu.CompilerParams(vmem_limit_bytes=VMEM_LIMIT),
        cost_estimate=pl.CostEstimate(
            flops=2 * slots * rhs_cols * block * block,
            bytes_accessed=slots * block * (block + 2 * rhs_cols) * 4,
            transcendentals=0,
        ),
        name=name,
    )(*codes, *sources, own, other)


def first_sum(code, sources, own, other):
    one = sources[0].shape[3:]
    parts = sum(v.shape[0] for v in sources)
    known = parts * sources[0].shape[2]
    store = jax.ShapeDtypeStruct((2048,) + one, jnp.bfloat16)
    extra = [
        pltpu.SemaphoreType.DMA((parts,)),
        pltpu.VMEM((known,) + one, jnp.bfloat16),
        pltpu.SemaphoreType.DMA,
    ]
    spaces = [pl.ANY] * len(sources)
    return sum_call(first_kernel, [code], sources, spaces, own, other, [store], [pltpu.HBM], extra, "first_sum")


def old_sum(level, known, code, fresh, store, solved, own, other):
    one = store.shape[1:]
    outs = [
        jax.ShapeDtypeStruct((code.shape[1] + 1,), jnp.int32),
        jax.ShapeDtypeStruct((NEAR, one[1], one[1]), jnp.bfloat16),
    ]
    kernel = functools.partial(old_kernel, level, known)
    extra = [pltpu.VMEM((code.shape[1],) + one, jnp.bfloat16), pltpu.SemaphoreType.DMA]
    if solved:
        extra.append(pltpu.VMEM((sum(v.shape[0] for v in solved),) + one, jnp.bfloat16))
    spaces = [pl.ANY] + [pltpu.VMEM] * len(solved)
    out_spaces = [pltpu.SMEM, pltpu.VMEM]
    return sum_call(kernel, [code, fresh], [store] + solved, spaces, own, other, outs, out_spaces, extra, "old_sum")


def fresh_kernel(level, list_ref, old_ref, x_ref, near_ref, own_ref, other_ref, out_ref, far, sem):
    per_row = own_ref.shape[2]
    out_ref[...] = old_ref[...]
    count = list_ref[0]

    def add(block, entry):
        row = ((entry & 1023) >= per_row).astype(jnp.int32)
        out_ref[row] += nt_dot(x_ref[entry >> 10], block)

    def add_near(n, carry):
        add(near_ref[n], list_ref[1 + n])
        return carry

    def add_far(n, carry):
        slot = list_ref[1 + n] & 1023

        @pl.when(slot < per_row)
        def _():
            pltpu.make_async_copy(own_ref.at[level - 1, 0, slot], far, sem).start()

        @pl.when(slot >= per_row)
        def _():
            pltpu.make_async_copy(other_ref.at[level - 1, 0, slot - per_row], far, sem).start()

        pltpu.make_async_copy(own_ref.at[level - 1, 0, 0], far, sem).wait()
        add(far[...], list_ref[1 + n])
        return carry

    lax.fori_loop(0, jnp.minimum(count, NEAR), add_near, 0)
    lax.fori_loop(NEAR, count, add_far, 0)


def fresh_sum(level, listed, solved, old, near, own, other):
    block = solved.shape[-1]
    vmem = pl.BlockSpec(memory_space=pltpu.VMEM)
    return pl.pallas_call(
        functools.partial(fresh_kernel, level),
        out_shape=jax.ShapeDtypeStruct(old.shape, jnp.float32),
        in_specs=[pl.BlockSpec(memory_space=pltpu.SMEM)] + [vmem] * 3 + [pl.BlockSpec(memory_space=pltpu.HBM)] * 2,
        out_specs=vmem,
        scratch_shapes=[pltpu.VMEM((block, block), jnp.bfloat16), pltpu.SemaphoreType.DMA],
        compiler_params=pltpu.CompilerParams(vmem_limit_bytes=VMEM_LIMIT),
        name="fresh_sum",
    )(listed, old, solved, near, own, other)


def solve_kernel(level, p0, p1, p2, p3, rhs_ref, own_d_ref, other_d_ref, out_ref, *refs):
    core = lax.axis_index("core")
    for r, d_ref in enumerate((own_d_ref, other_d_ref)):
        coupled = (p0[r] + p1[r]) + (p2[r] + p3[r])
        reduced = (rhs_ref[level, r].astype(jnp.float32) - coupled).astype(jnp.bfloat16)
        solved = nt_dot(reduced, d_ref[level, 0]).astype(jnp.bfloat16)
        out_ref[r] = solved
        if refs:
            refs[1][core ^ r] = solved
    if refs:
        all_ref, both, sems = refs
        sends = [pltpu.make_async_copy(both, all_ref.at[i], sems.at[i]) for i in range(all_ref.shape[0])]
        for send in sends:
            send.start()
        for send in sends:
            send.wait()


def solve_level(level, partials, rhs, own_d, other_d, copies):
    _, rhs_cols, block = partials[0].shape
    vmem = pl.BlockSpec(memory_space=pltpu.VMEM)
    out_shape, out_specs, scratch = [jax.ShapeDtypeStruct((2, rhs_cols, block), jnp.bfloat16)], [vmem], []
    if copies:
        out_shape.append(jax.ShapeDtypeStruct((copies, 2, rhs_cols, block), jnp.bfloat16))
        out_specs.append(pl.BlockSpec(memory_space=pltpu.HBM))
        scratch = [pltpu.VMEM((2, rhs_cols, block), jnp.bfloat16), pltpu.SemaphoreType.DMA((copies,))]
    return pl.pallas_call(
        functools.partial(solve_kernel, level),
        out_shape=out_shape,
        in_specs=[vmem] * 7,
        out_specs=out_specs,
        scratch_shapes=scratch,
        compiler_params=pltpu.CompilerParams(vmem_limit_bytes=VMEM_LIMIT),
        name="solve_level",
    )(*partials, rhs, own_d, other_d)


def on_device(rhs, boundary, diag_inv, off_blocks, coupling, present):
    levels, _, rhs_cols, block = rhs.shape
    outer_each = boundary.shape[0]
    outer = outer_each * 32
    half = rhs_cols // 2
    z, y, core = lax.axis_index("z"), lax.axis_index("y"), lax.axis_index("core")

    def my_half(v, axis):
        return lax.dynamic_slice_in_dim(v, core * half, half, axis)

    def their_half(v, axis):
        return lax.dynamic_slice_in_dim(v, (1 - core) * half, half, axis)

    first = jnp.einsum("rb,ab->ra", rhs[0, 0], diag_inv[0, 0], preferred_element_type=jnp.float32).astype(jnp.bfloat16)
    known = jnp.concatenate([boundary, first[None]])
    known = jnp.stack([my_half(known, 1), their_half(known, 1)])
    code_own = (coupling + 1024 * present)[:, 0]
    code_both = jnp.stack([code_own, swap_cores(code_own)], axis=1)
    rhs_both = jnp.concatenate([my_half(rhs, 2), swap_cores(their_half(rhs, 2))], axis=1)
    diag_other = swap_cores(diag_inv)
    off_sent, known = lax.optimization_barrier((off_blocks, known))
    off_other = swap_cores(off_sent)

    pieces = ring_gather(direct_gather(known))
    pieces = pieces + [swap_cores(piece) for piece in pieces]

    keep, index = code_both >= 1024, code_both % 1024
    in_outer = index < outer
    row = jnp.where(in_outer, index // outer_each, index - outer)
    member = jnp.where(in_outer, index % outer_each, outer_each)
    src_z, src_y, src_core = row // 8, (row // 2) % 4, row % 2
    each = outer_each + 1
    away = jnp.where(src_core == 0, src_y - y, src_z - z) % 4
    part = jnp.where(away == 3, 1, jnp.where(away == 1, 2, jnp.where(away == 2, 3, 0))) * 4
    part = part + jnp.where(src_core == 0, src_z ^ z, src_y ^ y) + jnp.where(src_core == core, 0, 16)
    known_place = part * each + member
    level_of = jnp.maximum(index - outer, 0) // 32
    this = jnp.arange(levels - 1)[:, None, None]
    is_fresh = (level_of == this) & (level_of > 0)
    place_level = (index - outer) % 32
    old_code = jnp.where(level_of == 0, known_place, 32 * each + (level_of - 1) * 32 + place_level)
    old_code = jnp.where(keep & ~is_fresh, old_code, -1).reshape(levels - 1, -1)
    fresh_code = jnp.where(keep & is_fresh, place_level, -1).reshape(levels - 1, -1)

    own_rows, other_rows = [], []
    value, store = first_sum(old_code, pieces, off_blocks, off_other)
    solved_levels = []
    for level in range(1, levels):
        partials = [value] + [lax.ppermute(value, "x", xor_pairs(4, k)) for k in (1, 2, 3)]
        last = level == levels - 1
        outs = solve_level(level, partials, rhs_both, diag_inv, diag_other, 0 if last else 16)
        own_rows.append(outs[0][0])
        other_rows.append(outs[0][1])
        if not last:
            next_fresh, sent = lax.optimization_barrier((fresh_code, outs[1]))
            solved = lax.all_to_all(sent, ("z", "y"), 0, 0).reshape(32, half, block)
            old, listed, near = old_sum(
                level + 1, 32 * each, old_code, next_fresh, store, solved_levels, off_blocks, off_other
            )
            value = fresh_sum(level + 1, listed, solved, old, near, off_blocks, off_other)
            solved_levels = solved_levels + [solved]

    mine = jnp.stack(own_rows)
    theirs = swap_cores(jnp.stack(other_rows))
    low = jnp.where(core == 0, mine, theirs)
    high = jnp.where(core == 0, theirs, mine)
    rest = jnp.concatenate([low, high], axis=1)
    return jnp.concatenate([first[None], rest])[:, None]


def solution(mesh):
    split = Mesh(mesh.devices.reshape(4, 4, 2, 4), ("z", "y", "core", "x"))
    in_specs = (
        P(None, ROWS, None, None),
        P(ROWS, None, None),
        P(None, ROWS, None, None),
        P(None, ROWS, "x", None, None),
        P(None, ROWS, "x"),
        P(None, ROWS, "x"),
    )
    return jax.shard_map(
        on_device, mesh=split, in_specs=in_specs, out_specs=P(None, ROWS, None, None), check_vma=False
    )
```

```python
import functools

import jax
import jax.numpy as jnp
from jax import lax
from jax.experimental import pallas as pl
from jax.experimental.pallas import tpu as pltpu
from jax.sharding import Mesh, PartitionSpec as P

ROWS = ("z", "y", "core")
VMEM_LIMIT = 48 * 1024 * 1024


def xor_pairs(n, k):
    return [(i, i ^ k) for i in range(n)]


def shift_pairs(n, k):
    return [(i, (i + k) % n) for i in range(n)]


def swap_cores(v):
    return lax.ppermute(v, "core", xor_pairs(2, 1))


def pairs(stage, move):
    result = []
    for z in range(4):
        for y in range(4):
            for core in range(2):
                to_z, to_y = (move(z), y) if core + 1 == stage else (z, move(y))
                result.append(((z * 4 + y) * 2 + core, (to_z * 4 + to_y) * 2 + core))
    return result


def gather_parts(v):
    near = [lax.ppermute(v, ROWS, pairs(1, lambda i, k=k: i ^ k)) for k in (1, 2, 3)]
    low, high = jnp.stack([v, near[0]]), jnp.stack(near[1:])
    up, down = pairs(2, lambda i: (i + 1) % 4), pairs(2, lambda i: (i + 3) % 4)
    before_low, after_high = lax.ppermute(low, ROWS, up), lax.ppermute(high, ROWS, down)
    before_high, after_low = lax.ppermute(high, ROWS, up), lax.ppermute(low, ROWS, down)
    far = [lax.ppermute(before_low, ROWS, up), lax.ppermute(after_high, ROWS, down)]
    return [low, high, before_low, before_high, after_low, after_high] + far


def nt_dot(x, a):
    return lax.dot_general(x, a, (((1,), (1,)), ((), ())), preferred_element_type=jnp.float32)


GROUP = 8
NEAR = 16


def gather_sum(level, code_ref, picks, known, solved_ref, own_ref, other_ref, out_ref, blocks, block_sems, between):
    slots = code_ref.shape[1]
    per_row = slots // 2
    loads = [
        pltpu.make_async_copy(a_ref.at[level - 1, 0], blocks.at[pl.ds(r * per_row, per_row)], block_sems.at[r])
        for r, a_ref in enumerate((own_ref, other_ref))
    ]
    for load in loads:
        load.start()
    between()
    for r in range(2):
        loads[r].wait()
        total = None
        for g in range(r * per_row, (r + 1) * per_row, GROUP):
            xs, group = [], []
            for k in range(g, g + GROUP):
                code = code_ref[level - 1, k]
                kept = (code >= 0).astype(jnp.float32)
                picked = picks(k, jnp.clip(code, 0, known - 1))
                if solved_ref is not None:
                    picked = jnp.where(code >= known, solved_ref[jnp.maximum(code - known, 0)], picked)
                xs.append((picked.astype(jnp.float32) * kept).astype(jnp.bfloat16))
                group.append(blocks[k])
            part = nt_dot(jnp.concatenate(xs, axis=1), jnp.concatenate(group, axis=1))
            total = part if total is None else total + part
        out_ref[r] = total.astype(out_ref.dtype)


def first_kernel(code_ref, *refs):
    sources, refs = refs[:-9], refs[-9:]
    own_ref, other_ref, out_ref, store_ref, blocks, block_sems, pack_sems, packed, store_sem = refs
    packs, start = [], 0
    for i, source in enumerate(sources):
        which = 0 if i < len(sources) // 2 else 1
        for part in range(source.shape[0]):
            target = packed.at[pl.ds(start, source.shape[2])]
            packs.append(pltpu.make_async_copy(source.at[part, which], target, pack_sems.at[len(packs)]))
            start += source.shape[2]
    keep = pltpu.make_async_copy(packed, store_ref.at[pl.ds(0, start)], store_sem)

    def between():
        for pack in packs:
            pack.start()
        for pack in packs:
            pack.wait()
        keep.start()

    picks = lambda k, code: packed[code]
    gather_sum(1, code_ref, picks, start, None, own_ref, other_ref, out_ref, blocks, block_sems, between)
    keep.wait()


def old_kernel(level, known, code_ref, fresh_ref, store_ref, *refs):
    solved, refs = refs[: level - 2], refs[level - 2 :]
    own_ref, other_ref, out_ref, list_ref, near_ref, blocks, block_sems, picked, pick_sem = refs[:9]
    solved_ref = refs[9] if solved else None
    slots = code_ref.shape[1]

    def between():
        for k in range(slots):
            place = jnp.clip(code_ref[level - 1, k], 0, known - 1)
            pltpu.make_async_copy(store_ref.at[place], picked.at[k], pick_sem).start()
        for i, one in enumerate(solved):
            solved_ref[i * one.shape[0] : (i + 1) * one.shape[0]] = one[...]
        pltpu.make_async_copy(store_ref.at[pl.ds(0, slots)], picked, pick_sem).wait()

    picks = lambda k, code: picked[k]
    gather_sum(level, code_ref, picks, known, solved_ref, own_ref, other_ref, out_ref, blocks, block_sems, between)

    def note(slot, count):
        code = fresh_ref[level - 1, slot]

        @pl.when(code >= 0)
        def _():
            list_ref[1 + count] = code * 1024 + slot

        @pl.when((code >= 0) & (count < NEAR))
        def _():
            near_ref[count] = blocks[slot]

        return count + (code >= 0).astype(jnp.int32)

    list_ref[0] = lax.fori_loop(0, fresh_ref.shape[1], note, jnp.int32(0))


def sum_call(kernel, codes, sources, source_spaces, own, other, outs, out_spaces, extra, name, kind):
    slots, (rhs_cols, block) = codes[0].shape[1], sources[0].shape[-2:]
    return pl.pallas_call(
        kernel,
        out_shape=[jax.ShapeDtypeStruct((2, rhs_cols, block), kind)] + outs,
        in_specs=[pl.BlockSpec(memory_space=pltpu.SMEM)] * len(codes)
        + [pl.BlockSpec(memory_space=space) for space in source_spaces]
        + [pl.BlockSpec(memory_space=pltpu.HBM)] * 2,
        out_specs=[pl.BlockSpec(memory_space=space) for space in [pltpu.VMEM] + out_spaces],
        scratch_shapes=[pltpu.VMEM((slots, block, block), jnp.bfloat16), pltpu.SemaphoreType.DMA((2,))] + extra,
        compiler_params=pltpu.CompilerParams(vmem_limit_bytes=VMEM_LIMIT),
        cost_estimate=pl.CostEstimate(
            flops=2 * slots * rhs_cols * block * block,
            bytes_accessed=slots * block * (block + 2 * rhs_cols) * 4,
            transcendentals=0,
        ),
        name=name,
    )(*codes, *sources, own, other)


def first_sum(code, sources, own, other):
    one = sources[0].shape[3:]
    parts = sum(v.shape[0] for v in sources)
    known = parts * sources[0].shape[2]
    store = jax.ShapeDtypeStruct((2048,) + one, jnp.bfloat16)
    extra = [
        pltpu.SemaphoreType.DMA((parts,)),
        pltpu.VMEM((known,) + one, jnp.bfloat16),
        pltpu.SemaphoreType.DMA,
    ]
    spaces = [pl.ANY] * len(sources)
    return sum_call(first_kernel, [code], sources, spaces, own, other, [store], [pltpu.HBM], extra, "first_sum", jnp.bfloat16)


def old_sum(level, known, code, fresh, store, solved, own, other):
    one = store.shape[1:]
    outs = [
        jax.ShapeDtypeStruct((code.shape[1] + 1,), jnp.int32),
        jax.ShapeDtypeStruct((NEAR, one[1], one[1]), jnp.bfloat16),
    ]
    kernel = functools.partial(old_kernel, level, known)
    extra = [pltpu.VMEM((code.shape[1],) + one, jnp.bfloat16), pltpu.SemaphoreType.DMA]
    if solved:
        extra.append(pltpu.VMEM((sum(v.shape[0] for v in solved),) + one, jnp.bfloat16))
    spaces = [pl.ANY] + [pltpu.VMEM] * len(solved)
    out_spaces = [pltpu.SMEM, pltpu.VMEM]
    return sum_call(kernel, [code, fresh], [store] + solved, spaces, own, other, outs, out_spaces, extra, "old_sum", jnp.float32)


def fresh_kernel(level, list_ref, old_ref, x_ref, near_ref, own_ref, other_ref, out_ref, total, far, sem):
    per_row = own_ref.shape[2]
    total[...] = old_ref[...]
    count = list_ref[0]

    def add(block, entry):
        row = ((entry & 1023) >= per_row).astype(jnp.int32)
        total[row] += nt_dot(x_ref[entry >> 10], block)

    def add_near(n, carry):
        add(near_ref[n], list_ref[1 + n])
        return carry

    def add_far(n, carry):
        slot = list_ref[1 + n] & 1023

        @pl.when(slot < per_row)
        def _():
            pltpu.make_async_copy(own_ref.at[level - 1, 0, slot], far, sem).start()

        @pl.when(slot >= per_row)
        def _():
            pltpu.make_async_copy(other_ref.at[level - 1, 0, slot - per_row], far, sem).start()

        pltpu.make_async_copy(own_ref.at[level - 1, 0, 0], far, sem).wait()
        add(far[...], list_ref[1 + n])
        return carry

    lax.fori_loop(0, jnp.minimum(count, NEAR), add_near, 0)
    lax.fori_loop(NEAR, count, add_far, 0)
    out_ref[...] = total[...].astype(out_ref.dtype)


def fresh_sum(level, listed, solved, old, near, own, other):
    block = solved.shape[-1]
    vmem = pl.BlockSpec(memory_space=pltpu.VMEM)
    return pl.pallas_call(
        functools.partial(fresh_kernel, level),
        out_shape=jax.ShapeDtypeStruct(old.shape, jnp.bfloat16),
        in_specs=[pl.BlockSpec(memory_space=pltpu.SMEM)] + [vmem] * 3 + [pl.BlockSpec(memory_space=pltpu.HBM)] * 2,
        out_specs=vmem,
        scratch_shapes=[
            pltpu.VMEM(old.shape, jnp.float32),
            pltpu.VMEM((block, block), jnp.bfloat16),
            pltpu.SemaphoreType.DMA,
        ],
        compiler_params=pltpu.CompilerParams(vmem_limit_bytes=VMEM_LIMIT),
        name="fresh_sum",
    )(listed, old, solved, near, own, other)


def solve_kernel(level, p0, p1, p2, p3, rhs_ref, own_d_ref, other_d_ref, out_ref, *refs):
    core = lax.axis_index("core")
    for r, d_ref in enumerate((own_d_ref, other_d_ref)):
        q0, q1, q2, q3 = (p[r].astype(jnp.float32) for p in (p0, p1, p2, p3))
        coupled = (q0 + q1) + (q2 + q3)
        reduced = (rhs_ref[level, r].astype(jnp.float32) - coupled).astype(jnp.bfloat16)
        solved = nt_dot(reduced, d_ref[level, 0]).astype(jnp.bfloat16)
        out_ref[r] = solved
        if refs:
            refs[1][core ^ r] = solved
    if refs:
        all_ref, both, sems = refs
        sends = [pltpu.make_async_copy(both, all_ref.at[i], sems.at[i]) for i in range(all_ref.shape[0])]
        for send in sends:
            send.start()
        for send in sends:
            send.wait()


def solve_level(level, partials, rhs, own_d, other_d, copies):
    _, rhs_cols, block = partials[0].shape
    vmem = pl.BlockSpec(memory_space=pltpu.VMEM)
    out_shape, out_specs, scratch = [jax.ShapeDtypeStruct((2, rhs_cols, block), jnp.bfloat16)], [vmem], []
    if copies:
        out_shape.append(jax.ShapeDtypeStruct((copies, 2, rhs_cols, block), jnp.bfloat16))
        out_specs.append(pl.BlockSpec(memory_space=pltpu.HBM))
        scratch = [pltpu.VMEM((2, rhs_cols, block), jnp.bfloat16), pltpu.SemaphoreType.DMA((copies,))]
    return pl.pallas_call(
        functools.partial(solve_kernel, level),
        out_shape=out_shape,
        in_specs=[vmem] * 7,
        out_specs=out_specs,
        scratch_shapes=scratch,
        compiler_params=pltpu.CompilerParams(vmem_limit_bytes=VMEM_LIMIT),
        name="solve_level",
    )(*partials, rhs, own_d, other_d)


def on_device(rhs, boundary, diag_inv, off_blocks, coupling, present):
    levels, _, rhs_cols, block = rhs.shape
    outer_each = boundary.shape[0]
    outer = outer_each * 32
    half = rhs_cols // 2
    z, y, core = lax.axis_index("z"), lax.axis_index("y"), lax.axis_index("core")

    def my_half(v, axis):
        return lax.dynamic_slice_in_dim(v, core * half, half, axis)

    def their_half(v, axis):
        return lax.dynamic_slice_in_dim(v, (1 - core) * half, half, axis)

    first = jnp.einsum("rb,ab->ra", rhs[0, 0], diag_inv[0, 0], preferred_element_type=jnp.float32).astype(jnp.bfloat16)
    known = jnp.concatenate([boundary, first[None]])
    known = jnp.stack([my_half(known, 1), their_half(known, 1)])
    code_own = (coupling + 1024 * present)[:, 0]
    code_both = jnp.stack([code_own, swap_cores(code_own)], axis=1)
    rhs_both = jnp.concatenate([my_half(rhs, 2), swap_cores(their_half(rhs, 2))], axis=1)
    diag_other = swap_cores(diag_inv)
    off_sent, known = lax.optimization_barrier((off_blocks, known))
    off_other = swap_cores(off_sent)

    pieces = gather_parts(known)
    pieces = pieces + [swap_cores(piece) for piece in pieces]

    keep, index = code_both >= 1024, code_both % 1024
    in_outer = index < outer
    row = jnp.where(in_outer, index // outer_each, index - outer)
    member = jnp.where(in_outer, index % outer_each, outer_each)
    src_z, src_y, src_core = row // 8, (row // 2) % 4, row % 2
    each = outer_each + 1
    away = jnp.where(src_core == 0, src_y - y, src_z - z) % 4
    part = jnp.where(away == 3, 1, jnp.where(away == 1, 2, jnp.where(away == 2, 3, 0))) * 4
    part = part + jnp.where(src_core == 0, src_z ^ z, src_y ^ y) + jnp.where(src_core == core, 0, 16)
    known_place = part * each + member
    level_of = jnp.maximum(index - outer, 0) // 32
    this = jnp.arange(levels - 1)[:, None, None]
    is_fresh = (level_of == this) & (level_of > 0)
    place_level = (index - outer) % 32
    old_code = jnp.where(level_of == 0, known_place, 32 * each + (level_of - 1) * 32 + place_level)
    old_code = jnp.where(keep & ~is_fresh, old_code, -1).reshape(levels - 1, -1)
    fresh_code = jnp.where(keep & is_fresh, place_level, -1).reshape(levels - 1, -1)

    own_rows, other_rows = [], []
    value, store = first_sum(old_code, pieces, off_blocks, off_other)
    solved_levels = []
    for level in range(1, levels):
        partials = [value] + [lax.ppermute(value, "x", xor_pairs(4, k)) for k in (1, 2, 3)]
        last = level == levels - 1
        outs = solve_level(level, partials, rhs_both, diag_inv, diag_other, 0 if last else 16)
        own_rows.append(outs[0][0])
        other_rows.append(outs[0][1])
        if not last:
            next_fresh, sent = lax.optimization_barrier((fresh_code, outs[1]))
            solved = lax.all_to_all(sent, ("z", "y"), 0, 0).reshape(32, half, block)
            old, listed, near = old_sum(
                level + 1, 32 * each, old_code, next_fresh, store, solved_levels, off_blocks, off_other
            )
            value = fresh_sum(level + 1, listed, solved, old, near, off_blocks, off_other)
            solved_levels = solved_levels + [solved]

    mine = jnp.stack(own_rows)
    theirs = swap_cores(jnp.stack(other_rows))
    low = jnp.where(core == 0, mine, theirs)
    high = jnp.where(core == 0, theirs, mine)
    rest = jnp.concatenate([low, high], axis=1)
    return jnp.concatenate([first[None], rest])[:, None]


def solution(mesh):
    split = Mesh(mesh.devices.reshape(4, 4, 2, 4), ("z", "y", "core", "x"))
    in_specs = (
        P(None, ROWS, None, None),
        P(ROWS, None, None),
        P(None, ROWS, None, None),
        P(None, ROWS, "x", None, None),
        P(None, ROWS, "x"),
        P(None, ROWS, "x"),
    )
    return jax.shard_map(
        on_device, mesh=split, in_specs=in_specs, out_specs=P(None, ROWS, None, None), check_vma=False
    )
```

```python
import functools

import jax
import jax.numpy as jnp
from jax import lax
from jax.experimental import pallas as pl
from jax.experimental.pallas import tpu as pltpu
from jax.sharding import Mesh, PartitionSpec as P

ROWS = ("z", "y", "core")
VMEM_LIMIT = 48 * 1024 * 1024


def xor_pairs(n, k):
    return [(i, i ^ k) for i in range(n)]


def shift_pairs(n, k):
    return [(i, (i + k) % n) for i in range(n)]


def swap_cores(v):
    return lax.ppermute(v, "core", xor_pairs(2, 1))


def pairs(stage, move):
    result = []
    for z in range(4):
        for y in range(4):
            for core in range(2):
                to_z, to_y = (move(z), y) if core + 1 == stage else (z, move(y))
                result.append(((z * 4 + y) * 2 + core, (to_z * 4 + to_y) * 2 + core))
    return result


def gather_parts(v):
    near = [lax.ppermute(v, ROWS, pairs(1, lambda i, k=k: i ^ k)) for k in (1, 2, 3)]
    low, high = jnp.stack([v, near[0]]), jnp.stack(near[1:])
    up, down = pairs(2, lambda i: (i + 1) % 4), pairs(2, lambda i: (i + 3) % 4)
    before_low, after_high = lax.ppermute(low, ROWS, up), lax.ppermute(high, ROWS, down)
    before_high, after_low = lax.ppermute(high, ROWS, up), lax.ppermute(low, ROWS, down)
    far = [lax.ppermute(before_low, ROWS, up), lax.ppermute(after_high, ROWS, down)]
    return [low, high, before_low, before_high, after_low, after_high] + far


def nt_dot(x, a):
    return lax.dot_general(x, a, (((1,), (1,)), ((), ())), preferred_element_type=jnp.float32)


GROUP = 8
NEAR = 16


def gather_sum(level, code_ref, picks, known, solved_ref, own_ref, other_ref, out_ref, blocks, block_sems, between):
    slots = code_ref.shape[1]
    per_row = slots // 2
    loads = [
        pltpu.make_async_copy(a_ref.at[level - 1, 0], blocks.at[pl.ds(r * per_row, per_row)], block_sems.at[r])
        for r, a_ref in enumerate((own_ref, other_ref))
    ]
    for load in loads:
        load.start()
    between()
    for r in range(2):
        loads[r].wait()
        total = None
        for g in range(r * per_row, (r + 1) * per_row, GROUP):
            xs, group = [], []
            for k in range(g, g + GROUP):
                code = code_ref[level - 1, k]
                kept = (code >= 0).astype(jnp.float32)
                picked = picks(k, jnp.clip(code, 0, known - 1))
                if solved_ref is not None:
                    picked = jnp.where(code >= known, solved_ref[jnp.maximum(code - known, 0)], picked)
                xs.append((picked.astype(jnp.float32) * kept).astype(jnp.bfloat16))
                group.append(blocks[k])
            part = nt_dot(jnp.concatenate(xs, axis=1), jnp.concatenate(group, axis=1))
            total = part if total is None else total + part
        out_ref[r] = total


def first_kernel(code_ref, *refs):
    sources, refs = refs[:-9], refs[-9:]
    own_ref, other_ref, out_ref, store_ref, blocks, block_sems, pack_sems, packed, store_sem = refs
    packs, start = [], 0
    for i, source in enumerate(sources):
        which = 0 if i < len(sources) // 2 else 1
        for part in range(source.shape[0]):
            target = packed.at[pl.ds(start, source.shape[2])]
            packs.append(pltpu.make_async_copy(source.at[part, which], target, pack_sems.at[len(packs)]))
            start += source.shape[2]
    keep = pltpu.make_async_copy(packed, store_ref.at[pl.ds(0, start)], store_sem)

    def between():
        for pack in packs:
            pack.start()
        for pack in packs:
            pack.wait()
        keep.start()

    picks = lambda k, code: packed[code]
    gather_sum(1, code_ref, picks, start, None, own_ref, other_ref, out_ref, blocks, block_sems, between)
    keep.wait()


def old_kernel(level, known, code_ref, fresh_ref, store_ref, *refs):
    solved, refs = refs[: level - 2], refs[level - 2 :]
    own_ref, other_ref, out_ref, list_ref, near_ref, blocks, block_sems, picked, pick_sem = refs[:9]
    solved_ref = refs[9] if solved else None
    slots = code_ref.shape[1]

    def between():
        for k in range(slots):
            place = jnp.clip(code_ref[level - 1, k], 0, known - 1)
            pltpu.make_async_copy(store_ref.at[place], picked.at[k], pick_sem).start()
        for i, one in enumerate(solved):
            solved_ref[i * one.shape[0] : (i + 1) * one.shape[0]] = one[...]
        pltpu.make_async_copy(store_ref.at[pl.ds(0, slots)], picked, pick_sem).wait()

    picks = lambda k, code: picked[k]
    gather_sum(level, code_ref, picks, known, solved_ref, own_ref, other_ref, out_ref, blocks, block_sems, between)

    def note(slot, count):
        code = fresh_ref[level - 1, slot]

        @pl.when(code >= 0)
        def _():
            list_ref[1 + count] = code * 1024 + slot

        @pl.when((code >= 0) & (count < NEAR))
        def _():
            near_ref[count] = blocks[slot]

        return count + (code >= 0).astype(jnp.int32)

    list_ref[0] = lax.fori_loop(0, fresh_ref.shape[1], note, jnp.int32(0))


def sum_call(kernel, codes, sources, source_spaces, own, other, outs, out_spaces, extra, name, limit):
    slots, (rhs_cols, block) = codes[0].shape[1], sources[0].shape[-2:]
    return pl.pallas_call(
        kernel,
        out_shape=[jax.ShapeDtypeStruct((2, rhs_cols, block), jnp.float32)] + outs,
        in_specs=[pl.BlockSpec(memory_space=pltpu.SMEM)] * len(codes)
        + [pl.BlockSpec(memory_space=space) for space in source_spaces]
        + [pl.BlockSpec(memory_space=pltpu.HBM)] * 2,
        out_specs=[pl.BlockSpec(memory_space=space) for space in [pltpu.VMEM] + out_spaces],
        scratch_shapes=[pltpu.VMEM((slots, block, block), jnp.bfloat16), pltpu.SemaphoreType.DMA((2,))] + extra,
        compiler_params=pltpu.CompilerParams(vmem_limit_bytes=limit),
        cost_estimate=pl.CostEstimate(
            flops=2 * slots * rhs_cols * block * block,
            bytes_accessed=slots * block * (block + 2 * rhs_cols) * 4,
            transcendentals=0,
        ),
        name=name,
    )(*codes, *sources, own, other)


def first_sum(code, sources, own, other):
    one = sources[0].shape[3:]
    parts = sum(v.shape[0] for v in sources)
    known = parts * sources[0].shape[2]
    store = jax.ShapeDtypeStruct((2048,) + one, jnp.bfloat16)
    extra = [
        pltpu.SemaphoreType.DMA((parts,)),
        pltpu.VMEM((known,) + one, jnp.bfloat16),
        pltpu.SemaphoreType.DMA,
    ]
    spaces = [pl.ANY] * len(sources)
    return sum_call(first_kernel, [code], sources, spaces, own, other, [store], [pltpu.HBM], extra, "first_sum", 12 * 1024 * 1024)


def old_sum(level, known, code, fresh, store, solved, own, other):
    one = store.shape[1:]
    outs = [
        jax.ShapeDtypeStruct((code.shape[1] + 1,), jnp.int32),
        jax.ShapeDtypeStruct((NEAR, one[1], one[1]), jnp.bfloat16),
    ]
    kernel = functools.partial(old_kernel, level, known)
    extra = [pltpu.VMEM((code.shape[1],) + one, jnp.bfloat16), pltpu.SemaphoreType.DMA]
    if solved:
        extra.append(pltpu.VMEM((sum(v.shape[0] for v in solved),) + one, jnp.bfloat16))
    spaces = [pl.ANY] + [pltpu.VMEM] * len(solved)
    out_spaces = [pltpu.SMEM, pltpu.VMEM]
    return sum_call(kernel, [code, fresh], [store] + solved, spaces, own, other, outs, out_spaces, extra, "old_sum", VMEM_LIMIT)


def fresh_kernel(level, list_ref, old_ref, x_ref, near_ref, own_ref, other_ref, out_ref, far, sem):
    per_row = own_ref.shape[2]
    out_ref[...] = old_ref[...]
    count = list_ref[0]

    def add(block, entry):
        row = ((entry & 1023) >= per_row).astype(jnp.int32)
        out_ref[row] += nt_dot(x_ref[entry >> 10], block)

    def add_near(n, carry):
        add(near_ref[n], list_ref[1 + n])
        return carry

    def add_far(n, carry):
        slot = list_ref[1 + n] & 1023

        @pl.when(slot < per_row)
        def _():
            pltpu.make_async_copy(own_ref.at[level - 1, 0, slot], far, sem).start()

        @pl.when(slot >= per_row)
        def _():
            pltpu.make_async_copy(other_ref.at[level - 1, 0, slot - per_row], far, sem).start()

        pltpu.make_async_copy(own_ref.at[level - 1, 0, 0], far, sem).wait()
        add(far[...], list_ref[1 + n])
        return carry

    lax.fori_loop(0, jnp.minimum(count, NEAR), add_near, 0)
    lax.fori_loop(NEAR, count, add_far, 0)


def fresh_sum(level, listed, solved, old, near, own, other):
    block = solved.shape[-1]
    vmem = pl.BlockSpec(memory_space=pltpu.VMEM)
    return pl.pallas_call(
        functools.partial(fresh_kernel, level),
        out_shape=jax.ShapeDtypeStruct(old.shape, jnp.float32),
        in_specs=[pl.BlockSpec(memory_space=pltpu.SMEM)] + [vmem] * 3 + [pl.BlockSpec(memory_space=pltpu.HBM)] * 2,
        out_specs=vmem,
        scratch_shapes=[
            pltpu.VMEM((block, block), jnp.bfloat16),
            pltpu.SemaphoreType.DMA,
        ],
        compiler_params=pltpu.CompilerParams(vmem_limit_bytes=VMEM_LIMIT),
        name="fresh_sum",
    )(listed, old, solved, near, own, other)


def solve_kernel(level, p0, p1, p2, p3, rhs_ref, own_d_ref, other_d_ref, out_ref, *refs):
    core = lax.axis_index("core")
    for r, d_ref in enumerate((own_d_ref, other_d_ref)):
        coupled = (p0[r] + p1[r]) + (p2[r] + p3[r])
        reduced = (rhs_ref[level, r].astype(jnp.float32) - coupled).astype(jnp.bfloat16)
        solved = nt_dot(reduced, d_ref[level, 0]).astype(jnp.bfloat16)
        out_ref[r] = solved
        if refs:
            refs[1][core ^ r] = solved
    if refs:
        all_ref, both, sems = refs
        sends = [pltpu.make_async_copy(both, all_ref.at[i], sems.at[i]) for i in range(all_ref.shape[0])]
        for send in sends:
            send.start()
        for send in sends:
            send.wait()


def solve_level(level, partials, rhs, own_d, other_d, copies):
    _, rhs_cols, block = partials[0].shape
    vmem = pl.BlockSpec(memory_space=pltpu.VMEM)
    out_shape, out_specs, scratch = [jax.ShapeDtypeStruct((2, rhs_cols, block), jnp.bfloat16)], [vmem], []
    if copies:
        out_shape.append(jax.ShapeDtypeStruct((copies, 2, rhs_cols, block), jnp.bfloat16))
        out_specs.append(pl.BlockSpec(memory_space=pltpu.HBM))
        scratch = [pltpu.VMEM((2, rhs_cols, block), jnp.bfloat16), pltpu.SemaphoreType.DMA((copies,))]
    return pl.pallas_call(
        functools.partial(solve_kernel, level),
        out_shape=out_shape,
        in_specs=[vmem] * 7,
        out_specs=out_specs,
        scratch_shapes=scratch,
        compiler_params=pltpu.CompilerParams(vmem_limit_bytes=VMEM_LIMIT),
        name="solve_level",
    )(*partials, rhs, own_d, other_d)


def on_device(rhs, boundary, diag_inv, off_blocks, coupling, present):
    levels, _, rhs_cols, block = rhs.shape
    outer_each = boundary.shape[0]
    outer = outer_each * 32
    half = rhs_cols // 2
    z, y, core = lax.axis_index("z"), lax.axis_index("y"), lax.axis_index("core")

    def my_half(v, axis):
        return lax.dynamic_slice_in_dim(v, core * half, half, axis)

    def their_half(v, axis):
        return lax.dynamic_slice_in_dim(v, (1 - core) * half, half, axis)

    first = jnp.einsum("rb,ab->ra", rhs[0, 0], diag_inv[0, 0], preferred_element_type=jnp.float32).astype(jnp.bfloat16)
    known = jnp.concatenate([boundary, first[None]])
    known = jnp.stack([my_half(known, 1), their_half(known, 1)])
    code_own = (coupling + 1024 * present)[:, 0]
    code_both = jnp.stack([code_own, swap_cores(code_own)], axis=1)
    rhs_both = jnp.concatenate([my_half(rhs, 2), swap_cores(their_half(rhs, 2))], axis=1)
    diag_other = swap_cores(diag_inv)
    off_sent, known = lax.optimization_barrier((off_blocks, known))
    off_other = swap_cores(off_sent)
    off_first = off_sent[:1]
    off_first_other = swap_cores(off_first)

    pieces = gather_parts(known)
    pieces = pieces + [swap_cores(piece) for piece in pieces]

    keep, index = code_both >= 1024, code_both % 1024
    in_outer = index < outer
    row = jnp.where(in_outer, index // outer_each, index - outer)
    member = jnp.where(in_outer, index % outer_each, outer_each)
    src_z, src_y, src_core = row // 8, (row // 2) % 4, row % 2
    each = outer_each + 1
    away = jnp.where(src_core == 0, src_y - y, src_z - z) % 4
    part = jnp.where(away == 3, 1, jnp.where(away == 1, 2, jnp.where(away == 2, 3, 0))) * 4
    part = part + jnp.where(src_core == 0, src_z ^ z, src_y ^ y) + jnp.where(src_core == core, 0, 16)
    known_place = part * each + member
    level_of = jnp.maximum(index - outer, 0) // 32
    this = jnp.arange(levels - 1)[:, None, None]
    is_fresh = (level_of == this) & (level_of > 0)
    place_level = (index - outer) % 32
    old_code = jnp.where(level_of == 0, known_place, 32 * each + (level_of - 1) * 32 + place_level)
    old_code = jnp.where(keep & ~is_fresh, old_code, -1).reshape(levels - 1, -1)
    fresh_code = jnp.where(keep & is_fresh, place_level, -1).reshape(levels - 1, -1)

    own_rows, other_rows = [], []
    value, store = first_sum(old_code, pieces, off_first, off_first_other)
    solved_levels = []
    for level in range(1, levels):
        partials = [value] + [lax.ppermute(value, "x", xor_pairs(4, k)) for k in (1, 2, 3)]
        last = level == levels - 1
        outs = solve_level(level, partials, rhs_both, diag_inv, diag_other, 0 if last else 16)
        own_rows.append(outs[0][0])
        other_rows.append(outs[0][1])
        if not last:
            next_fresh, sent = lax.optimization_barrier((fresh_code, outs[1]))
            solved = lax.all_to_all(sent, ("z", "y"), 0, 0).reshape(32, half, block)
            old, listed, near = old_sum(
                level + 1, 32 * each, old_code, next_fresh, store, solved_levels, off_blocks, off_other
            )
            value = fresh_sum(level + 1, listed, solved, old, near, off_blocks, off_other)
            solved_levels = solved_levels + [solved]

    mine = jnp.stack(own_rows)
    theirs = swap_cores(jnp.stack(other_rows))
    low = jnp.where(core == 0, mine, theirs)
    high = jnp.where(core == 0, theirs, mine)
    rest = jnp.concatenate([low, high], axis=1)
    return jnp.concatenate([first[None], rest])[:, None]


def solution(mesh):
    split = Mesh(mesh.devices.reshape(4, 4, 2, 4), ("z", "y", "core", "x"))
    in_specs = (
        P(None, ROWS, None, None),
        P(ROWS, None, None),
        P(None, ROWS, None, None),
        P(None, ROWS, "x", None, None),
        P(None, ROWS, "x"),
        P(None, ROWS, "x"),
    )
    return jax.shard_map(
        on_device, mesh=split, in_specs=in_specs, out_specs=P(None, ROWS, None, None), check_vma=False
    )
```

```python
import functools

import jax
import jax.numpy as jnp
from jax import lax
from jax.experimental import pallas as pl
from jax.experimental.pallas import tpu as pltpu
from jax.sharding import Mesh, PartitionSpec as P

ROWS = ("z", "y", "core")
VMEM_LIMIT = 48 * 1024 * 1024


def xor_pairs(n, k):
    return [(i, i ^ k) for i in range(n)]


def shift_pairs(n, k):
    return [(i, (i + k) % n) for i in range(n)]


def swap_cores(v):
    return lax.ppermute(v, "core", xor_pairs(2, 1))


def pairs(stage, move):
    result = []
    for z in range(4):
        for y in range(4):
            for core in range(2):
                to_z, to_y = (move(z), y) if core + 1 == stage else (z, move(y))
                result.append(((z * 4 + y) * 2 + core, (to_z * 4 + to_y) * 2 + core))
    return result


def gather_parts(v):
    near = [lax.ppermute(v, ROWS, pairs(1, lambda i, k=k: i ^ k)) for k in (1, 2, 3)]
    low, high = jnp.stack([v, near[0]]), jnp.stack(near[1:])
    up, down = pairs(2, lambda i: (i + 1) % 4), pairs(2, lambda i: (i + 3) % 4)
    before_low, after_high = lax.ppermute(low, ROWS, up), lax.ppermute(high, ROWS, down)
    before_high, after_low = lax.ppermute(high, ROWS, up), lax.ppermute(low, ROWS, down)
    far = [lax.ppermute(before_low, ROWS, up), lax.ppermute(after_high, ROWS, down)]
    return [low, high, before_low, before_high, after_low, after_high] + far


def nt_dot(x, a):
    return lax.dot_general(x, a, (((1,), (1,)), ((), ())), preferred_element_type=jnp.float32)


GROUP = 8
NEAR = 16


def gather_sum(level, code_ref, picks, known, solved_ref, own_ref, other_ref, out_ref, blocks, block_sems, between):
    slots = code_ref.shape[1]
    per_row = slots // 2
    loads = [
        pltpu.make_async_copy(a_ref.at[level - 1, 0], blocks.at[pl.ds(r * per_row, per_row)], block_sems.at[r])
        for r, a_ref in enumerate((own_ref, other_ref))
    ]
    for load in loads:
        load.start()
    between()
    for r in range(2):
        loads[r].wait()
        total = None
        for g in range(r * per_row, (r + 1) * per_row, GROUP):
            xs, group = [], []
            for k in range(g, g + GROUP):
                code = code_ref[level - 1, k]
                kept = (code >= 0).astype(jnp.float32)
                picked = picks(k, jnp.clip(code, 0, known - 1))
                if solved_ref is not None:
                    picked = jnp.where(code >= known, solved_ref[jnp.maximum(code - known, 0)], picked)
                xs.append((picked.astype(jnp.float32) * kept).astype(jnp.bfloat16))
                group.append(blocks[k])
            part = nt_dot(jnp.concatenate(xs, axis=1), jnp.concatenate(group, axis=1))
            total = part if total is None else total + part
        out_ref[r] = total


def first_kernel(code_ref, *refs):
    sources, refs = refs[:-9], refs[-9:]
    own_ref, other_ref, out_ref, store_ref, blocks, block_sems, pack_sems, packed, store_sem = refs
    packs, start = [], 0
    for i, source in enumerate(sources):
        which = 0 if i < len(sources) // 2 else 1
        for part in range(source.shape[0]):
            target = packed.at[pl.ds(start, source.shape[2])]
            packs.append(pltpu.make_async_copy(source.at[part, which], target, pack_sems.at[len(packs)]))
            start += source.shape[2]
    keep = pltpu.make_async_copy(packed, store_ref.at[pl.ds(0, start)], store_sem)

    def between():
        for pack in packs:
            pack.start()
        for pack in packs:
            pack.wait()
        keep.start()

    picks = lambda k, code: packed[code]
    gather_sum(1, code_ref, picks, start, None, own_ref, other_ref, out_ref, blocks, block_sems, between)
    keep.wait()


def old_kernel(level, known, code_ref, fresh_ref, store_ref, *refs):
    solved, refs = refs[: level - 2], refs[level - 2 :]
    own_ref, other_ref, out_ref, list_ref, near_ref, blocks, block_sems, picked, pick_sem = refs[:9]
    solved_ref = refs[9] if solved else None
    slots = code_ref.shape[1]

    def between():
        for k in range(slots):
            place = jnp.clip(code_ref[level - 1, k], 0, known - 1)
            pltpu.make_async_copy(store_ref.at[place], picked.at[k], pick_sem).start()
        for i, one in enumerate(solved):
            solved_ref[i * one.shape[0] : (i + 1) * one.shape[0]] = one[...]
        pltpu.make_async_copy(store_ref.at[pl.ds(0, slots)], picked, pick_sem).wait()

    picks = lambda k, code: picked[k]
    gather_sum(level, code_ref, picks, known, solved_ref, own_ref, other_ref, out_ref, blocks, block_sems, between)

    def note(slot, count):
        code = fresh_ref[level - 1, slot]

        @pl.when(code >= 0)
        def _():
            list_ref[1 + count] = code * 1024 + slot

        @pl.when((code >= 0) & (count < NEAR))
        def _():
            near_ref[count] = blocks[slot]

        return count + (code >= 0).astype(jnp.int32)

    list_ref[0] = lax.fori_loop(0, fresh_ref.shape[1], note, jnp.int32(0))


def sum_call(kernel, codes, sources, source_spaces, own, other, outs, out_spaces, extra, name, limit):
    slots, (rhs_cols, block) = codes[0].shape[1], sources[0].shape[-2:]
    return pl.pallas_call(
        kernel,
        out_shape=[jax.ShapeDtypeStruct((2, rhs_cols, block), jnp.float32)] + outs,
        in_specs=[pl.BlockSpec(memory_space=pltpu.SMEM)] * len(codes)
        + [pl.BlockSpec(memory_space=space) for space in source_spaces]
        + [pl.BlockSpec(memory_space=pltpu.HBM)] * 2,
        out_specs=[pl.BlockSpec(memory_space=space) for space in [pltpu.VMEM] + out_spaces],
        scratch_shapes=[pltpu.VMEM((slots, block, block), jnp.bfloat16), pltpu.SemaphoreType.DMA((2,))] + extra,
        compiler_params=pltpu.CompilerParams(vmem_limit_bytes=limit),
        cost_estimate=pl.CostEstimate(
            flops=2 * slots * rhs_cols * block * block,
            bytes_accessed=slots * block * (block + 2 * rhs_cols) * 4,
            transcendentals=0,
        ),
        name=name,
    )(*codes, *sources, own, other)


def first_sum(code, sources, own, other):
    one = sources[0].shape[3:]
    parts = sum(v.shape[0] for v in sources)
    known = parts * sources[0].shape[2]
    store = jax.ShapeDtypeStruct((2048,) + one, jnp.bfloat16)
    extra = [
        pltpu.SemaphoreType.DMA((parts,)),
        pltpu.VMEM((known,) + one, jnp.bfloat16),
        pltpu.SemaphoreType.DMA,
    ]
    spaces = [pl.ANY] * len(sources)
    return sum_call(first_kernel, [code], sources, spaces, own, other, [store], [pltpu.HBM], extra, "first_sum", 61 * 1024 * 1024)


def old_sum(level, known, code, fresh, store, solved, own, other):
    one = store.shape[1:]
    outs = [
        jax.ShapeDtypeStruct((code.shape[1] + 1,), jnp.int32),
        jax.ShapeDtypeStruct((NEAR, one[1], one[1]), jnp.bfloat16),
    ]
    kernel = functools.partial(old_kernel, level, known)
    extra = [pltpu.VMEM((code.shape[1],) + one, jnp.bfloat16), pltpu.SemaphoreType.DMA]
    if solved:
        extra.append(pltpu.VMEM((sum(v.shape[0] for v in solved),) + one, jnp.bfloat16))
    spaces = [pl.ANY] + [pltpu.VMEM] * len(solved)
    out_spaces = [pltpu.SMEM, pltpu.VMEM]
    return sum_call(kernel, [code, fresh], [store] + solved, spaces, own, other, outs, out_spaces, extra, "old_sum", VMEM_LIMIT)


def fresh_kernel(level, list_ref, old_ref, x_ref, near_ref, own_ref, other_ref, out_ref, far, sem):
    per_row = own_ref.shape[2]
    out_ref[...] = old_ref[...]
    count = list_ref[0]

    def add(block, entry):
        row = ((entry & 1023) >= per_row).astype(jnp.int32)
        out_ref[row] += nt_dot(x_ref[entry >> 10], block)

    def add_near(n, carry):
        add(near_ref[n], list_ref[1 + n])
        return carry

    def add_far(n, carry):
        slot = list_ref[1 + n] & 1023

        @pl.when(slot < per_row)
        def _():
            pltpu.make_async_copy(own_ref.at[level - 1, 0, slot], far, sem).start()

        @pl.when(slot >= per_row)
        def _():
            pltpu.make_async_copy(other_ref.at[level - 1, 0, slot - per_row], far, sem).start()

        pltpu.make_async_copy(own_ref.at[level - 1, 0, 0], far, sem).wait()
        add(far[...], list_ref[1 + n])
        return carry

    lax.fori_loop(0, jnp.minimum(count, NEAR), add_near, 0)
    lax.fori_loop(NEAR, count, add_far, 0)


def fresh_sum(level, listed, solved, old, near, own, other):
    block = solved.shape[-1]
    vmem = pl.BlockSpec(memory_space=pltpu.VMEM)
    return pl.pallas_call(
        functools.partial(fresh_kernel, level),
        out_shape=jax.ShapeDtypeStruct(old.shape, jnp.float32),
        in_specs=[pl.BlockSpec(memory_space=pltpu.SMEM)] + [vmem] * 3 + [pl.BlockSpec(memory_space=pltpu.HBM)] * 2,
        out_specs=vmem,
        scratch_shapes=[
            pltpu.VMEM((block, block), jnp.bfloat16),
            pltpu.SemaphoreType.DMA,
        ],
        compiler_params=pltpu.CompilerParams(vmem_limit_bytes=VMEM_LIMIT),
        name="fresh_sum",
    )(listed, old, solved, near, own, other)


def solve_kernel(level, p0, p1, p2, p3, rhs_ref, own_d_ref, other_d_ref, out_ref, *refs):
    core = lax.axis_index("core")
    for r, d_ref in enumerate((own_d_ref, other_d_ref)):
        coupled = (p0[r] + p1[r]) + (p2[r] + p3[r])
        reduced = (rhs_ref[level, r].astype(jnp.float32) - coupled).astype(jnp.bfloat16)
        solved = nt_dot(reduced, d_ref[level, 0]).astype(jnp.bfloat16)
        out_ref[r] = solved
        if refs:
            refs[1][core ^ r] = solved
    if refs:
        all_ref, both, sems = refs
        sends = [pltpu.make_async_copy(both, all_ref.at[i], sems.at[i]) for i in range(all_ref.shape[0])]
        for send in sends:
            send.start()
        for send in sends:
            send.wait()


def solve_level(level, partials, rhs, own_d, other_d, copies):
    _, rhs_cols, block = partials[0].shape
    vmem = pl.BlockSpec(memory_space=pltpu.VMEM)
    out_shape, out_specs, scratch = [jax.ShapeDtypeStruct((2, rhs_cols, block), jnp.bfloat16)], [vmem], []
    if copies:
        out_shape.append(jax.ShapeDtypeStruct((copies, 2, rhs_cols, block), jnp.bfloat16))
        out_specs.append(pl.BlockSpec(memory_space=pltpu.HBM))
        scratch = [pltpu.VMEM((2, rhs_cols, block), jnp.bfloat16), pltpu.SemaphoreType.DMA((copies,))]
    return pl.pallas_call(
        functools.partial(solve_kernel, level),
        out_shape=out_shape,
        in_specs=[vmem] * 7,
        out_specs=out_specs,
        scratch_shapes=scratch,
        compiler_params=pltpu.CompilerParams(vmem_limit_bytes=VMEM_LIMIT),
        name="solve_level",
    )(*partials, rhs, own_d, other_d)


def on_device(rhs, boundary, diag_inv, off_blocks, coupling, present):
    levels, _, rhs_cols, block = rhs.shape
    outer_each = boundary.shape[0]
    outer = outer_each * 32
    half = rhs_cols // 2
    z, y, core = lax.axis_index("z"), lax.axis_index("y"), lax.axis_index("core")

    def my_half(v, axis):
        return lax.dynamic_slice_in_dim(v, core * half, half, axis)

    def their_half(v, axis):
        return lax.dynamic_slice_in_dim(v, (1 - core) * half, half, axis)

    first = jnp.einsum("rb,ab->ra", rhs[0, 0], diag_inv[0, 0], preferred_element_type=jnp.float32).astype(jnp.bfloat16)
    known = jnp.concatenate([boundary, first[None]])
    known = jnp.stack([my_half(known, 1), their_half(known, 1)])
    code_own = (coupling + 1024 * present)[:, 0]
    code_both = jnp.stack([code_own, swap_cores(code_own)], axis=1)
    rhs_both = jnp.concatenate([my_half(rhs, 2), swap_cores(their_half(rhs, 2))], axis=1)
    diag_other = swap_cores(diag_inv)
    off_sent, known = lax.optimization_barrier((off_blocks, known))
    off_other = swap_cores(off_sent)

    pieces = gather_parts(known)
    pieces = pieces + [swap_cores(piece) for piece in pieces]

    keep, index = code_both >= 1024, code_both % 1024
    in_outer = index < outer
    row = jnp.where(in_outer, index // outer_each, index - outer)
    member = jnp.where(in_outer, index % outer_each, outer_each)
    src_z, src_y, src_core = row // 8, (row // 2) % 4, row % 2
    each = outer_each + 1
    away = jnp.where(src_core == 0, src_y - y, src_z - z) % 4
    part = jnp.where(away == 3, 1, jnp.where(away == 1, 2, jnp.where(away == 2, 3, 0))) * 4
    part = part + jnp.where(src_core == 0, src_z ^ z, src_y ^ y) + jnp.where(src_core == core, 0, 16)
    known_place = part * each + member
    level_of = jnp.maximum(index - outer, 0) // 32
    this = jnp.arange(levels - 1)[:, None, None]
    is_fresh = (level_of == this) & (level_of > 0)
    place_level = (index - outer) % 32
    old_code = jnp.where(level_of == 0, known_place, 32 * each + (level_of - 1) * 32 + place_level)
    old_code = jnp.where(keep & ~is_fresh, old_code, -1).reshape(levels - 1, -1)
    fresh_code = jnp.where(keep & is_fresh, place_level, -1).reshape(levels - 1, -1)

    own_rows, other_rows = [], []
    value, store = first_sum(old_code, pieces, off_blocks, off_other)
    solved_levels = []
    for level in range(1, levels):
        partials = [value] + [lax.ppermute(value, "x", xor_pairs(4, k)) for k in (1, 2, 3)]
        last = level == levels - 1
        outs = solve_level(level, partials, rhs_both, diag_inv, diag_other, 0 if last else 16)
        own_rows.append(outs[0][0])
        other_rows.append(outs[0][1])
        if not last:
            next_fresh, sent = lax.optimization_barrier((fresh_code, outs[1]))
            solved = lax.all_to_all(sent, ("z", "y"), 0, 0).reshape(32, half, block)
            old, listed, near = old_sum(
                level + 1, 32 * each, old_code, next_fresh, store, solved_levels, off_blocks, off_other
            )
            value = fresh_sum(level + 1, listed, solved, old, near, off_blocks, off_other)
            solved_levels = solved_levels + [solved]

    mine = jnp.stack(own_rows)
    theirs = swap_cores(jnp.stack(other_rows))
    low = jnp.where(core == 0, mine, theirs)
    high = jnp.where(core == 0, theirs, mine)
    rest = jnp.concatenate([low, high], axis=1)
    return jnp.concatenate([first[None], rest])[:, None]


def solution(mesh):
    split = Mesh(mesh.devices.reshape(4, 4, 2, 4), ("z", "y", "core", "x"))
    in_specs = (
        P(None, ROWS, None, None),
        P(ROWS, None, None),
        P(None, ROWS, None, None),
        P(None, ROWS, "x", None, None),
        P(None, ROWS, "x"),
        P(None, ROWS, "x"),
    )
    return jax.shard_map(
        on_device, mesh=split, in_specs=in_specs, out_specs=P(None, ROWS, None, None), check_vma=False
    )
```

```python
import functools

import jax
import jax.numpy as jnp
from jax import lax
from jax.experimental import pallas as pl
from jax.experimental.pallas import tpu as pltpu
from jax.sharding import Mesh, PartitionSpec as P

ROWS = ("z", "y", "core")
VMEM_LIMIT = 48 * 1024 * 1024


def xor_pairs(n, k):
    return [(i, i ^ k) for i in range(n)]


def shift_pairs(n, k):
    return [(i, (i + k) % n) for i in range(n)]


def swap_cores(v):
    return lax.ppermute(v, "core", xor_pairs(2, 1))


def pairs(stage, move):
    result = []
    for z in range(4):
        for y in range(4):
            for core in range(2):
                to_z, to_y = (move(z), y) if core + 1 == stage else (z, move(y))
                result.append(((z * 4 + y) * 2 + core, (to_z * 4 + to_y) * 2 + core))
    return result


def gather_parts(v):
    near = [lax.ppermute(v, ROWS, pairs(1, lambda i, k=k: i ^ k)) for k in (1, 2, 3)]
    low, high = jnp.stack([v, near[0]]), jnp.stack(near[1:])
    up, down = pairs(2, lambda i: (i + 1) % 4), pairs(2, lambda i: (i + 3) % 4)
    before_low, after_high = lax.ppermute(low, ROWS, up), lax.ppermute(high, ROWS, down)
    low_now, high_now, sent_up, sent_down = lax.optimization_barrier((low, high, before_low, after_high))
    before_high, after_low = lax.ppermute(high_now, ROWS, up), lax.ppermute(low_now, ROWS, down)
    far = [lax.ppermute(sent_up, ROWS, up), lax.ppermute(sent_down, ROWS, down)]
    return [low, high, before_low, before_high, after_low, after_high] + far


def nt_dot(x, a):
    return lax.dot_general(x, a, (((1,), (1,)), ((), ())), preferred_element_type=jnp.float32)


GROUP = 8
SUM_LIMIT = 61 * 1024 * 1024
NEAR = 16


def pick(sources, first, code, target, sem):
    if len(sources) == 1:
        source, which = sources[0]
        pltpu.make_async_copy(source.at[(code >> 5) & 1, which, code & 31], target, sem).start()
        return
    middle = len(sources) // 2

    @pl.when((code >> 6) < first + middle)
    def _():
        pick(sources[:middle], first, code, target, sem)

    @pl.when((code >> 6) >= first + middle)
    def _():
        pick(sources[middle:], first + middle, code, target, sem)


def gather_sum(level, code_ref, pieces, solved_ref, base_ref, own_ref, other_ref, out_ref, scratch, between=None):
    blocks, block_sems, picked, pick_sem = scratch
    slots = code_ref.shape[1]
    per_row = slots // 2
    row = code_ref.shape[0] - 1 if code_ref.shape[0] < level else level - 1
    loads = [
        pltpu.make_async_copy(a_ref.at[level - 1, 0], blocks.at[pl.ds(r * per_row, per_row)], block_sems.at[r])
        for r, a_ref in enumerate((own_ref, other_ref))
    ]
    for load in loads:
        load.start()
    sources = [(piece, 0 if i < len(pieces) // 2 else 1) for i, piece in enumerate(pieces)]

    def fetch(k, carry):
        code = code_ref[row, k]
        pick(sources, 0, jnp.where((code < 0) | (code >= 1024), 0, code), picked.at[k], pick_sem)
        return carry

    lax.fori_loop(0, slots, fetch, 0)
    if between is not None:
        between()
    pltpu.make_async_copy(picked, picked, pick_sem).wait()
    for r in range(2):
        loads[r].wait()
        total = None if base_ref is None else base_ref[r]
        for g in range(r * per_row, (r + 1) * per_row, GROUP):
            xs, group = [], []
            for k in range(g, g + GROUP):
                code = code_ref[row, k]
                kept = (code >= 0).astype(jnp.float32)
                x = picked[k]
                if solved_ref is not None:
                    x = jnp.where(code >= 1024, solved_ref[jnp.maximum(code - 1024, 0)], x)
                xs.append((x.astype(jnp.float32) * kept).astype(jnp.bfloat16))
                group.append(blocks[k])
            part = nt_dot(jnp.concatenate(xs, axis=1), jnp.concatenate(group, axis=1))
            total = part if total is None else total + part
        out_ref[r] = total


def first_kernel(count, based, code_ref, *refs):
    pieces, refs = refs[:count], refs[count:]
    base_ref = refs[0] if based else None
    own_ref, other_ref, out_ref = refs[based : based + 3]
    gather_sum(1, code_ref, pieces, None, base_ref, own_ref, other_ref, out_ref, refs[based + 3 :])


def old_kernel(level, count, code_ref, fresh_ref, *refs):
    pieces, refs = refs[:count], refs[count:]
    solved, refs = refs[: level - 2], refs[level - 2 :]
    own_ref, other_ref, out_ref, list_ref, near_ref = refs[:5]
    scratch = refs[5:9]
    blocks = scratch[0]
    solved_ref = refs[9] if solved else None

    def between():
        for i, one in enumerate(solved):
            solved_ref[i * one.shape[0] : (i + 1) * one.shape[0]] = one[...]

    gather_sum(level, code_ref, pieces, solved_ref, None, own_ref, other_ref, out_ref, scratch, between)

    def note(slot, count):
        code = fresh_ref[level - 1, slot]

        @pl.when(code >= 0)
        def _():
            list_ref[1 + count] = code * 1024 + slot

        @pl.when((code >= 0) & (count < NEAR))
        def _():
            near_ref[count] = blocks[slot]

        return count + (code >= 0).astype(jnp.int32)

    list_ref[0] = lax.fori_loop(0, fresh_ref.shape[1], note, jnp.int32(0))


def sum_call(kernel, codes, sources, source_spaces, own, other, one, outs, out_spaces, extra, name):
    slots, (rhs_cols, block) = codes[0].shape[1], one
    return pl.pallas_call(
        kernel,
        out_shape=[jax.ShapeDtypeStruct((2, rhs_cols, block), jnp.float32)] + outs,
        in_specs=[pl.BlockSpec(memory_space=pltpu.SMEM)] * len(codes)
        + [pl.BlockSpec(memory_space=space) for space in source_spaces]
        + [pl.BlockSpec(memory_space=pltpu.HBM)] * 2,
        out_specs=[pl.BlockSpec(memory_space=space) for space in [pltpu.VMEM] + out_spaces],
        scratch_shapes=[
            pltpu.VMEM((slots, block, block), jnp.bfloat16),
            pltpu.SemaphoreType.DMA((2,)),
            pltpu.VMEM((slots, rhs_cols, block), jnp.bfloat16),
            pltpu.SemaphoreType.DMA,
        ]
        + extra,
        compiler_params=pltpu.CompilerParams(vmem_limit_bytes=SUM_LIMIT),
        cost_estimate=pl.CostEstimate(
            flops=2 * slots * rhs_cols * block * block,
            bytes_accessed=slots * block * (block + 2 * rhs_cols) * 4,
            transcendentals=0,
        ),
        name=name,
    )(*codes, *sources, own, other)


def first_sum(code, pieces, base, own, other):
    spaces = [pl.ANY] * len(pieces) + [pltpu.VMEM] * len(base)
    kernel = functools.partial(first_kernel, len(pieces), len(base))
    one = pieces[0].shape[-2:]
    return sum_call(kernel, [code], [*pieces, *base], spaces, own, other, one, [], [], [], "first_sum")[0]


def old_sum(level, code, fresh, pieces, solved, own, other):
    one = pieces[0].shape[-2:]
    outs = [
        jax.ShapeDtypeStruct((code.shape[1] + 1,), jnp.int32),
        jax.ShapeDtypeStruct((NEAR, one[1], one[1]), jnp.bfloat16),
    ]
    kernel = functools.partial(old_kernel, level, len(pieces))
    extra = []
    if solved:
        extra.append(pltpu.VMEM((sum(v.shape[0] for v in solved),) + one, jnp.bfloat16))
    spaces = [pl.ANY] * len(pieces) + [pltpu.VMEM] * len(solved)
    out_spaces = [pltpu.SMEM, pltpu.VMEM]
    sources = [*pieces, *solved]
    return sum_call(kernel, [code, fresh], sources, spaces, own, other, one, outs, out_spaces, extra, "old_sum")


def fresh_kernel(level, list_ref, old_ref, x_ref, near_ref, own_ref, other_ref, out_ref, far, sem):
    per_row = own_ref.shape[2]
    out_ref[...] = old_ref[...]
    count = list_ref[0]

    def add(block, entry):
        row = ((entry & 1023) >= per_row).astype(jnp.int32)
        out_ref[row] += nt_dot(x_ref[entry >> 10], block)

    def add_near(n, carry):
        add(near_ref[n], list_ref[1 + n])
        return carry

    def add_far(n, carry):
        slot = list_ref[1 + n] & 1023

        @pl.when(slot < per_row)
        def _():
            pltpu.make_async_copy(own_ref.at[level - 1, 0, slot], far, sem).start()

        @pl.when(slot >= per_row)
        def _():
            pltpu.make_async_copy(other_ref.at[level - 1, 0, slot - per_row], far, sem).start()

        pltpu.make_async_copy(own_ref.at[level - 1, 0, 0], far, sem).wait()
        add(far[...], list_ref[1 + n])
        return carry

    lax.fori_loop(0, jnp.minimum(count, NEAR), add_near, 0)
    lax.fori_loop(NEAR, count, add_far, 0)


def fresh_sum(level, listed, solved, old, near, own, other):
    block = solved.shape[-1]
    vmem = pl.BlockSpec(memory_space=pltpu.VMEM)
    return pl.pallas_call(
        functools.partial(fresh_kernel, level),
        out_shape=jax.ShapeDtypeStruct(old.shape, jnp.float32),
        in_specs=[pl.BlockSpec(memory_space=pltpu.SMEM)] + [vmem] * 3 + [pl.BlockSpec(memory_space=pltpu.HBM)] * 2,
        out_specs=vmem,
        scratch_shapes=[
            pltpu.VMEM((block, block), jnp.bfloat16),
            pltpu.SemaphoreType.DMA,
        ],
        compiler_params=pltpu.CompilerParams(vmem_limit_bytes=VMEM_LIMIT),
        name="fresh_sum",
    )(listed, old, solved, near, own, other)


def solve_kernel(level, p0, p1, p2, p3, rhs_ref, own_d_ref, other_d_ref, out_ref, *refs):
    core = lax.axis_index("core")
    for r, d_ref in enumerate((own_d_ref, other_d_ref)):
        coupled = (p0[r] + p1[r]) + (p2[r] + p3[r])
        reduced = (rhs_ref[level, r].astype(jnp.float32) - coupled).astype(jnp.bfloat16)
        solved = nt_dot(reduced, d_ref[level, 0]).astype(jnp.bfloat16)
        out_ref[r] = solved
        if refs:
            for i in range(refs[1].shape[0]):
                refs[1][i, core ^ r] = solved
    if refs:
        all_ref, copies, sem = refs
        send = pltpu.make_async_copy(copies, all_ref, sem)
        send.start()
        send.wait()


def solve_level(level, partials, rhs, own_d, other_d, copies):
    _, rhs_cols, block = partials[0].shape
    vmem = pl.BlockSpec(memory_space=pltpu.VMEM)
    out_shape, out_specs, scratch = [jax.ShapeDtypeStruct((2, rhs_cols, block), jnp.bfloat16)], [vmem], []
    if copies:
        out_shape.append(jax.ShapeDtypeStruct((copies, 2, rhs_cols, block), jnp.bfloat16))
        out_specs.append(pl.BlockSpec(memory_space=pltpu.HBM))
        scratch = [pltpu.VMEM((copies, 2, rhs_cols, block), jnp.bfloat16), pltpu.SemaphoreType.DMA]
    return pl.pallas_call(
        functools.partial(solve_kernel, level),
        out_shape=out_shape,
        in_specs=[vmem] * 7,
        out_specs=out_specs,
        scratch_shapes=scratch,
        compiler_params=pltpu.CompilerParams(vmem_limit_bytes=VMEM_LIMIT),
        name="solve_level",
    )(*partials, rhs, own_d, other_d)


def on_device(rhs, boundary, diag_inv, off_blocks, coupling, present):
    levels, _, rhs_cols, block = rhs.shape
    outer_each = boundary.shape[0]
    outer = outer_each * 32
    half = rhs_cols // 2
    z, y, core = lax.axis_index("z"), lax.axis_index("y"), lax.axis_index("core")

    def my_half(v, axis):
        return lax.dynamic_slice_in_dim(v, core * half, half, axis)

    def their_half(v, axis):
        return lax.dynamic_slice_in_dim(v, (1 - core) * half, half, axis)

    first = jnp.einsum("rb,ab->ra", rhs[0, 0], diag_inv[0, 0], preferred_element_type=jnp.float32).astype(jnp.bfloat16)
    known = jnp.concatenate([boundary, first[None]])
    known = jnp.stack([my_half(known, 1), their_half(known, 1)])
    code_own = (coupling + 1024 * present)[:, 0]
    code_both = jnp.stack([code_own, swap_cores(code_own)], axis=1)
    rhs_both = jnp.concatenate([my_half(rhs, 2), swap_cores(their_half(rhs, 2))], axis=1)
    diag_other = swap_cores(diag_inv)
    off_sent, known = lax.optimization_barrier((off_blocks, known))
    off_other = swap_cores(off_sent)

    pieces = gather_parts(known)
    pieces = pieces + [swap_cores(piece) for piece in pieces]

    keep, index = code_both >= 1024, code_both % 1024
    in_outer = index < outer
    row = jnp.where(in_outer, index // outer_each, index - outer)
    member = jnp.where(in_outer, index % outer_each, outer_each)
    src_z, src_y, src_core = row // 8, (row // 2) % 4, row % 2
    each = outer_each + 1
    away = jnp.where(src_core == 0, src_y - y, src_z - z) % 4
    part = jnp.where(src_core == 0, src_z ^ z, src_y ^ y)
    side = jnp.where(away == 3, 1, jnp.where(away == 1, 2, jnp.where(away == 2, 3, 0)))
    mine = src_core == core
    piece = side * 2 + part // 2
    in_piece = (part % 2) * 32 + member
    known_code = (piece + jnp.where(mine, 0, 8)) * 64 + in_piece
    level_of = jnp.maximum(index - outer, 0) // 32
    this = jnp.arange(levels - 1)[:, None, None]
    is_fresh = (level_of == this) & (level_of > 0)
    place_level = (index - outer) % 32
    old_code = jnp.where(level_of == 0, known_code, 1024 + (level_of - 1) * 32 + place_level)
    old_code = jnp.where(keep & ~is_fresh, old_code, -1).reshape(levels - 1, -1)
    fresh_code = jnp.where(keep & is_fresh, place_level, -1).reshape(levels - 1, -1)

    own_rows, other_rows = [], []
    steps = ((0, 1, 2, 5), (3, 4, 6, 7))
    early_code, late_code = (
        sum(jnp.where(keep & (piece == p), (n + jnp.where(mine, 0, 4)) * 64 + in_piece + 1, 0) for n, p in enumerate(some))[
            0
        ].reshape(1, -1)
        - 1
        for some in steps
    )
    early_pieces, late_pieces = ([pieces[p] for p in some] + [pieces[8 + p] for p in some] for some in steps)
    early = first_sum(early_code, early_pieces, [], off_blocks, off_other)
    value = first_sum(late_code, late_pieces, [early], off_blocks, off_other)
    solved_levels = []
    for level in range(1, levels):
        partials = [value] + [lax.ppermute(value, "x", xor_pairs(4, k)) for k in (1, 2, 3)]
        last = level == levels - 1
        outs = solve_level(level, partials, rhs_both, diag_inv, diag_other, 0 if last else 16)
        own_rows.append(outs[0][0])
        other_rows.append(outs[0][1])
        if not last:
            next_fresh, sent = lax.optimization_barrier((fresh_code, outs[1]))
            solved = lax.all_to_all(sent, ("z", "y"), 0, 0).reshape(32, half, block)
            old, listed, near = old_sum(
                level + 1, old_code, next_fresh, pieces, solved_levels, off_blocks, off_other
            )
            value = fresh_sum(level + 1, listed, solved, old, near, off_blocks, off_other)
            solved_levels = solved_levels + [solved]

    mine = jnp.stack(own_rows)
    theirs = swap_cores(jnp.stack(other_rows))
    low = jnp.where(core == 0, mine, theirs)
    high = jnp.where(core == 0, theirs, mine)
    rest = jnp.concatenate([low, high], axis=1)
    return jnp.concatenate([first[None], rest])[:, None]


def solution(mesh):
    split = Mesh(mesh.devices.reshape(4, 4, 2, 4), ("z", "y", "core", "x"))
    in_specs = (
        P(None, ROWS, None, None),
        P(ROWS, None, None),
        P(None, ROWS, None, None),
        P(None, ROWS, "x", None, None),
        P(None, ROWS, "x"),
        P(None, ROWS, "x"),
    )
    return jax.shard_map(
        on_device, mesh=split, in_specs=in_specs, out_specs=P(None, ROWS, None, None), check_vma=False
    )
```

```python
import functools

import jax
import jax.numpy as jnp
from jax import lax
from jax.experimental import pallas as pl
from jax.experimental.pallas import tpu as pltpu
from jax.sharding import Mesh, PartitionSpec as P

ROWS = ("z", "y", "core")
VMEM_LIMIT = 48 * 1024 * 1024


def xor_pairs(n, k):
    return [(i, i ^ k) for i in range(n)]


def shift_pairs(n, k):
    return [(i, (i + k) % n) for i in range(n)]


def swap_cores(v):
    return lax.ppermute(v, "core", xor_pairs(2, 1))


def pairs(stage, move):
    result = []
    for z in range(4):
        for y in range(4):
            for core in range(2):
                to_z, to_y = (move(z), y) if core + 1 == stage else (z, move(y))
                result.append(((z * 4 + y) * 2 + core, (to_z * 4 + to_y) * 2 + core))
    return result


def gather_parts(v):
    near = [lax.ppermute(v, ROWS, pairs(1, lambda i, k=k: i ^ k)) for k in (1, 2, 3)]
    low, high = jnp.stack([v, near[0]]), jnp.stack(near[1:])
    up, down = pairs(2, lambda i: (i + 1) % 4), pairs(2, lambda i: (i + 3) % 4)
    before_low, after_high = lax.ppermute(low, ROWS, up), lax.ppermute(high, ROWS, down)
    before_high, after_low = lax.ppermute(high, ROWS, up), lax.ppermute(low, ROWS, down)
    far = [lax.ppermute(before_low, ROWS, up), lax.ppermute(after_high, ROWS, down)]
    return [low, high, before_low, before_high, after_low, after_high] + far


def nt_dot(x, a):
    return lax.dot_general(x, a, (((1,), (1,)), ((), ())), preferred_element_type=jnp.float32)


GROUP = 8
NEAR = 16


def gather_sum(level, code_ref, picks, known, solved_ref, own_ref, other_ref, out_ref, blocks, block_sems, between):
    slots = code_ref.shape[1]
    per_row = slots // 2
    loads = [
        pltpu.make_async_copy(a_ref.at[level - 1, 0], blocks.at[pl.ds(r * per_row, per_row)], block_sems.at[r])
        for r, a_ref in enumerate((own_ref, other_ref))
    ]
    for load in loads:
        load.start()
    between()
    for r in range(2):
        loads[r].wait()
        total = None
        for g in range(r * per_row, (r + 1) * per_row, GROUP):
            xs, group = [], []
            for k in range(g, g + GROUP):
                code = code_ref[level - 1, k]
                kept = (code >= 0).astype(jnp.float32)
                picked = picks(k, jnp.clip(code, 0, known - 1))
                if solved_ref is not None:
                    picked = jnp.where(code >= known, solved_ref[jnp.maximum(code - known, 0)], picked)
                xs.append((picked.astype(jnp.float32) * kept).astype(jnp.bfloat16))
                group.append(blocks[k])
            part = nt_dot(jnp.concatenate(xs, axis=1), jnp.concatenate(group, axis=1))
            total = part if total is None else total + part
        out_ref[r] = total


def first_kernel(code_ref, *refs):
    sources, refs = refs[:-9], refs[-9:]
    own_ref, other_ref, out_ref, store_ref, blocks, block_sems, pack_sems, packed, store_sem = refs
    packs, start = [], 0
    for i, source in enumerate(sources):
        which = 0 if i < len(sources) // 2 else 1
        target = packed.at[pl.ds(start, source.shape[0])]
        packs.append(pltpu.make_async_copy(source.at[:, which], target, pack_sems.at[i]))
        start += source.shape[0]
    keep = pltpu.make_async_copy(packed, store_ref.at[pl.ds(0, start)], store_sem)

    def between():
        for pack in packs:
            pack.start()
        for pack in packs:
            pack.wait()
        keep.start()

    each = packed.shape[1]
    picks = lambda k, code: packed[code // each, code % each]
    gather_sum(1, code_ref, picks, start * each, None, own_ref, other_ref, out_ref, blocks, block_sems, between)
    keep.wait()


def old_kernel(level, known, code_ref, fresh_ref, store_ref, *refs):
    solved, refs = refs[: level - 2], refs[level - 2 :]
    own_ref, other_ref, out_ref, list_ref, near_ref, blocks, block_sems, picked, pick_sem = refs[:9]
    solved_ref = refs[9] if solved else None
    slots = code_ref.shape[1]

    def between():
        for k in range(slots):
            place = jnp.clip(code_ref[level - 1, k], 0, known - 1)
            pltpu.make_async_copy(store_ref.at[place], picked.at[k], pick_sem).start()
        for i, one in enumerate(solved):
            solved_ref[i * one.shape[0] : (i + 1) * one.shape[0]] = one[...]
        pltpu.make_async_copy(store_ref.at[pl.ds(0, slots)], picked, pick_sem).wait()

    picks = lambda k, code: picked[k]
    gather_sum(level, code_ref, picks, known, solved_ref, own_ref, other_ref, out_ref, blocks, block_sems, between)

    def note(slot, count):
        code = fresh_ref[level - 1, slot]

        @pl.when(code >= 0)
        def _():
            list_ref[1 + count] = code * 1024 + slot

        @pl.when((code >= 0) & (count < NEAR))
        def _():
            near_ref[count] = blocks[slot]

        return count + (code >= 0).astype(jnp.int32)

    list_ref[0] = lax.fori_loop(0, fresh_ref.shape[1], note, jnp.int32(0))


def sum_call(kernel, codes, sources, source_spaces, own, other, outs, out_spaces, extra, name, limit):
    slots, (rhs_cols, block) = codes[0].shape[1], sources[0].shape[-2:]
    return pl.pallas_call(
        kernel,
        out_shape=[jax.ShapeDtypeStruct((2, rhs_cols, block), jnp.float32)] + outs,
        in_specs=[pl.BlockSpec(memory_space=pltpu.SMEM)] * len(codes)
        + [pl.BlockSpec(memory_space=space) for space in source_spaces]
        + [pl.BlockSpec(memory_space=pltpu.HBM)] * 2,
        out_specs=[pl.BlockSpec(memory_space=space) for space in [pltpu.VMEM] + out_spaces],
        scratch_shapes=[pltpu.VMEM((slots, block, block), jnp.bfloat16), pltpu.SemaphoreType.DMA((2,))] + extra,
        compiler_params=pltpu.CompilerParams(vmem_limit_bytes=limit),
        cost_estimate=pl.CostEstimate(
            flops=2 * slots * rhs_cols * block * block,
            bytes_accessed=slots * block * (block + 2 * rhs_cols) * 4,
            transcendentals=0,
        ),
        name=name,
    )(*codes, *sources, own, other)


def first_sum(code, sources, own, other):
    one = sources[0].shape[3:]
    parts = sum(v.shape[0] for v in sources)
    each = sources[0].shape[2]
    store = jax.ShapeDtypeStruct((2048 // each, each) + one, jnp.bfloat16)
    extra = [
        pltpu.SemaphoreType.DMA((len(sources),)),
        pltpu.VMEM((parts, each) + one, jnp.bfloat16),
        pltpu.SemaphoreType.DMA,
    ]
    spaces = [pl.ANY] * len(sources)
    return sum_call(first_kernel, [code], sources, spaces, own, other, [store], [pltpu.HBM], extra, "first_sum", 60 * 1024 * 1024)


def old_sum(level, known, code, fresh, store, solved, own, other):
    one = store.shape[1:]
    outs = [
        jax.ShapeDtypeStruct((code.shape[1] + 1,), jnp.int32),
        jax.ShapeDtypeStruct((NEAR, one[1], one[1]), jnp.bfloat16),
    ]
    kernel = functools.partial(old_kernel, level, known)
    extra = [pltpu.VMEM((code.shape[1],) + one, jnp.bfloat16), pltpu.SemaphoreType.DMA]
    if solved:
        extra.append(pltpu.VMEM((sum(v.shape[0] for v in solved),) + one, jnp.bfloat16))
    spaces = [pl.ANY] + [pltpu.VMEM] * len(solved)
    out_spaces = [pltpu.SMEM, pltpu.VMEM]
    return sum_call(kernel, [code, fresh], [store] + solved, spaces, own, other, outs, out_spaces, extra, "old_sum", VMEM_LIMIT)


def fresh_kernel(level, list_ref, old_ref, x_ref, near_ref, own_ref, other_ref, out_ref, far, sem):
    per_row = own_ref.shape[2]
    out_ref[...] = old_ref[...]
    count = list_ref[0]

    def add(block, entry):
        row = ((entry & 1023) >= per_row).astype(jnp.int32)
        out_ref[row] += nt_dot(x_ref[entry >> 10], block)

    def add_near(n, carry):
        add(near_ref[n], list_ref[1 + n])
        return carry

    def add_far(n, carry):
        slot = list_ref[1 + n] & 1023

        @pl.when(slot < per_row)
        def _():
            pltpu.make_async_copy(own_ref.at[level - 1, 0, slot], far, sem).start()

        @pl.when(slot >= per_row)
        def _():
            pltpu.make_async_copy(other_ref.at[level - 1, 0, slot - per_row], far, sem).start()

        pltpu.make_async_copy(own_ref.at[level - 1, 0, 0], far, sem).wait()
        add(far[...], list_ref[1 + n])
        return carry

    lax.fori_loop(0, jnp.minimum(count, NEAR), add_near, 0)
    lax.fori_loop(NEAR, count, add_far, 0)


def fresh_sum(level, listed, solved, old, near, own, other):
    block = solved.shape[-1]
    vmem = pl.BlockSpec(memory_space=pltpu.VMEM)
    return pl.pallas_call(
        functools.partial(fresh_kernel, level),
        out_shape=jax.ShapeDtypeStruct(old.shape, jnp.float32),
        in_specs=[pl.BlockSpec(memory_space=pltpu.SMEM)] + [vmem] * 3 + [pl.BlockSpec(memory_space=pltpu.HBM)] * 2,
        out_specs=vmem,
        scratch_shapes=[
            pltpu.VMEM((block, block), jnp.bfloat16),
            pltpu.SemaphoreType.DMA,
        ],
        compiler_params=pltpu.CompilerParams(vmem_limit_bytes=VMEM_LIMIT),
        name="fresh_sum",
    )(listed, old, solved, near, own, other)


def solve_kernel(level, p0, p1, p2, p3, rhs_ref, own_d_ref, other_d_ref, out_ref, *refs):
    core = lax.axis_index("core")
    for r, d_ref in enumerate((own_d_ref, other_d_ref)):
        coupled = (p0[r] + p1[r]) + (p2[r] + p3[r])
        reduced = (rhs_ref[level, r].astype(jnp.float32) - coupled).astype(jnp.bfloat16)
        solved = nt_dot(reduced, d_ref[level, 0]).astype(jnp.bfloat16)
        out_ref[r] = solved
        if refs:
            for i in range(refs[1].shape[0]):
                refs[1][i, core ^ r] = solved
    if refs:
        all_ref, copies, sem = refs
        send = pltpu.make_async_copy(copies, all_ref, sem)
        send.start()
        send.wait()


def solve_level(level, partials, rhs, own_d, other_d, copies):
    _, rhs_cols, block = partials[0].shape
    vmem = pl.BlockSpec(memory_space=pltpu.VMEM)
    out_shape, out_specs, scratch = [jax.ShapeDtypeStruct((2, rhs_cols, block), jnp.bfloat16)], [vmem], []
    if copies:
        out_shape.append(jax.ShapeDtypeStruct((copies, 2, rhs_cols, block), jnp.bfloat16))
        out_specs.append(pl.BlockSpec(memory_space=pltpu.HBM))
        scratch = [pltpu.VMEM((copies, 2, rhs_cols, block), jnp.bfloat16), pltpu.SemaphoreType.DMA]
    return pl.pallas_call(
        functools.partial(solve_kernel, level),
        out_shape=out_shape,
        in_specs=[vmem] * 7,
        out_specs=out_specs,
        scratch_shapes=scratch,
        compiler_params=pltpu.CompilerParams(vmem_limit_bytes=VMEM_LIMIT),
        name="solve_level",
    )(*partials, rhs, own_d, other_d)


def on_device(rhs, boundary, diag_inv, off_blocks, coupling, present):
    levels, _, rhs_cols, block = rhs.shape
    outer_each = boundary.shape[0]
    outer = outer_each * 32
    half = rhs_cols // 2
    z, y, core = lax.axis_index("z"), lax.axis_index("y"), lax.axis_index("core")

    def my_half(v, axis):
        return lax.dynamic_slice_in_dim(v, core * half, half, axis)

    def their_half(v, axis):
        return lax.dynamic_slice_in_dim(v, (1 - core) * half, half, axis)

    first = jnp.einsum("rb,ab->ra", rhs[0, 0], diag_inv[0, 0], preferred_element_type=jnp.float32).astype(jnp.bfloat16)
    known = jnp.concatenate([boundary, first[None]])
    known = jnp.stack([my_half(known, 1), their_half(known, 1)])
    code_own = (coupling + 1024 * present)[:, 0]
    code_both = jnp.stack([code_own, swap_cores(code_own)], axis=1)
    rhs_both = jnp.concatenate([my_half(rhs, 2), swap_cores(their_half(rhs, 2))], axis=1)
    diag_other = swap_cores(diag_inv)
    off_sent, known = lax.optimization_barrier((off_blocks, known))
    off_other = swap_cores(off_sent)

    pieces = gather_parts(known)
    arrived = lax.optimization_barrier(tuple(pieces[:6]))
    pieces = pieces + [swap_cores(piece) for piece in [*arrived, *pieces[6:]]]

    keep, index = code_both >= 1024, code_both % 1024
    in_outer = index < outer
    row = jnp.where(in_outer, index // outer_each, index - outer)
    member = jnp.where(in_outer, index % outer_each, outer_each)
    src_z, src_y, src_core = row // 8, (row // 2) % 4, row % 2
    each = outer_each + 1
    away = jnp.where(src_core == 0, src_y - y, src_z - z) % 4
    part = jnp.where(away == 3, 1, jnp.where(away == 1, 2, jnp.where(away == 2, 3, 0))) * 4
    part = part + jnp.where(src_core == 0, src_z ^ z, src_y ^ y) + jnp.where(src_core == core, 0, 16)
    known_place = part * each + member
    level_of = jnp.maximum(index - outer, 0) // 32
    this = jnp.arange(levels - 1)[:, None, None]
    is_fresh = (level_of == this) & (level_of > 0)
    place_level = (index - outer) % 32
    old_code = jnp.where(level_of == 0, known_place, 32 * each + (level_of - 1) * 32 + place_level)
    old_code = jnp.where(keep & ~is_fresh, old_code, -1).reshape(levels - 1, -1)
    fresh_code = jnp.where(keep & is_fresh, place_level, -1).reshape(levels - 1, -1)

    own_rows, other_rows = [], []
    value, store = first_sum(old_code, pieces, off_blocks, off_other)
    store = store.reshape((-1,) + store.shape[2:])
    solved_levels = []
    for level in range(1, levels):
        partials = [value] + [lax.ppermute(value, "x", xor_pairs(4, k)) for k in (1, 2, 3)]
        last = level == levels - 1
        outs = solve_level(level, partials, rhs_both, diag_inv, diag_other, 0 if last else 16)
        own_rows.append(outs[0][0])
        other_rows.append(outs[0][1])
        if not last:
            next_fresh, sent = lax.optimization_barrier((fresh_code, outs[1]))
            solved = lax.all_to_all(sent, ("z", "y"), 0, 0).reshape(32, half, block)
            old, listed, near = old_sum(
                level + 1, 32 * each, old_code, next_fresh, store, solved_levels, off_blocks, off_other
            )
            value = fresh_sum(level + 1, listed, solved, old, near, off_blocks, off_other)
            solved_levels = solved_levels + [solved]

    mine = jnp.stack(own_rows)
    theirs = swap_cores(jnp.stack(other_rows))
    low = jnp.where(core == 0, mine, theirs)
    high = jnp.where(core == 0, theirs, mine)
    rest = jnp.concatenate([low, high], axis=1)
    return jnp.concatenate([first[None], rest])[:, None]


def solution(mesh):
    split = Mesh(mesh.devices.reshape(4, 4, 2, 4), ("z", "y", "core", "x"))
    in_specs = (
        P(None, ROWS, None, None),
        P(ROWS, None, None),
        P(None, ROWS, None, None),
        P(None, ROWS, "x", None, None),
        P(None, ROWS, "x"),
        P(None, ROWS, "x"),
    )
    return jax.shard_map(
        on_device, mesh=split, in_specs=in_specs, out_specs=P(None, ROWS, None, None), check_vma=False
    )
```

```python
import functools

import jax
import jax.numpy as jnp
from jax import lax
from jax.experimental import pallas as pl
from jax.experimental.pallas import tpu as pltpu
from jax.sharding import Mesh, PartitionSpec as P

ROWS = ("z", "y", "core")
VMEM_LIMIT = 48 * 1024 * 1024


def xor_pairs(n, k):
    return [(i, i ^ k) for i in range(n)]


def shift_pairs(n, k):
    return [(i, (i + k) % n) for i in range(n)]


def swap_cores(v):
    return lax.ppermute(v, "core", xor_pairs(2, 1))


def pairs(stage, move):
    result = []
    for z in range(4):
        for y in range(4):
            for core in range(2):
                to_z, to_y = (move(z), y) if core + 1 == stage else (z, move(y))
                result.append(((z * 4 + y) * 2 + core, (to_z * 4 + to_y) * 2 + core))
    return result


def gather_parts(v):
    near = [lax.ppermute(v, ROWS, pairs(1, lambda i, k=k: i ^ k)) for k in (1, 2, 3)]
    low, high = jnp.stack([v, near[0]]), jnp.stack(near[1:])
    up, down = pairs(2, lambda i: (i + 1) % 4), pairs(2, lambda i: (i + 3) % 4)
    before_low, after_high = lax.ppermute(low, ROWS, up), lax.ppermute(high, ROWS, down)
    before_high, after_low = lax.ppermute(high, ROWS, up), lax.ppermute(low, ROWS, down)
    far = [lax.ppermute(before_low, ROWS, up), lax.ppermute(after_high, ROWS, down)]
    return [low, high, before_low, before_high, after_low, after_high] + far


def nt_dot(x, a):
    return lax.dot_general(x, a, (((1,), (1,)), ((), ())), preferred_element_type=jnp.float32)


GROUP = 8
NEAR = 16


def gather_sum(level, code_ref, picks, known, solved_ref, own_ref, other_ref, out_ref, blocks, block_sems, between):
    slots = code_ref.shape[1]
    per_row = slots // 2
    loads = [
        pltpu.make_async_copy(a_ref.at[level - 1, 0], blocks.at[pl.ds(r * per_row, per_row)], block_sems.at[r])
        for r, a_ref in enumerate((own_ref, other_ref))
    ]
    for load in loads:
        load.start()
    between()
    for r in range(2):
        loads[r].wait()
        total = None
        for g in range(r * per_row, (r + 1) * per_row, GROUP):
            xs, group = [], []
            for k in range(g, g + GROUP):
                code = code_ref[level - 1, k]
                kept = (code >= 0).astype(jnp.float32)
                picked = picks(k, jnp.clip(code, 0, known - 1))
                if solved_ref is not None:
                    picked = jnp.where(code >= known, solved_ref[jnp.maximum(code - known, 0)], picked)
                xs.append((picked.astype(jnp.float32) * kept).astype(jnp.bfloat16))
                group.append(blocks[k])
            part = nt_dot(jnp.concatenate(xs, axis=1), jnp.concatenate(group, axis=1))
            total = part if total is None else total + part
        out_ref[r] = total


def first_kernel(code_ref, *refs):
    sources, refs = refs[:-9], refs[-9:]
    own_ref, other_ref, out_ref, store_ref, blocks, block_sems, pack_sems, packed, store_sem = refs
    packs, start = [], 0
    for i, source in enumerate(sources):
        which = 0 if i < len(sources) // 2 else 1
        target = packed.at[pl.ds(start, source.shape[0])]
        packs.append(pltpu.make_async_copy(source.at[:, which], target, pack_sems.at[i]))
        start += source.shape[0]
    keep = pltpu.make_async_copy(packed, store_ref.at[pl.ds(0, start)], store_sem)

    def between():
        for pack in packs:
            pack.start()
        for pack in packs:
            pack.wait()
        keep.start()

    each = packed.shape[1]
    picks = lambda k, code: packed[code // each, code % each]
    gather_sum(1, code_ref, picks, start * each, None, own_ref, other_ref, out_ref, blocks, block_sems, between)
    keep.wait()


def old_kernel(level, known, code_ref, fresh_ref, store_ref, *refs):
    solved, refs = refs[: level - 2], refs[level - 2 :]
    own_ref, other_ref, out_ref, list_ref, near_ref, blocks, block_sems, picked, pick_sem = refs[:9]
    solved_ref = refs[9] if solved else None
    slots = code_ref.shape[1]

    def between():
        for k in range(slots):
            place = jnp.clip(code_ref[level - 1, k], 0, known - 1)
            pltpu.make_async_copy(store_ref.at[place], picked.at[k], pick_sem).start()
        for i, one in enumerate(solved):
            solved_ref[i * one.shape[0] : (i + 1) * one.shape[0]] = one[...]
        pltpu.make_async_copy(store_ref.at[pl.ds(0, slots)], picked, pick_sem).wait()

    picks = lambda k, code: picked[k]
    gather_sum(level, code_ref, picks, known, solved_ref, own_ref, other_ref, out_ref, blocks, block_sems, between)

    def note(slot, count):
        code = fresh_ref[level - 1, slot]

        @pl.when(code >= 0)
        def _():
            list_ref[1 + count] = code * 1024 + slot

        @pl.when((code >= 0) & (count < NEAR))
        def _():
            near_ref[count] = blocks[slot]

        return count + (code >= 0).astype(jnp.int32)

    list_ref[0] = lax.fori_loop(0, fresh_ref.shape[1], note, jnp.int32(0))


def sum_call(kernel, codes, sources, source_spaces, own, other, outs, out_spaces, extra, name, limit):
    slots, (rhs_cols, block) = codes[0].shape[1], sources[0].shape[-2:]
    return pl.pallas_call(
        kernel,
        out_shape=[jax.ShapeDtypeStruct((2, rhs_cols, block), jnp.float32)] + outs,
        in_specs=[pl.BlockSpec(memory_space=pltpu.SMEM)] * len(codes)
        + [pl.BlockSpec(memory_space=space) for space in source_spaces]
        + [pl.BlockSpec(memory_space=pltpu.HBM)] * 2,
        out_specs=[pl.BlockSpec(memory_space=space) for space in [pltpu.VMEM] + out_spaces],
        scratch_shapes=[pltpu.VMEM((slots, block, block), jnp.bfloat16), pltpu.SemaphoreType.DMA((2,))] + extra,
        compiler_params=pltpu.CompilerParams(vmem_limit_bytes=limit),
        cost_estimate=pl.CostEstimate(
            flops=2 * slots * rhs_cols * block * block,
            bytes_accessed=slots * block * (block + 2 * rhs_cols) * 4,
            transcendentals=0,
        ),
        name=name,
    )(*codes, *sources, own, other)


def first_sum(code, sources, own, other):
    one = sources[0].shape[3:]
    parts = sum(v.shape[0] for v in sources)
    each = sources[0].shape[2]
    store = jax.ShapeDtypeStruct((2048 // each, each) + one, jnp.bfloat16)
    extra = [
        pltpu.SemaphoreType.DMA((len(sources),)),
        pltpu.VMEM((parts, each) + one, jnp.bfloat16),
        pltpu.SemaphoreType.DMA,
    ]
    spaces = [pl.ANY] * len(sources)
    return sum_call(first_kernel, [code], sources, spaces, own, other, [store], [pltpu.HBM], extra, "first_sum", 60 * 1024 * 1024)


def old_sum(level, known, code, fresh, store, solved, own, other):
    one = store.shape[1:]
    outs = [
        jax.ShapeDtypeStruct((code.shape[1] + 1,), jnp.int32),
        jax.ShapeDtypeStruct((NEAR, one[1], one[1]), jnp.bfloat16),
    ]
    kernel = functools.partial(old_kernel, level, known)
    extra = [pltpu.VMEM((code.shape[1],) + one, jnp.bfloat16), pltpu.SemaphoreType.DMA]
    if solved:
        extra.append(pltpu.VMEM((sum(v.shape[0] for v in solved),) + one, jnp.bfloat16))
    spaces = [pl.ANY] + [pltpu.VMEM] * len(solved)
    out_spaces = [pltpu.SMEM, pltpu.VMEM]
    return sum_call(kernel, [code, fresh], [store] + solved, spaces, own, other, outs, out_spaces, extra, "old_sum", VMEM_LIMIT)


def fresh_kernel(level, list_ref, old_ref, x_ref, near_ref, own_ref, other_ref, out_ref, far, sem):
    per_row = own_ref.shape[2]
    out_ref[...] = old_ref[...]
    count = list_ref[0]

    def add(block, entry):
        row = ((entry & 1023) >= per_row).astype(jnp.int32)
        out_ref[row] += nt_dot(x_ref[entry >> 10], block)

    def add_near(n, carry):
        add(near_ref[n], list_ref[1 + n])
        return carry

    def add_far(n, carry):
        slot = list_ref[1 + n] & 1023

        @pl.when(slot < per_row)
        def _():
            pltpu.make_async_copy(own_ref.at[level - 1, 0, slot], far, sem).start()

        @pl.when(slot >= per_row)
        def _():
            pltpu.make_async_copy(other_ref.at[level - 1, 0, slot - per_row], far, sem).start()

        pltpu.make_async_copy(own_ref.at[level - 1, 0, 0], far, sem).wait()
        add(far[...], list_ref[1 + n])
        return carry

    lax.fori_loop(0, jnp.minimum(count, NEAR), add_near, 0)
    lax.fori_loop(NEAR, count, add_far, 0)


def fresh_sum(level, listed, solved, old, near, own, other):
    block = solved.shape[-1]
    vmem = pl.BlockSpec(memory_space=pltpu.VMEM)
    return pl.pallas_call(
        functools.partial(fresh_kernel, level),
        out_shape=jax.ShapeDtypeStruct(old.shape, jnp.float32),
        in_specs=[pl.BlockSpec(memory_space=pltpu.SMEM)] + [vmem] * 3 + [pl.BlockSpec(memory_space=pltpu.HBM)] * 2,
        out_specs=vmem,
        scratch_shapes=[
            pltpu.VMEM((block, block), jnp.bfloat16),
            pltpu.SemaphoreType.DMA,
        ],
        compiler_params=pltpu.CompilerParams(vmem_limit_bytes=VMEM_LIMIT),
        name="fresh_sum",
    )(listed, old, solved, near, own, other)


def solve_kernel(level, p0, p1, p2, p3, rhs_ref, own_d_ref, other_d_ref, out_ref, *refs):
    core = lax.axis_index("core")
    for r, d_ref in enumerate((own_d_ref, other_d_ref)):
        coupled = (p0[r] + p1[r]) + (p2[r] + p3[r])
        reduced = (rhs_ref[level, r].astype(jnp.float32) - coupled).astype(jnp.bfloat16)
        solved = nt_dot(reduced, d_ref[level, 0]).astype(jnp.bfloat16)
        out_ref[r] = solved
        if refs:
            for i in range(refs[1].shape[0]):
                refs[1][i, core ^ r] = solved
    if refs:
        all_ref, copies, sem = refs
        send = pltpu.make_async_copy(copies, all_ref, sem)
        send.start()
        send.wait()


def solve_level(level, partials, rhs, own_d, other_d, copies):
    _, rhs_cols, block = partials[0].shape
    vmem = pl.BlockSpec(memory_space=pltpu.VMEM)
    out_shape, out_specs, scratch = [jax.ShapeDtypeStruct((2, rhs_cols, block), jnp.bfloat16)], [vmem], []
    if copies:
        out_shape.append(jax.ShapeDtypeStruct((copies, 2, rhs_cols, block), jnp.bfloat16))
        out_specs.append(pl.BlockSpec(memory_space=pltpu.HBM))
        scratch = [pltpu.VMEM((copies, 2, rhs_cols, block), jnp.bfloat16), pltpu.SemaphoreType.DMA]
    return pl.pallas_call(
        functools.partial(solve_kernel, level),
        out_shape=out_shape,
        in_specs=[vmem] * 7,
        out_specs=out_specs,
        scratch_shapes=scratch,
        compiler_params=pltpu.CompilerParams(vmem_limit_bytes=VMEM_LIMIT),
        name="solve_level",
    )(*partials, rhs, own_d, other_d)


def on_device(rhs, boundary, diag_inv, off_blocks, coupling, present):
    levels, _, rhs_cols, block = rhs.shape
    outer_each = boundary.shape[0]
    outer = outer_each * 32
    half = rhs_cols // 2
    z, y, core = lax.axis_index("z"), lax.axis_index("y"), lax.axis_index("core")

    def my_half(v, axis):
        return lax.dynamic_slice_in_dim(v, core * half, half, axis)

    def their_half(v, axis):
        return lax.dynamic_slice_in_dim(v, (1 - core) * half, half, axis)

    first = jnp.einsum("rb,ab->ra", rhs[0, 0], diag_inv[0, 0], preferred_element_type=jnp.float32).astype(jnp.bfloat16)
    known = jnp.concatenate([boundary, first[None]])
    known = jnp.stack([my_half(known, 1), their_half(known, 1)])
    code_own = (coupling + 1024 * present)[:, 0]
    code_both = jnp.stack([code_own, swap_cores(code_own)], axis=1)
    rhs_both = jnp.concatenate([my_half(rhs, 2), swap_cores(their_half(rhs, 2))], axis=1)
    diag_other = swap_cores(diag_inv)
    off_sent, known = lax.optimization_barrier((off_blocks, known))
    off_other = swap_cores(off_sent)

    pieces = gather_parts(known)
    pieces = pieces + [swap_cores(piece) for piece in pieces]

    keep, index = code_both >= 1024, code_both % 1024
    in_outer = index < outer
    row = jnp.where(in_outer, index // outer_each, index - outer)
    member = jnp.where(in_outer, index % outer_each, outer_each)
    src_z, src_y, src_core = row // 8, (row // 2) % 4, row % 2
    each = outer_each + 1
    away = jnp.where(src_core == 0, src_y - y, src_z - z) % 4
    part = jnp.where(away == 3, 1, jnp.where(away == 1, 2, jnp.where(away == 2, 3, 0))) * 4
    part = part + jnp.where(src_core == 0, src_z ^ z, src_y ^ y) + jnp.where(src_core == core, 0, 16)
    known_place = part * each + member
    level_of = jnp.maximum(index - outer, 0) // 32
    this = jnp.arange(levels - 1)[:, None, None]
    is_fresh = (level_of == this) & (level_of > 0)
    place_level = (index - outer) % 32
    old_code = jnp.where(level_of == 0, known_place, 32 * each + (level_of - 1) * 32 + place_level)
    old_code = jnp.where(keep & ~is_fresh, old_code, -1).reshape(levels - 1, -1)
    fresh_code = jnp.where(keep & is_fresh, place_level, -1).reshape(levels - 1, -1)

    own_rows, other_rows = [], []
    value, store = first_sum(old_code, pieces, off_blocks, off_other)
    store = store.reshape((-1,) + store.shape[2:])
    solved_levels = []
    for level in range(1, levels):
        partials = [value] + [lax.ppermute(value, "x", xor_pairs(4, k)) for k in (1, 2, 3)]
        last = level == levels - 1
        outs = solve_level(level, partials, rhs_both, diag_inv, diag_other, 0 if last else 16)
        own_rows.append(outs[0][0])
        other_rows.append(outs[0][1])
        if not last:
            next_fresh, sent = lax.optimization_barrier((fresh_code, outs[1]))
            solved = lax.all_to_all(sent, ("z", "y"), 0, 0).reshape(32, half, block)
            old, listed, near = old_sum(
                level + 1, 32 * each, old_code, next_fresh, store, solved_levels, off_blocks, off_other
            )
            value = fresh_sum(level + 1, listed, solved, old, near, off_blocks, off_other)
            solved_levels = solved_levels + [solved]

    mine = jnp.stack(own_rows)
    theirs = swap_cores(jnp.stack(other_rows))
    low = jnp.where(core == 0, mine, theirs)
    high = jnp.where(core == 0, theirs, mine)
    rest = jnp.concatenate([low, high], axis=1)
    return jnp.concatenate([first[None], rest])[:, None]


def solution(mesh):
    split = Mesh(mesh.devices.reshape(4, 4, 2, 4), ("z", "y", "core", "x"))
    in_specs = (
        P(None, ROWS, None, None),
        P(ROWS, None, None),
        P(None, ROWS, None, None),
        P(None, ROWS, "x", None, None),
        P(None, ROWS, "x"),
        P(None, ROWS, "x"),
    )
    return jax.shard_map(
        on_device, mesh=split, in_specs=in_specs, out_specs=P(None, ROWS, None, None), check_vma=False
    )
```

```python
import functools

import jax
import jax.numpy as jnp
from jax import lax
from jax.experimental import pallas as pl
from jax.experimental.pallas import tpu as pltpu
from jax.sharding import Mesh, PartitionSpec as P

ROWS = ("z", "y", "core")
VMEM_LIMIT = 48 * 1024 * 1024


def xor_pairs(n, k):
    return [(i, i ^ k) for i in range(n)]


def shift_pairs(n, k):
    return [(i, (i + k) % n) for i in range(n)]


def swap_cores(v):
    return lax.ppermute(v, "core", xor_pairs(2, 1))


def pairs(stage, move, cross=False):
    result = []
    for z in range(4):
        for y in range(4):
            for core in range(2):
                to_z, to_y = (move(z), y) if core + 1 == stage else (z, move(y))
                to_core = 1 - core if cross else core
                result.append(((z * 4 + y) * 2 + core, (to_z * 4 + to_y) * 2 + to_core))
    return result


def gather_parts(v):
    after_one, before_one = lambda i: (i + 1) % 4, lambda i: (i + 3) % 4
    near = [v] + [lax.ppermute(v, ROWS, pairs(1, lambda i, k=k: i ^ k)) for k in (1, 2, 3)]
    mine, theirs = jnp.stack([one[0] for one in near]), jnp.stack([one[1] for one in near])

    def spread(part, cross):
        again = 1 if cross else 2
        before = lax.ppermute(part, ROWS, pairs(2, after_one, cross))
        after = lax.ppermute(part, ROWS, pairs(2, before_one, cross))
        far_low = lax.ppermute(before[:2], ROWS, pairs(again, after_one))
        far_high = lax.ppermute(after[2:], ROWS, pairs(again, before_one))
        return [before, after, far_low, far_high]

    return [mine, *spread(mine, False), swap_cores(theirs), *spread(theirs, True)]


def nt_dot(x, a):
    return lax.dot_general(x, a, (((1,), (1,)), ((), ())), preferred_element_type=jnp.float32)


GROUP = 8
NEAR = 16


def gather_sum(level, code_ref, picks, known, solved_ref, own_ref, other_ref, out_ref, blocks, block_sems, between):
    slots = code_ref.shape[1]
    per_row = slots // 2
    loads = [
        pltpu.make_async_copy(a_ref.at[level - 1, 0], blocks.at[pl.ds(r * per_row, per_row)], block_sems.at[r])
        for r, a_ref in enumerate((own_ref, other_ref))
    ]
    for load in loads:
        load.start()
    between()
    for r in range(2):
        loads[r].wait()
        total = None
        for g in range(r * per_row, (r + 1) * per_row, GROUP):
            xs, group = [], []
            for k in range(g, g + GROUP):
                code = code_ref[level - 1, k]
                kept = (code >= 0).astype(jnp.float32)
                picked = picks(k, jnp.clip(code, 0, known - 1))
                if solved_ref is not None:
                    picked = jnp.where(code >= known, solved_ref[jnp.maximum(code - known, 0)], picked)
                xs.append((picked.astype(jnp.float32) * kept).astype(jnp.bfloat16))
                group.append(blocks[k])
            part = nt_dot(jnp.concatenate(xs, axis=1), jnp.concatenate(group, axis=1))
            total = part if total is None else total + part
        out_ref[r] = total


def first_kernel(code_ref, *refs):
    sources, refs = refs[:-9], refs[-9:]
    own_ref, other_ref, out_ref, store_ref, blocks, block_sems, pack_sems, packed, store_sem = refs
    packs, start = [], 0
    for i, source in enumerate(sources):
        target = packed.at[pl.ds(start, source.shape[0])]
        packs.append(pltpu.make_async_copy(source, target, pack_sems.at[i]))
        start += source.shape[0]
    keep = pltpu.make_async_copy(packed, store_ref.at[pl.ds(0, start)], store_sem)

    def between():
        for pack in packs:
            pack.start()
        for pack in packs:
            pack.wait()
        keep.start()

    each = packed.shape[1]
    picks = lambda k, code: packed[code // each, code % each]
    gather_sum(1, code_ref, picks, start * each, None, own_ref, other_ref, out_ref, blocks, block_sems, between)
    keep.wait()


def old_kernel(level, known, code_ref, fresh_ref, store_ref, *refs):
    solved, refs = refs[: level - 2], refs[level - 2 :]
    own_ref, other_ref, out_ref, list_ref, near_ref, blocks, block_sems, picked, pick_sem = refs[:9]
    solved_ref = refs[9] if solved else None
    slots = code_ref.shape[1]

    def between():
        for k in range(slots):
            place = jnp.clip(code_ref[level - 1, k], 0, known - 1)
            pltpu.make_async_copy(store_ref.at[place], picked.at[k], pick_sem).start()
        for i, one in enumerate(solved):
            solved_ref[i * one.shape[0] : (i + 1) * one.shape[0]] = one[...]
        pltpu.make_async_copy(store_ref.at[pl.ds(0, slots)], picked, pick_sem).wait()

    picks = lambda k, code: picked[k]
    gather_sum(level, code_ref, picks, known, solved_ref, own_ref, other_ref, out_ref, blocks, block_sems, between)

    def note(slot, count):
        code = fresh_ref[level - 1, slot]

        @pl.when(code >= 0)
        def _():
            list_ref[1 + count] = code * 1024 + slot

        @pl.when((code >= 0) & (count < NEAR))
        def _():
            near_ref[count] = blocks[slot]

        return count + (code >= 0).astype(jnp.int32)

    list_ref[0] = lax.fori_loop(0, fresh_ref.shape[1], note, jnp.int32(0))


def sum_call(kernel, codes, sources, source_spaces, own, other, outs, out_spaces, extra, name, limit):
    slots, (rhs_cols, block) = codes[0].shape[1], sources[0].shape[-2:]
    return pl.pallas_call(
        kernel,
        out_shape=[jax.ShapeDtypeStruct((2, rhs_cols, block), jnp.float32)] + outs,
        in_specs=[pl.BlockSpec(memory_space=pltpu.SMEM)] * len(codes)
        + [pl.BlockSpec(memory_space=space) for space in source_spaces]
        + [pl.BlockSpec(memory_space=pltpu.HBM)] * 2,
        out_specs=[pl.BlockSpec(memory_space=space) for space in [pltpu.VMEM] + out_spaces],
        scratch_shapes=[pltpu.VMEM((slots, block, block), jnp.bfloat16), pltpu.SemaphoreType.DMA((2,))] + extra,
        compiler_params=pltpu.CompilerParams(vmem_limit_bytes=limit),
        cost_estimate=pl.CostEstimate(
            flops=2 * slots * rhs_cols * block * block,
            bytes_accessed=slots * block * (block + 2 * rhs_cols) * 4,
            transcendentals=0,
        ),
        name=name,
    )(*codes, *sources, own, other)


def first_sum(code, sources, own, other):
    one = sources[0].shape[2:]
    parts = sum(v.shape[0] for v in sources)
    each = sources[0].shape[1]
    store = jax.ShapeDtypeStruct((2048 // each, each) + one, jnp.bfloat16)
    extra = [
        pltpu.SemaphoreType.DMA((len(sources),)),
        pltpu.VMEM((parts, each) + one, jnp.bfloat16),
        pltpu.SemaphoreType.DMA,
    ]
    spaces = [pl.ANY] * len(sources)
    return sum_call(first_kernel, [code], sources, spaces, own, other, [store], [pltpu.HBM], extra, "first_sum", 60 * 1024 * 1024)


def old_sum(level, known, code, fresh, store, solved, own, other):
    one = store.shape[1:]
    outs = [
        jax.ShapeDtypeStruct((code.shape[1] + 1,), jnp.int32),
        jax.ShapeDtypeStruct((NEAR, one[1], one[1]), jnp.bfloat16),
    ]
    kernel = functools.partial(old_kernel, level, known)
    extra = [pltpu.VMEM((code.shape[1],) + one, jnp.bfloat16), pltpu.SemaphoreType.DMA]
    if solved:
        extra.append(pltpu.VMEM((sum(v.shape[0] for v in solved),) + one, jnp.bfloat16))
    spaces = [pl.ANY] + [pltpu.VMEM] * len(solved)
    out_spaces = [pltpu.SMEM, pltpu.VMEM]
    return sum_call(kernel, [code, fresh], [store] + solved, spaces, own, other, outs, out_spaces, extra, "old_sum", VMEM_LIMIT)


def fresh_kernel(level, list_ref, old_ref, x_ref, near_ref, own_ref, other_ref, out_ref, far, sem):
    per_row = own_ref.shape[2]
    out_ref[...] = old_ref[...]
    count = list_ref[0]

    def add(block, entry):
        row = ((entry & 1023) >= per_row).astype(jnp.int32)
        out_ref[row] += nt_dot(x_ref[entry >> 10], block)

    def add_near(n, carry):
        add(near_ref[n], list_ref[1 + n])
        return carry

    def add_far(n, carry):
        slot = list_ref[1 + n] & 1023

        @pl.when(slot < per_row)
        def _():
            pltpu.make_async_copy(own_ref.at[level - 1, 0, slot], far, sem).start()

        @pl.when(slot >= per_row)
        def _():
            pltpu.make_async_copy(other_ref.at[level - 1, 0, slot - per_row], far, sem).start()

        pltpu.make_async_copy(own_ref.at[level - 1, 0, 0], far, sem).wait()
        add(far[...], list_ref[1 + n])
        return carry

    lax.fori_loop(0, jnp.minimum(count, NEAR), add_near, 0)
    lax.fori_loop(NEAR, count, add_far, 0)


def fresh_sum(level, listed, solved, old, near, own, other):
    block = solved.shape[-1]
    vmem = pl.BlockSpec(memory_space=pltpu.VMEM)
    return pl.pallas_call(
        functools.partial(fresh_kernel, level),
        out_shape=jax.ShapeDtypeStruct(old.shape, jnp.float32),
        in_specs=[pl.BlockSpec(memory_space=pltpu.SMEM)] + [vmem] * 3 + [pl.BlockSpec(memory_space=pltpu.HBM)] * 2,
        out_specs=vmem,
        scratch_shapes=[
            pltpu.VMEM((block, block), jnp.bfloat16),
            pltpu.SemaphoreType.DMA,
        ],
        compiler_params=pltpu.CompilerParams(vmem_limit_bytes=VMEM_LIMIT),
        name="fresh_sum",
    )(listed, old, solved, near, own, other)


def solve_kernel(level, p0, p1, p2, p3, rhs_ref, own_d_ref, other_d_ref, out_ref, *refs):
    core = lax.axis_index("core")
    for r, d_ref in enumerate((own_d_ref, other_d_ref)):
        coupled = (p0[r] + p1[r]) + (p2[r] + p3[r])
        reduced = (rhs_ref[level, r].astype(jnp.float32) - coupled).astype(jnp.bfloat16)
        solved = nt_dot(reduced, d_ref[level, 0]).astype(jnp.bfloat16)
        out_ref[r] = solved
        if refs:
            for i in range(refs[1].shape[0]):
                refs[1][i, core ^ r] = solved
    if refs:
        all_ref, copies, sem = refs
        send = pltpu.make_async_copy(copies, all_ref, sem)
        send.start()
        send.wait()


def solve_level(level, partials, rhs, own_d, other_d, copies):
    _, rhs_cols, block = partials[0].shape
    vmem = pl.BlockSpec(memory_space=pltpu.VMEM)
    out_shape, out_specs, scratch = [jax.ShapeDtypeStruct((2, rhs_cols, block), jnp.bfloat16)], [vmem], []
    if copies:
        out_shape.append(jax.ShapeDtypeStruct((copies, 2, rhs_cols, block), jnp.bfloat16))
        out_specs.append(pl.BlockSpec(memory_space=pltpu.HBM))
        scratch = [pltpu.VMEM((copies, 2, rhs_cols, block), jnp.bfloat16), pltpu.SemaphoreType.DMA]
    return pl.pallas_call(
        functools.partial(solve_kernel, level),
        out_shape=out_shape,
        in_specs=[vmem] * 7,
        out_specs=out_specs,
        scratch_shapes=scratch,
        compiler_params=pltpu.CompilerParams(vmem_limit_bytes=VMEM_LIMIT),
        name="solve_level",
    )(*partials, rhs, own_d, other_d)


def on_device(rhs, boundary, diag_inv, off_blocks, coupling, present):
    levels, _, rhs_cols, block = rhs.shape
    outer_each = boundary.shape[0]
    outer = outer_each * 32
    half = rhs_cols // 2
    z, y, core = lax.axis_index("z"), lax.axis_index("y"), lax.axis_index("core")

    def my_half(v, axis):
        return lax.dynamic_slice_in_dim(v, core * half, half, axis)

    def their_half(v, axis):
        return lax.dynamic_slice_in_dim(v, (1 - core) * half, half, axis)

    first = jnp.einsum("rb,ab->ra", rhs[0, 0], diag_inv[0, 0], preferred_element_type=jnp.float32).astype(jnp.bfloat16)
    known = jnp.concatenate([boundary, first[None]])
    known = jnp.stack([my_half(known, 1), their_half(known, 1)])
    code_own = (coupling + 1024 * present)[:, 0]
    code_both = jnp.stack([code_own, swap_cores(code_own)], axis=1)
    rhs_both = jnp.concatenate([my_half(rhs, 2), swap_cores(their_half(rhs, 2))], axis=1)
    diag_other = swap_cores(diag_inv)
    off_sent, known = lax.optimization_barrier((off_blocks, known))
    off_other = swap_cores(off_sent)

    pieces = gather_parts(known)

    keep, index = code_both >= 1024, code_both % 1024
    in_outer = index < outer
    row = jnp.where(in_outer, index // outer_each, index - outer)
    member = jnp.where(in_outer, index % outer_each, outer_each)
    src_z, src_y, src_core = row // 8, (row // 2) % 4, row % 2
    each = outer_each + 1
    away = jnp.where(src_core == 0, src_y - y, src_z - z) % 4
    part = jnp.where(away == 3, 1, jnp.where(away == 1, 2, jnp.where(away == 2, 3, 0))) * 4
    part = part + jnp.where(src_core == 0, src_z ^ z, src_y ^ y) + jnp.where(src_core == core, 0, 16)
    known_place = part * each + member
    level_of = jnp.maximum(index - outer, 0) // 32
    this = jnp.arange(levels - 1)[:, None, None]
    is_fresh = (level_of == this) & (level_of > 0)
    place_level = (index - outer) % 32
    old_code = jnp.where(level_of == 0, known_place, 32 * each + (level_of - 1) * 32 + place_level)
    old_code = jnp.where(keep & ~is_fresh, old_code, -1).reshape(levels - 1, -1)
    fresh_code = jnp.where(keep & is_fresh, place_level, -1).reshape(levels - 1, -1)

    own_rows, other_rows = [], []
    value, store = first_sum(old_code, pieces, off_blocks, off_other)
    store = store.reshape((-1,) + store.shape[2:])
    solved_levels = []
    for level in range(1, levels):
        partials = [value] + [lax.ppermute(value, "x", xor_pairs(4, k)) for k in (1, 2, 3)]
        last = level == levels - 1
        outs = solve_level(level, partials, rhs_both, diag_inv, diag_other, 0 if last else 16)
        own_rows.append(outs[0][0])
        other_rows.append(outs[0][1])
        if not last:
            next_fresh, sent = lax.optimization_barrier((fresh_code, outs[1]))
            solved = lax.all_to_all(sent, ("z", "y"), 0, 0).reshape(32, half, block)
            old, listed, near = old_sum(
                level + 1, 32 * each, old_code, next_fresh, store, solved_levels, off_blocks, off_other
            )
            value = fresh_sum(level + 1, listed, solved, old, near, off_blocks, off_other)
            solved_levels = solved_levels + [solved]

    mine = jnp.stack(own_rows)
    theirs = swap_cores(jnp.stack(other_rows))
    low = jnp.where(core == 0, mine, theirs)
    high = jnp.where(core == 0, theirs, mine)
    rest = jnp.concatenate([low, high], axis=1)
    return jnp.concatenate([first[None], rest])[:, None]


def solution(mesh):
    split = Mesh(mesh.devices.reshape(4, 4, 2, 4), ("z", "y", "core", "x"))
    in_specs = (
        P(None, ROWS, None, None),
        P(ROWS, None, None),
        P(None, ROWS, None, None),
        P(None, ROWS, "x", None, None),
        P(None, ROWS, "x"),
        P(None, ROWS, "x"),
    )
    return jax.shard_map(
        on_device, mesh=split, in_specs=in_specs, out_specs=P(None, ROWS, None, None), check_vma=False
    )
```

```python
import functools

import jax
import jax.numpy as jnp
from jax import lax
from jax.experimental import pallas as pl
from jax.experimental.pallas import tpu as pltpu
from jax.sharding import Mesh, PartitionSpec as P

ROWS = ("z", "y", "core")
VMEM_LIMIT = 48 * 1024 * 1024


def xor_pairs(n, k):
    return [(i, i ^ k) for i in range(n)]


def shift_pairs(n, k):
    return [(i, (i + k) % n) for i in range(n)]


def swap_cores(v):
    return lax.ppermute(v, "core", xor_pairs(2, 1))


def pairs(stage, move, cross=False):
    result = []
    for z in range(4):
        for y in range(4):
            for core in range(2):
                to_z, to_y = (move(z), y) if core + 1 == stage else (z, move(y))
                to_core = 1 - core if cross else core
                result.append(((z * 4 + y) * 2 + core, (to_z * 4 + to_y) * 2 + to_core))
    return result


def gather_near(v):
    return [v] + [lax.ppermute(v, ROWS, pairs(1, lambda i, k=k: i ^ k)) for k in (1, 2, 3)]


def gather_parts(near):
    after_one, before_one = lambda i: (i + 1) % 4, lambda i: (i + 3) % 4
    mine, theirs = jnp.stack([one[0] for one in near]), jnp.stack([one[1] for one in near])

    def spread(part, cross):
        again = 1 if cross else 2
        before = lax.ppermute(part, ROWS, pairs(2, after_one, cross))
        after = lax.ppermute(part, ROWS, pairs(2, before_one, cross))
        far_low = lax.ppermute(before[:2], ROWS, pairs(again, after_one))
        far_high = lax.ppermute(after[2:], ROWS, pairs(again, before_one))
        return [before, after, far_low, far_high]

    return [mine, *spread(mine, False), swap_cores(theirs), *spread(theirs, True)]


def nt_dot(x, a):
    return lax.dot_general(x, a, (((1,), (1,)), ((), ())), preferred_element_type=jnp.float32)


GROUP = 8
NEAR = 16


def gather_sum(level, code_ref, picks, known, solved_ref, own_ref, other_ref, out_ref, blocks, block_sems, between):
    slots = code_ref.shape[1]
    per_row = slots // 2
    loads = [
        pltpu.make_async_copy(a_ref.at[level - 1, 0], blocks.at[pl.ds(r * per_row, per_row)], block_sems.at[r])
        for r, a_ref in enumerate((own_ref, other_ref))
    ]
    for load in loads:
        load.start()
    between()
    for r in range(2):
        loads[r].wait()
        total = None
        for g in range(r * per_row, (r + 1) * per_row, GROUP):
            xs, group = [], []
            for k in range(g, g + GROUP):
                code = code_ref[level - 1, k]
                kept = (code >= 0).astype(jnp.float32)
                picked = picks(k, jnp.clip(code, 0, known - 1))
                if solved_ref is not None:
                    picked = jnp.where(code >= known, solved_ref[jnp.maximum(code - known, 0)], picked)
                xs.append((picked.astype(jnp.float32) * kept).astype(jnp.bfloat16))
                group.append(blocks[k])
            part = nt_dot(jnp.concatenate(xs, axis=1), jnp.concatenate(group, axis=1))
            total = part if total is None else total + part
        out_ref[r] = total


def first_kernel(code_ref, *refs):
    sources, refs = refs[:-9], refs[-9:]
    own_ref, other_ref, out_ref, store_ref, blocks, block_sems, pack_sems, packed, store_sems = refs
    packs, keeps, start = [], [], 0
    for i, source in enumerate(sources):
        target = packed.at[pl.ds(start, source.shape[0])]
        packs.append(pltpu.make_async_copy(source, target, pack_sems.at[i]))
        keeps.append(pltpu.make_async_copy(target, store_ref.at[pl.ds(start, source.shape[0])], store_sems.at[i]))
        start += source.shape[0]

    def between():
        for pack in packs:
            pack.start()
        for pack, keep in zip(packs, keeps):
            pack.wait()
            keep.start()

    each = packed.shape[1]
    picks = lambda k, code: packed[code // each, code % each]
    gather_sum(1, code_ref, picks, start * each, None, own_ref, other_ref, out_ref, blocks, block_sems, between)
    for keep in keeps:
        keep.wait()


def old_kernel(level, known, code_ref, fresh_ref, store_ref, *refs):
    solved, refs = refs[: level - 2], refs[level - 2 :]
    own_ref, other_ref, out_ref, list_ref, near_ref, blocks, block_sems, picked, pick_sem = refs[:9]
    solved_ref = refs[9] if solved else None
    slots = code_ref.shape[1]

    def between():
        for k in range(slots):
            place = jnp.clip(code_ref[level - 1, k], 0, known - 1)
            pltpu.make_async_copy(store_ref.at[place], picked.at[k], pick_sem).start()
        for i, one in enumerate(solved):
            solved_ref[i * one.shape[0] : (i + 1) * one.shape[0]] = one[...]
        pltpu.make_async_copy(store_ref.at[pl.ds(0, slots)], picked, pick_sem).wait()

    picks = lambda k, code: picked[k]
    gather_sum(level, code_ref, picks, known, solved_ref, own_ref, other_ref, out_ref, blocks, block_sems, between)

    def note(slot, count):
        code = fresh_ref[level - 1, slot]

        @pl.when(code >= 0)
        def _():
            list_ref[1 + count] = code * 1024 + slot

        @pl.when((code >= 0) & (count < NEAR))
        def _():
            near_ref[count] = blocks[slot]

        return count + (code >= 0).astype(jnp.int32)

    list_ref[0] = lax.fori_loop(0, fresh_ref.shape[1], note, jnp.int32(0))


def sum_call(kernel, codes, sources, source_spaces, own, other, outs, out_spaces, extra, name, limit):
    slots, (rhs_cols, block) = codes[0].shape[1], sources[0].shape[-2:]
    return pl.pallas_call(
        kernel,
        out_shape=[jax.ShapeDtypeStruct((2, rhs_cols, block), jnp.float32)] + outs,
        in_specs=[pl.BlockSpec(memory_space=pltpu.SMEM)] * len(codes)
        + [pl.BlockSpec(memory_space=space) for space in source_spaces]
        + [pl.BlockSpec(memory_space=pltpu.HBM)] * 2,
        out_specs=[pl.BlockSpec(memory_space=space) for space in [pltpu.VMEM] + out_spaces],
        scratch_shapes=[pltpu.VMEM((slots, block, block), jnp.bfloat16), pltpu.SemaphoreType.DMA((2,))] + extra,
        compiler_params=pltpu.CompilerParams(vmem_limit_bytes=limit),
        cost_estimate=pl.CostEstimate(
            flops=2 * slots * rhs_cols * block * block,
            bytes_accessed=slots * block * (block + 2 * rhs_cols) * 4,
            transcendentals=0,
        ),
        name=name,
    )(*codes, *sources, own, other)


def first_sum(code, sources, own, other):
    one = sources[0].shape[2:]
    parts = sum(v.shape[0] for v in sources)
    each = sources[0].shape[1]
    store = jax.ShapeDtypeStruct((2048 // each, each) + one, jnp.bfloat16)
    extra = [
        pltpu.SemaphoreType.DMA((len(sources),)),
        pltpu.VMEM((parts, each) + one, jnp.bfloat16),
        pltpu.SemaphoreType.DMA((len(sources),)),
    ]
    spaces = [pl.ANY] * len(sources)
    return sum_call(first_kernel, [code], sources, spaces, own, other, [store], [pltpu.HBM], extra, "first_sum", 54 * 1024 * 1024)


def old_sum(level, known, code, fresh, store, solved, own, other):
    one = store.shape[1:]
    outs = [
        jax.ShapeDtypeStruct((code.shape[1] + 1,), jnp.int32),
        jax.ShapeDtypeStruct((NEAR, one[1], one[1]), jnp.bfloat16),
    ]
    kernel = functools.partial(old_kernel, level, known)
    extra = [pltpu.VMEM((code.shape[1],) + one, jnp.bfloat16), pltpu.SemaphoreType.DMA]
    if solved:
        extra.append(pltpu.VMEM((sum(v.shape[0] for v in solved),) + one, jnp.bfloat16))
    spaces = [pl.ANY] + [pltpu.VMEM] * len(solved)
    out_spaces = [pltpu.SMEM, pltpu.VMEM]
    return sum_call(kernel, [code, fresh], [store] + solved, spaces, own, other, outs, out_spaces, extra, "old_sum", VMEM_LIMIT)


def fresh_kernel(level, list_ref, old_ref, x_ref, near_ref, own_ref, other_ref, out_ref, far, sem):
    per_row = own_ref.shape[2]
    out_ref[...] = old_ref[...]
    count = list_ref[0]

    def add(block, entry):
        row = ((entry & 1023) >= per_row).astype(jnp.int32)
        out_ref[row] += nt_dot(x_ref[entry >> 10], block)

    def add_near(n, carry):
        add(near_ref[n], list_ref[1 + n])
        return carry

    def add_far(n, carry):
        slot = list_ref[1 + n] & 1023

        @pl.when(slot < per_row)
        def _():
            pltpu.make_async_copy(own_ref.at[level - 1, 0, slot], far, sem).start()

        @pl.when(slot >= per_row)
        def _():
            pltpu.make_async_copy(other_ref.at[level - 1, 0, slot - per_row], far, sem).start()

        pltpu.make_async_copy(own_ref.at[level - 1, 0, 0], far, sem).wait()
        add(far[...], list_ref[1 + n])
        return carry

    lax.fori_loop(0, jnp.minimum(count, NEAR), add_near, 0)
    lax.fori_loop(NEAR, count, add_far, 0)


def fresh_sum(level, listed, solved, old, near, own, other):
    block = solved.shape[-1]
    vmem = pl.BlockSpec(memory_space=pltpu.VMEM)
    return pl.pallas_call(
        functools.partial(fresh_kernel, level),
        out_shape=jax.ShapeDtypeStruct(old.shape, jnp.float32),
        in_specs=[pl.BlockSpec(memory_space=pltpu.SMEM)] + [vmem] * 3 + [pl.BlockSpec(memory_space=pltpu.HBM)] * 2,
        out_specs=vmem,
        scratch_shapes=[
            pltpu.VMEM((block, block), jnp.bfloat16),
            pltpu.SemaphoreType.DMA,
        ],
        compiler_params=pltpu.CompilerParams(vmem_limit_bytes=VMEM_LIMIT),
        name="fresh_sum",
    )(listed, old, solved, near, own, other)


def solve_kernel(level, p0, p1, p2, p3, rhs_ref, own_d_ref, other_d_ref, out_ref, *refs):
    core = lax.axis_index("core")
    for r, d_ref in enumerate((own_d_ref, other_d_ref)):
        coupled = (p0[r] + p1[r]) + (p2[r] + p3[r])
        reduced = (rhs_ref[level, r].astype(jnp.float32) - coupled).astype(jnp.bfloat16)
        solved = nt_dot(reduced, d_ref[level, 0]).astype(jnp.bfloat16)
        out_ref[r] = solved
        if refs:
            for i in range(refs[1].shape[0]):
                refs[1][i, core ^ r] = solved
    if refs:
        all_ref, copies, sem = refs
        send = pltpu.make_async_copy(copies, all_ref, sem)
        send.start()
        send.wait()


def solve_level(level, partials, rhs, own_d, other_d, copies):
    _, rhs_cols, block = partials[0].shape
    vmem = pl.BlockSpec(memory_space=pltpu.VMEM)
    out_shape, out_specs, scratch = [jax.ShapeDtypeStruct((2, rhs_cols, block), jnp.bfloat16)], [vmem], []
    if copies:
        out_shape.append(jax.ShapeDtypeStruct((copies, 2, rhs_cols, block), jnp.bfloat16))
        out_specs.append(pl.BlockSpec(memory_space=pltpu.HBM))
        scratch = [pltpu.VMEM((copies, 2, rhs_cols, block), jnp.bfloat16), pltpu.SemaphoreType.DMA]
    return pl.pallas_call(
        functools.partial(solve_kernel, level),
        out_shape=out_shape,
        in_specs=[vmem] * 7,
        out_specs=out_specs,
        scratch_shapes=scratch,
        compiler_params=pltpu.CompilerParams(vmem_limit_bytes=VMEM_LIMIT),
        name="solve_level",
    )(*partials, rhs, own_d, other_d)


def on_device(rhs, boundary, diag_inv, off_blocks, coupling, present):
    levels, _, rhs_cols, block = rhs.shape
    outer_each = boundary.shape[0]
    outer = outer_each * 32
    half = rhs_cols // 2
    z, y, core = lax.axis_index("z"), lax.axis_index("y"), lax.axis_index("core")

    def my_half(v, axis):
        return lax.dynamic_slice_in_dim(v, core * half, half, axis)

    def their_half(v, axis):
        return lax.dynamic_slice_in_dim(v, (1 - core) * half, half, axis)

    first = jnp.einsum("rb,ab->ra", rhs[0, 0], diag_inv[0, 0], preferred_element_type=jnp.float32).astype(jnp.bfloat16)
    known = jnp.concatenate([boundary, first[None]])
    known = jnp.stack([my_half(known, 1), their_half(known, 1)])
    code_own = (coupling + 1024 * present)[:, 0]
    code_both = jnp.stack([code_own, swap_cores(code_own)], axis=1)
    rhs_both = jnp.concatenate([my_half(rhs, 2), swap_cores(their_half(rhs, 2))], axis=1)
    diag_other = swap_cores(diag_inv)
    off_sent, known = lax.optimization_barrier((off_blocks, known))
    off_other = swap_cores(off_sent)

    near_known = gather_near(known)

    keep, index = code_both >= 1024, code_both % 1024
    in_outer = index < outer
    row = jnp.where(in_outer, index // outer_each, index - outer)
    member = jnp.where(in_outer, index % outer_each, outer_each)
    src_z, src_y, src_core = row // 8, (row // 2) % 4, row % 2
    each = outer_each + 1
    away = jnp.where(src_core == 0, src_y - y, src_z - z) % 4
    part = jnp.where(away == 3, 1, jnp.where(away == 1, 2, jnp.where(away == 2, 3, 0))) * 4
    part = part + jnp.where(src_core == 0, src_z ^ z, src_y ^ y) + jnp.where(src_core == core, 0, 16)
    known_place = part * each + member
    level_of = jnp.maximum(index - outer, 0) // 32
    this = jnp.arange(levels - 1)[:, None, None]
    is_fresh = (level_of == this) & (level_of > 0)
    place_level = (index - outer) % 32
    old_code = jnp.where(level_of == 0, known_place, 32 * each + (level_of - 1) * 32 + place_level)
    old_code = jnp.where(keep & ~is_fresh, old_code, -1).reshape(levels - 1, -1)
    fresh_code = jnp.where(keep & is_fresh, place_level, -1).reshape(levels - 1, -1)

    own_rows, other_rows = [], []
    near_known, rhs_both, old_code, fresh_code = lax.optimization_barrier((near_known, rhs_both, old_code, fresh_code))
    pieces = gather_parts(near_known)
    value, store = first_sum(old_code, pieces, off_blocks, off_other)
    store = store.reshape((-1,) + store.shape[2:])
    solved_levels = []
    for level in range(1, levels):
        partials = [value] + [lax.ppermute(value, "x", xor_pairs(4, k)) for k in (1, 2, 3)]
        last = level == levels - 1
        outs = solve_level(level, partials, rhs_both, diag_inv, diag_other, 0 if last else 16)
        own_rows.append(outs[0][0])
        other_rows.append(outs[0][1])
        if not last:
            next_fresh, sent = lax.optimization_barrier((fresh_code, outs[1]))
            solved = lax.all_to_all(sent, ("z", "y"), 0, 0).reshape(32, half, block)
            old, listed, near = old_sum(
                level + 1, 32 * each, old_code, next_fresh, store, solved_levels, off_blocks, off_other
            )
            value = fresh_sum(level + 1, listed, solved, old, near, off_blocks, off_other)
            solved_levels = solved_levels + [solved]

    mine = jnp.stack(own_rows)
    theirs = swap_cores(jnp.stack(other_rows))
    low = jnp.where(core == 0, mine, theirs)
    high = jnp.where(core == 0, theirs, mine)
    rest = jnp.concatenate([low, high], axis=1)
    return jnp.concatenate([first[None], rest])[:, None]


def solution(mesh):
    split = Mesh(mesh.devices.reshape(4, 4, 2, 4), ("z", "y", "core", "x"))
    in_specs = (
        P(None, ROWS, None, None),
        P(ROWS, None, None),
        P(None, ROWS, None, None),
        P(None, ROWS, "x", None, None),
        P(None, ROWS, "x"),
        P(None, ROWS, "x"),
    )
    return jax.shard_map(
        on_device, mesh=split, in_specs=in_specs, out_specs=P(None, ROWS, None, None), check_vma=False
    )
```

```python
import functools

import jax
import jax.numpy as jnp
from jax import lax
from jax.experimental import pallas as pl
from jax.experimental.pallas import tpu as pltpu
from jax.sharding import Mesh, PartitionSpec as P

ROWS = ("z", "y", "core")
VMEM_LIMIT = 48 * 1024 * 1024


def xor_pairs(n, k):
    return [(i, i ^ k) for i in range(n)]


def shift_pairs(n, k):
    return [(i, (i + k) % n) for i in range(n)]


def swap_cores(v):
    return lax.ppermute(v, "core", xor_pairs(2, 1))


def pairs(stage, move, cross=False):
    result = []
    for z in range(4):
        for y in range(4):
            for core in range(2):
                to_z, to_y = (move(z), y) if core + 1 == stage else (z, move(y))
                to_core = 1 - core if cross else core
                result.append(((z * 4 + y) * 2 + core, (to_z * 4 + to_y) * 2 + to_core))
    return result


def gather_parts(v):
    after_one, before_one = lambda i: (i + 1) % 4, lambda i: (i + 3) % 4
    near = [v] + [lax.ppermute(v, ROWS, pairs(1, lambda i, k=k: i ^ k)) for k in (1, 2, 3)]
    mine, theirs = jnp.stack([one[0] for one in near]), jnp.stack([one[1] for one in near])

    def spread(part, cross):
        again = 1 if cross else 2
        before = lax.ppermute(part, ROWS, pairs(2, after_one, cross))
        after = lax.ppermute(part, ROWS, pairs(2, before_one, cross))
        far_low = lax.ppermute(before[:2], ROWS, pairs(again, after_one))
        far_high = lax.ppermute(after[2:], ROWS, pairs(again, before_one))
        return [before, after, far_low, far_high]

    return [mine, *spread(mine, False), swap_cores(theirs), *spread(theirs, True)]


def nt_dot(x, a):
    return lax.dot_general(x, a, (((1,), (1,)), ((), ())), preferred_element_type=jnp.float32)


GROUP = 8
NEAR = 16


def gather_sum(level, code_ref, picks, known, solved_ref, own_ref, other_ref, out_ref, blocks, block_sems, between):
    slots = code_ref.shape[1]
    per_row = slots // 2
    loads = [
        pltpu.make_async_copy(a_ref.at[level - 1, 0], blocks.at[pl.ds(r * per_row, per_row)], block_sems.at[r])
        for r, a_ref in enumerate((own_ref, other_ref))
    ]
    for load in loads:
        load.start()
    between()
    for r in range(2):
        loads[r].wait()
        total = None
        for g in range(r * per_row, (r + 1) * per_row, GROUP):
            xs, group = [], []
            for k in range(g, g + GROUP):
                code = code_ref[level - 1, k]
                kept = (code >= 0).astype(jnp.float32)
                picked = picks(k, jnp.clip(code, 0, known - 1))
                if solved_ref is not None:
                    picked = jnp.where(code >= known, solved_ref[jnp.maximum(code - known, 0)], picked)
                xs.append((picked.astype(jnp.float32) * kept).astype(jnp.bfloat16))
                group.append(blocks[k])
            part = nt_dot(jnp.concatenate(xs, axis=1), jnp.concatenate(group, axis=1))
            total = part if total is None else total + part
        out_ref[r] = total


def first_kernel(code_ref, *refs):
    sources, refs = refs[:-7], refs[-7:]
    own_ref, other_ref, out_ref, store_ref, blocks, block_sems, store_sems = refs
    keeps, starts, known = [], [], 0
    for i, source in enumerate(sources):
        target = store_ref.at[pl.ds(known, source.shape[0])]
        keeps.append(pltpu.make_async_copy(source, target, store_sems.at[i]))
        starts.append(known)
        known += source.shape[0]

    def between():
        for keep in keeps:
            keep.start()

    def picks(k, code):
        value = None
        for start, source in zip(starts, sources):
            one = source[jnp.clip(code - start, 0, source.shape[0] - 1)]
            value = one if value is None else jnp.where(code >= start, one, value)
        return value

    gather_sum(1, code_ref, picks, known, None, own_ref, other_ref, out_ref, blocks, block_sems, between)
    for keep in keeps:
        keep.wait()


def old_kernel(level, known, code_ref, fresh_ref, store_ref, *refs):
    solved, refs = refs[: level - 2], refs[level - 2 :]
    own_ref, other_ref, out_ref, list_ref, near_ref, blocks, block_sems, picked, pick_sem = refs[:9]
    solved_ref = refs[9] if solved else None
    slots = code_ref.shape[1]

    def between():
        for k in range(slots):
            place = jnp.clip(code_ref[level - 1, k], 0, known - 1)
            pltpu.make_async_copy(store_ref.at[place], picked.at[k], pick_sem).start()
        for i, one in enumerate(solved):
            solved_ref[i * one.shape[0] : (i + 1) * one.shape[0]] = one[...]
        pltpu.make_async_copy(store_ref.at[pl.ds(0, slots)], picked, pick_sem).wait()

    picks = lambda k, code: picked[k]
    gather_sum(level, code_ref, picks, known, solved_ref, own_ref, other_ref, out_ref, blocks, block_sems, between)

    def note(slot, count):
        code = fresh_ref[level - 1, slot]

        @pl.when(code >= 0)
        def _():
            list_ref[1 + count] = code * 1024 + slot

        @pl.when((code >= 0) & (count < NEAR))
        def _():
            near_ref[count] = blocks[slot]

        return count + (code >= 0).astype(jnp.int32)

    list_ref[0] = lax.fori_loop(0, fresh_ref.shape[1], note, jnp.int32(0))


def sum_call(kernel, codes, sources, source_spaces, own, other, outs, out_spaces, extra, name, limit):
    slots, (rhs_cols, block) = codes[0].shape[1], sources[0].shape[-2:]
    return pl.pallas_call(
        kernel,
        out_shape=[jax.ShapeDtypeStruct((2, rhs_cols, block), jnp.float32)] + outs,
        in_specs=[pl.BlockSpec(memory_space=pltpu.SMEM)] * len(codes)
        + [pl.BlockSpec(memory_space=space) for space in source_spaces]
        + [pl.BlockSpec(memory_space=pltpu.HBM)] * 2,
        out_specs=[pl.BlockSpec(memory_space=space) for space in [pltpu.VMEM] + out_spaces],
        scratch_shapes=[pltpu.VMEM((slots, block, block), jnp.bfloat16), pltpu.SemaphoreType.DMA((2,))] + extra,
        compiler_params=pltpu.CompilerParams(vmem_limit_bytes=limit),
        cost_estimate=pl.CostEstimate(
            flops=2 * slots * rhs_cols * block * block,
            bytes_accessed=slots * block * (block + 2 * rhs_cols) * 4,
            transcendentals=0,
        ),
        name=name,
    )(*codes, *sources, own, other)


def first_sum(code, sources, own, other):
    store = jax.ShapeDtypeStruct((2048,) + sources[0].shape[1:], jnp.bfloat16)
    extra = [pltpu.SemaphoreType.DMA((len(sources),))]
    spaces = [pltpu.VMEM] * len(sources)
    return sum_call(first_kernel, [code], sources, spaces, own, other, [store], [pltpu.HBM], extra, "first_sum", VMEM_LIMIT)


def old_sum(level, known, code, fresh, store, solved, own, other):
    one = store.shape[1:]
    outs = [
        jax.ShapeDtypeStruct((code.shape[1] + 1,), jnp.int32),
        jax.ShapeDtypeStruct((NEAR, one[1], one[1]), jnp.bfloat16),
    ]
    kernel = functools.partial(old_kernel, level, known)
    extra = [pltpu.VMEM((code.shape[1],) + one, jnp.bfloat16), pltpu.SemaphoreType.DMA]
    if solved:
        extra.append(pltpu.VMEM((sum(v.shape[0] for v in solved),) + one, jnp.bfloat16))
    spaces = [pl.ANY] + [pltpu.VMEM] * len(solved)
    out_spaces = [pltpu.SMEM, pltpu.VMEM]
    return sum_call(kernel, [code, fresh], [store] + solved, spaces, own, other, outs, out_spaces, extra, "old_sum", VMEM_LIMIT)


def fresh_kernel(level, list_ref, old_ref, x_ref, near_ref, own_ref, other_ref, out_ref, far, sem):
    per_row = own_ref.shape[2]
    out_ref[...] = old_ref[...]
    count = list_ref[0]

    def add(block, entry):
        row = ((entry & 1023) >= per_row).astype(jnp.int32)
        out_ref[row] += nt_dot(x_ref[entry >> 10], block)

    def add_near(n, carry):
        add(near_ref[n], list_ref[1 + n])
        return carry

    def add_far(n, carry):
        slot = list_ref[1 + n] & 1023

        @pl.when(slot < per_row)
        def _():
            pltpu.make_async_copy(own_ref.at[level - 1, 0, slot], far, sem).start()

        @pl.when(slot >= per_row)
        def _():
            pltpu.make_async_copy(other_ref.at[level - 1, 0, slot - per_row], far, sem).start()

        pltpu.make_async_copy(own_ref.at[level - 1, 0, 0], far, sem).wait()
        add(far[...], list_ref[1 + n])
        return carry

    lax.fori_loop(0, jnp.minimum(count, NEAR), add_near, 0)
    lax.fori_loop(NEAR, count, add_far, 0)


def fresh_sum(level, listed, solved, old, near, own, other):
    block = solved.shape[-1]
    vmem = pl.BlockSpec(memory_space=pltpu.VMEM)
    return pl.pallas_call(
        functools.partial(fresh_kernel, level),
        out_shape=jax.ShapeDtypeStruct(old.shape, jnp.float32),
        in_specs=[pl.BlockSpec(memory_space=pltpu.SMEM)] + [vmem] * 3 + [pl.BlockSpec(memory_space=pltpu.HBM)] * 2,
        out_specs=vmem,
        scratch_shapes=[
            pltpu.VMEM((block, block), jnp.bfloat16),
            pltpu.SemaphoreType.DMA,
        ],
        compiler_params=pltpu.CompilerParams(vmem_limit_bytes=VMEM_LIMIT),
        name="fresh_sum",
    )(listed, old, solved, near, own, other)


def solve_kernel(level, p0, p1, p2, p3, rhs_ref, own_d_ref, other_d_ref, out_ref, *refs):
    core = lax.axis_index("core")
    for r, d_ref in enumerate((own_d_ref, other_d_ref)):
        coupled = (p0[r] + p1[r]) + (p2[r] + p3[r])
        reduced = (rhs_ref[level, r].astype(jnp.float32) - coupled).astype(jnp.bfloat16)
        solved = nt_dot(reduced, d_ref[level, 0]).astype(jnp.bfloat16)
        out_ref[r] = solved
        if refs:
            for i in range(refs[1].shape[0]):
                refs[1][i, core ^ r] = solved
    if refs:
        all_ref, copies, sem = refs
        send = pltpu.make_async_copy(copies, all_ref, sem)
        send.start()
        send.wait()


def solve_level(level, partials, rhs, own_d, other_d, copies):
    _, rhs_cols, block = partials[0].shape
    vmem = pl.BlockSpec(memory_space=pltpu.VMEM)
    out_shape, out_specs, scratch = [jax.ShapeDtypeStruct((2, rhs_cols, block), jnp.bfloat16)], [vmem], []
    if copies:
        out_shape.append(jax.ShapeDtypeStruct((copies, 2, rhs_cols, block), jnp.bfloat16))
        out_specs.append(pl.BlockSpec(memory_space=pltpu.HBM))
        scratch = [pltpu.VMEM((copies, 2, rhs_cols, block), jnp.bfloat16), pltpu.SemaphoreType.DMA]
    return pl.pallas_call(
        functools.partial(solve_kernel, level),
        out_shape=out_shape,
        in_specs=[vmem] * 7,
        out_specs=out_specs,
        scratch_shapes=scratch,
        compiler_params=pltpu.CompilerParams(vmem_limit_bytes=VMEM_LIMIT),
        name="solve_level",
    )(*partials, rhs, own_d, other_d)


def on_device(rhs, boundary, diag_inv, off_blocks, coupling, present):
    levels, _, rhs_cols, block = rhs.shape
    outer_each = boundary.shape[0]
    outer = outer_each * 32
    half = rhs_cols // 2
    z, y, core = lax.axis_index("z"), lax.axis_index("y"), lax.axis_index("core")

    def my_half(v, axis):
        return lax.dynamic_slice_in_dim(v, core * half, half, axis)

    def their_half(v, axis):
        return lax.dynamic_slice_in_dim(v, (1 - core) * half, half, axis)

    first = jnp.einsum("rb,ab->ra", rhs[0, 0], diag_inv[0, 0], preferred_element_type=jnp.float32).astype(jnp.bfloat16)
    known = jnp.concatenate([boundary, first[None]])
    known = jnp.stack([my_half(known, 1), their_half(known, 1)])
    code_own = (coupling + 1024 * present)[:, 0]
    code_both = jnp.stack([code_own, swap_cores(code_own)], axis=1)
    rhs_both = jnp.concatenate([my_half(rhs, 2), swap_cores(their_half(rhs, 2))], axis=1)
    diag_other = swap_cores(diag_inv)
    off_sent, known = lax.optimization_barrier((off_blocks, known))
    off_other = swap_cores(off_sent)

    pieces = [piece.reshape((-1,) + piece.shape[2:]) for piece in gather_parts(known)]

    keep, index = code_both >= 1024, code_both % 1024
    in_outer = index < outer
    row = jnp.where(in_outer, index // outer_each, index - outer)
    member = jnp.where(in_outer, index % outer_each, outer_each)
    src_z, src_y, src_core = row // 8, (row // 2) % 4, row % 2
    each = outer_each + 1
    away = jnp.where(src_core == 0, src_y - y, src_z - z) % 4
    part = jnp.where(away == 3, 1, jnp.where(away == 1, 2, jnp.where(away == 2, 3, 0))) * 4
    part = part + jnp.where(src_core == 0, src_z ^ z, src_y ^ y) + jnp.where(src_core == core, 0, 16)
    known_place = part * each + member
    level_of = jnp.maximum(index - outer, 0) // 32
    this = jnp.arange(levels - 1)[:, None, None]
    is_fresh = (level_of == this) & (level_of > 0)
    place_level = (index - outer) % 32
    old_code = jnp.where(level_of == 0, known_place, 32 * each + (level_of - 1) * 32 + place_level)
    old_code = jnp.where(keep & ~is_fresh, old_code, -1).reshape(levels - 1, -1)
    fresh_code = jnp.where(keep & is_fresh, place_level, -1).reshape(levels - 1, -1)

    own_rows, other_rows = [], []
    value, store = first_sum(old_code, pieces, off_blocks, off_other)
    solved_levels = []
    for level in range(1, levels):
        partials = [value] + [lax.ppermute(value, "x", xor_pairs(4, k)) for k in (1, 2, 3)]
        last = level == levels - 1
        outs = solve_level(level, partials, rhs_both, diag_inv, diag_other, 0 if last else 16)
        own_rows.append(outs[0][0])
        other_rows.append(outs[0][1])
        if not last:
            next_fresh, sent = lax.optimization_barrier((fresh_code, outs[1]))
            solved = lax.all_to_all(sent, ("z", "y"), 0, 0).reshape(32, half, block)
            old, listed, near = old_sum(
                level + 1, 32 * each, old_code, next_fresh, store, solved_levels, off_blocks, off_other
            )
            value = fresh_sum(level + 1, listed, solved, old, near, off_blocks, off_other)
            solved_levels = solved_levels + [solved]

    mine = jnp.stack(own_rows)
    theirs = swap_cores(jnp.stack(other_rows))
    low = jnp.where(core == 0, mine, theirs)
    high = jnp.where(core == 0, theirs, mine)
    rest = jnp.concatenate([low, high], axis=1)
    return jnp.concatenate([first[None], rest])[:, None]


def solution(mesh):
    split = Mesh(mesh.devices.reshape(4, 4, 2, 4), ("z", "y", "core", "x"))
    in_specs = (
        P(None, ROWS, None, None),
        P(ROWS, None, None),
        P(None, ROWS, None, None),
        P(None, ROWS, "x", None, None),
        P(None, ROWS, "x"),
        P(None, ROWS, "x"),
    )
    return jax.shard_map(
        on_device, mesh=split, in_specs=in_specs, out_specs=P(None, ROWS, None, None), check_vma=False
    )
```

```python
import functools

import jax
import jax.numpy as jnp
from jax import lax
from jax.experimental import pallas as pl
from jax.experimental.pallas import tpu as pltpu
from jax.sharding import Mesh, PartitionSpec as P

ROWS = ("z", "y", "core")
VMEM_LIMIT = 48 * 1024 * 1024


def xor_pairs(n, k):
    return [(i, i ^ k) for i in range(n)]


def shift_pairs(n, k):
    return [(i, (i + k) % n) for i in range(n)]


def swap_cores(v):
    return lax.ppermute(v, "core", xor_pairs(2, 1))


def pairs(stage, move, cross=False):
    result = []
    for z in range(4):
        for y in range(4):
            for core in range(2):
                to_z, to_y = (move(z), y) if core + 1 == stage else (z, move(y))
                to_core = 1 - core if cross else core
                result.append(((z * 4 + y) * 2 + core, (to_z * 4 + to_y) * 2 + to_core))
    return result


def gather_parts(v):
    after_one, before_one = lambda i: (i + 1) % 4, lambda i: (i + 3) % 4
    near = [v] + [lax.ppermute(v, ROWS, pairs(1, lambda i, k=k: i ^ k)) for k in (1, 2, 3)]
    mine, theirs = jnp.stack([one[0] for one in near]), jnp.stack([one[1] for one in near])

    def spread(part, cross):
        again = 1 if cross else 2
        before = lax.ppermute(part, ROWS, pairs(2, after_one, cross))
        after = lax.ppermute(part, ROWS, pairs(2, before_one, cross))
        far_low = lax.ppermute(before[:2], ROWS, pairs(again, after_one))
        far_high = lax.ppermute(after[2:], ROWS, pairs(again, before_one))
        return [before, after, far_low, far_high]

    return [mine, *spread(mine, False), swap_cores(theirs), *spread(theirs, True)]


def nt_dot(x, a):
    return lax.dot_general(x, a, (((1,), (1,)), ((), ())), preferred_element_type=jnp.float32)


GROUP = 8
NEAR = 16


def gather_sum(level, code_ref, picks, known, solved_ref, own_ref, other_ref, out_ref, blocks, block_sems, between):
    slots = code_ref.shape[1]
    per_row = slots // 2
    loads = [
        pltpu.make_async_copy(a_ref.at[level - 1, 0], blocks.at[pl.ds(r * per_row, per_row)], block_sems.at[r])
        for r, a_ref in enumerate((own_ref, other_ref))
    ]
    for load in loads:
        load.start()
    between()
    for r in range(2):
        loads[r].wait()
        total = None
        for g in range(r * per_row, (r + 1) * per_row, GROUP):
            xs, group = [], []
            for k in range(g, g + GROUP):
                code = code_ref[level - 1, k]
                kept = (code >= 0).astype(jnp.float32)
                picked = picks(k, jnp.clip(code, 0, known - 1))
                if solved_ref is not None:
                    picked = jnp.where(code >= known, solved_ref[jnp.maximum(code - known, 0)], picked)
                xs.append((picked.astype(jnp.float32) * kept).astype(jnp.bfloat16))
                group.append(blocks[k])
            part = nt_dot(jnp.concatenate(xs, axis=1), jnp.concatenate(group, axis=1))
            total = part if total is None else total + part
        out_ref[r] = total


def first_kernel(code_ref, *refs):
    sources, refs = refs[:-7], refs[-7:]
    own_ref, other_ref, out_ref, store_ref, blocks, block_sems, store_sems = refs
    keeps, starts, known = [], [], 0
    for i, source in enumerate(sources):
        target = store_ref.at[pl.ds(known, source.shape[0])]
        keeps.append(pltpu.make_async_copy(source, target, store_sems.at[i]))
        starts.append(known)
        known += source.shape[0]

    def between():
        for keep in keeps:
            keep.start()

    def picks(k, code):
        value = None
        for start, source in zip(starts, sources):
            one = source[jnp.clip(code - start, 0, source.shape[0] - 1)]
            value = one if value is None else jnp.where(code >= start, one, value)
        return value

    gather_sum(1, code_ref, picks, known, None, own_ref, other_ref, out_ref, blocks, block_sems, between)
    for keep in keeps:
        keep.wait()


def old_kernel(level, known, code_ref, fresh_ref, store_ref, *refs):
    solved, refs = refs[: level - 2], refs[level - 2 :]
    own_ref, other_ref, out_ref, list_ref, near_ref, blocks, block_sems, picked, pick_sem = refs[:9]
    solved_ref = refs[9] if solved else None
    slots = code_ref.shape[1]

    def between():
        for k in range(slots):
            place = jnp.clip(code_ref[level - 1, k], 0, known - 1)
            pltpu.make_async_copy(store_ref.at[place], picked.at[k], pick_sem).start()
        for i, one in enumerate(solved):
            solved_ref[i * one.shape[0] : (i + 1) * one.shape[0]] = one[...]
        pltpu.make_async_copy(store_ref.at[pl.ds(0, slots)], picked, pick_sem).wait()

    picks = lambda k, code: picked[k]
    gather_sum(level, code_ref, picks, known, solved_ref, own_ref, other_ref, out_ref, blocks, block_sems, between)

    def note(slot, count):
        code = fresh_ref[level - 1, slot]

        @pl.when(code >= 0)
        def _():
            list_ref[1 + count] = code * 1024 + slot

        @pl.when((code >= 0) & (count < NEAR))
        def _():
            near_ref[count] = blocks[slot]

        return count + (code >= 0).astype(jnp.int32)

    list_ref[0] = lax.fori_loop(0, fresh_ref.shape[1], note, jnp.int32(0))


def sum_call(kernel, codes, sources, source_spaces, own, other, outs, out_spaces, extra, name, limit):
    slots, (rhs_cols, block) = codes[0].shape[1], sources[0].shape[-2:]
    return pl.pallas_call(
        kernel,
        out_shape=[jax.ShapeDtypeStruct((2, rhs_cols, block), jnp.float32)] + outs,
        in_specs=[pl.BlockSpec(memory_space=pltpu.SMEM)] * len(codes)
        + [pl.BlockSpec(memory_space=space) for space in source_spaces]
        + [pl.BlockSpec(memory_space=pltpu.HBM)] * 2,
        out_specs=[pl.BlockSpec(memory_space=space) for space in [pltpu.VMEM] + out_spaces],
        scratch_shapes=[pltpu.VMEM((slots, block, block), jnp.bfloat16), pltpu.SemaphoreType.DMA((2,))] + extra,
        compiler_params=pltpu.CompilerParams(vmem_limit_bytes=limit),
        cost_estimate=pl.CostEstimate(
            flops=2 * slots * rhs_cols * block * block,
            bytes_accessed=slots * block * (block + 2 * rhs_cols) * 4,
            transcendentals=0,
        ),
        name=name,
    )(*codes, *sources, own, other)


def first_sum(code, sources, own, other):
    store = jax.ShapeDtypeStruct((2048,) + sources[0].shape[1:], jnp.bfloat16)
    extra = [pltpu.SemaphoreType.DMA((len(sources),))]
    spaces = [pltpu.VMEM] * len(sources)
    return sum_call(first_kernel, [code], sources, spaces, own, other, [store], [pltpu.HBM], extra, "first_sum", VMEM_LIMIT)


def old_sum(level, known, code, fresh, store, solved, own, other):
    one = store.shape[1:]
    outs = [
        jax.ShapeDtypeStruct((code.shape[1] + 1,), jnp.int32),
        jax.ShapeDtypeStruct((NEAR, one[1], one[1]), jnp.bfloat16),
    ]
    kernel = functools.partial(old_kernel, level, known)
    extra = [pltpu.VMEM((code.shape[1],) + one, jnp.bfloat16), pltpu.SemaphoreType.DMA]
    if solved:
        extra.append(pltpu.VMEM((sum(v.shape[0] for v in solved),) + one, jnp.bfloat16))
    spaces = [pl.ANY] + [pltpu.VMEM] * len(solved)
    out_spaces = [pltpu.SMEM, pltpu.VMEM]
    return sum_call(kernel, [code, fresh], [store] + solved, spaces, own, other, outs, out_spaces, extra, "old_sum", VMEM_LIMIT)


def fresh_kernel(level, list_ref, old_ref, x_ref, near_ref, own_ref, other_ref, out_ref, far, sem):
    per_row = own_ref.shape[2]
    out_ref[...] = old_ref[...]
    count = list_ref[0]

    def add(block, entry):
        row = ((entry & 1023) >= per_row).astype(jnp.int32)
        out_ref[row] += nt_dot(x_ref[entry >> 10], block)

    def add_near(n, carry):
        add(near_ref[n], list_ref[1 + n])
        return carry

    def add_far(n, carry):
        slot = list_ref[1 + n] & 1023

        @pl.when(slot < per_row)
        def _():
            pltpu.make_async_copy(own_ref.at[level - 1, 0, slot], far, sem).start()

        @pl.when(slot >= per_row)
        def _():
            pltpu.make_async_copy(other_ref.at[level - 1, 0, slot - per_row], far, sem).start()

        pltpu.make_async_copy(own_ref.at[level - 1, 0, 0], far, sem).wait()
        add(far[...], list_ref[1 + n])
        return carry

    lax.fori_loop(0, jnp.minimum(count, NEAR), add_near, 0)
    lax.fori_loop(NEAR, count, add_far, 0)


def fresh_sum(level, listed, solved, old, near, own, other):
    block = solved.shape[-1]
    vmem = pl.BlockSpec(memory_space=pltpu.VMEM)
    return pl.pallas_call(
        functools.partial(fresh_kernel, level),
        out_shape=jax.ShapeDtypeStruct(old.shape, jnp.float32),
        in_specs=[pl.BlockSpec(memory_space=pltpu.SMEM)] + [vmem] * 3 + [pl.BlockSpec(memory_space=pltpu.HBM)] * 2,
        out_specs=vmem,
        scratch_shapes=[
            pltpu.VMEM((block, block), jnp.bfloat16),
            pltpu.SemaphoreType.DMA,
        ],
        compiler_params=pltpu.CompilerParams(vmem_limit_bytes=VMEM_LIMIT),
        name="fresh_sum",
    )(listed, old, solved, near, own, other)


def solve_kernel(level, p0, p1, p2, p3, rhs_ref, own_d_ref, other_d_ref, out_ref, *refs):
    core = lax.axis_index("core")
    for r, d_ref in enumerate((own_d_ref, other_d_ref)):
        coupled = (p0[r] + p1[r]) + (p2[r] + p3[r])
        reduced = (rhs_ref[level, r].astype(jnp.float32) - coupled).astype(jnp.bfloat16)
        solved = nt_dot(reduced, d_ref[level, 0]).astype(jnp.bfloat16)
        out_ref[r] = solved
        if refs:
            for i in range(refs[1].shape[0]):
                refs[1][i, core ^ r] = solved
    if refs:
        all_ref, copies, sem = refs
        send = pltpu.make_async_copy(copies, all_ref, sem)
        send.start()
        send.wait()


def solve_level(level, partials, rhs, own_d, other_d, copies):
    _, rhs_cols, block = partials[0].shape
    vmem = pl.BlockSpec(memory_space=pltpu.VMEM)
    out_shape, out_specs, scratch = [jax.ShapeDtypeStruct((2, rhs_cols, block), jnp.bfloat16)], [vmem], []
    if copies:
        out_shape.append(jax.ShapeDtypeStruct((copies, 2, rhs_cols, block), jnp.bfloat16))
        out_specs.append(pl.BlockSpec(memory_space=pltpu.HBM))
        scratch = [pltpu.VMEM((copies, 2, rhs_cols, block), jnp.bfloat16), pltpu.SemaphoreType.DMA]
    return pl.pallas_call(
        functools.partial(solve_kernel, level),
        out_shape=out_shape,
        in_specs=[vmem] * 7,
        out_specs=out_specs,
        scratch_shapes=scratch,
        compiler_params=pltpu.CompilerParams(vmem_limit_bytes=VMEM_LIMIT),
        name="solve_level",
    )(*partials, rhs, own_d, other_d)


def on_device(rhs, boundary, diag_inv, off_blocks, coupling, present):
    levels, _, rhs_cols, block = rhs.shape
    outer_each = boundary.shape[0]
    outer = outer_each * 32
    half = rhs_cols // 2
    z, y, core = lax.axis_index("z"), lax.axis_index("y"), lax.axis_index("core")

    def my_half(v, axis):
        return lax.dynamic_slice_in_dim(v, core * half, half, axis)

    def their_half(v, axis):
        return lax.dynamic_slice_in_dim(v, (1 - core) * half, half, axis)

    first = jnp.einsum("rb,ab->ra", rhs[0, 0], diag_inv[0, 0], preferred_element_type=jnp.float32).astype(jnp.bfloat16)
    known = jnp.concatenate([boundary, first[None]])
    known = jnp.stack([my_half(known, 1), their_half(known, 1)])
    code_own = (coupling + 1024 * present)[:, 0]
    code_both = jnp.stack([code_own, swap_cores(code_own)], axis=1)
    diag_other = swap_cores(diag_inv)
    off_sent, known = lax.optimization_barrier((off_blocks, known))
    off_other = swap_cores(off_sent)

    pieces = [piece.reshape((-1,) + piece.shape[2:]) for piece in gather_parts(known)]

    keep, index = code_both >= 1024, code_both % 1024
    in_outer = index < outer
    row = jnp.where(in_outer, index // outer_each, index - outer)
    member = jnp.where(in_outer, index % outer_each, outer_each)
    src_z, src_y, src_core = row // 8, (row // 2) % 4, row % 2
    each = outer_each + 1
    away = jnp.where(src_core == 0, src_y - y, src_z - z) % 4
    part = jnp.where(away == 3, 1, jnp.where(away == 1, 2, jnp.where(away == 2, 3, 0))) * 4
    part = part + jnp.where(src_core == 0, src_z ^ z, src_y ^ y) + jnp.where(src_core == core, 0, 16)
    known_place = part * each + member
    level_of = jnp.maximum(index - outer, 0) // 32
    this = jnp.arange(levels - 1)[:, None, None]
    is_fresh = (level_of == this) & (level_of > 0)
    place_level = (index - outer) % 32
    old_code = jnp.where(level_of == 0, known_place, 32 * each + (level_of - 1) * 32 + place_level)
    old_code = jnp.where(keep & ~is_fresh, old_code, -1).reshape(levels - 1, -1)
    fresh_code = jnp.where(keep & is_fresh, place_level, -1).reshape(levels - 1, -1)

    own_rows, other_rows = [], []
    value, store = first_sum(old_code, pieces, off_blocks, off_other)
    solved_levels = []
    rhs_late, value = lax.optimization_barrier((rhs, value))
    rhs_both = jnp.concatenate([my_half(rhs_late, 2), swap_cores(their_half(rhs_late, 2))], axis=1)
    for level in range(1, levels):
        partials = [value] + [lax.ppermute(value, "x", xor_pairs(4, k)) for k in (1, 2, 3)]
        last = level == levels - 1
        outs = solve_level(level, partials, rhs_both, diag_inv, diag_other, 0 if last else 16)
        own_rows.append(outs[0][0])
        other_rows.append(outs[0][1])
        if not last:
            next_fresh, sent = lax.optimization_barrier((fresh_code, outs[1]))
            solved = lax.all_to_all(sent, ("z", "y"), 0, 0).reshape(32, half, block)
            old, listed, near = old_sum(
                level + 1, 32 * each, old_code, next_fresh, store, solved_levels, off_blocks, off_other
            )
            value = fresh_sum(level + 1, listed, solved, old, near, off_blocks, off_other)
            solved_levels = solved_levels + [solved]

    mine = jnp.stack(own_rows)
    theirs = swap_cores(jnp.stack(other_rows))
    low = jnp.where(core == 0, mine, theirs)
    high = jnp.where(core == 0, theirs, mine)
    rest = jnp.concatenate([low, high], axis=1)
    return jnp.concatenate([first[None], rest])[:, None]


def solution(mesh):
    split = Mesh(mesh.devices.reshape(4, 4, 2, 4), ("z", "y", "core", "x"))
    in_specs = (
        P(None, ROWS, None, None),
        P(ROWS, None, None),
        P(None, ROWS, None, None),
        P(None, ROWS, "x", None, None),
        P(None, ROWS, "x"),
        P(None, ROWS, "x"),
    )
    return jax.shard_map(
        on_device, mesh=split, in_specs=in_specs, out_specs=P(None, ROWS, None, None), check_vma=False
    )
```

```python
import functools

import jax
import jax.numpy as jnp
from jax import lax
from jax.experimental import pallas as pl
from jax.experimental.pallas import tpu as pltpu
from jax.sharding import Mesh, PartitionSpec as P

ROWS = ("z", "y", "core")
VMEM_LIMIT = 48 * 1024 * 1024


def xor_pairs(n, k):
    return [(i, i ^ k) for i in range(n)]


def shift_pairs(n, k):
    return [(i, (i + k) % n) for i in range(n)]


def swap_cores(v):
    return lax.ppermute(v, "core", xor_pairs(2, 1))


def pairs(stage, move, cross=False):
    result = []
    for z in range(4):
        for y in range(4):
            for core in range(2):
                to_z, to_y = (move(z), y) if core + 1 == stage else (z, move(y))
                to_core = 1 - core if cross else core
                result.append(((z * 4 + y) * 2 + core, (to_z * 4 + to_y) * 2 + to_core))
    return result


def gather_parts(v):
    after_one, before_one = lambda i: (i + 1) % 4, lambda i: (i + 3) % 4
    near = [v] + [lax.ppermute(v, ROWS, pairs(1, lambda i, k=k: i ^ k)) for k in (2, 3, 1)]
    mine, theirs = jnp.stack([one[0] for one in near]), jnp.stack([one[1] for one in near])

    def spread(part, cross):
        again = 1 if cross else 2
        before = lax.ppermute(part, ROWS, pairs(2, after_one, cross))
        after = lax.ppermute(part, ROWS, pairs(2, before_one, cross))
        far_low = lax.ppermute(before[:2], ROWS, pairs(again, after_one))
        far_high = lax.ppermute(after[2:], ROWS, pairs(again, before_one))
        return [before, after, far_low, far_high]

    return [mine, *spread(mine, False), swap_cores(theirs), *spread(theirs, True)]


def nt_dot(x, a):
    return lax.dot_general(x, a, (((1,), (1,)), ((), ())), preferred_element_type=jnp.float32)


GROUP = 8
NEAR = 16


def gather_sum(level, code_ref, picks, known, solved_ref, own_ref, other_ref, out_ref, blocks, block_sems, between):
    slots = code_ref.shape[1]
    per_row = slots // 2
    loads = [
        pltpu.make_async_copy(a_ref.at[level - 1, 0], blocks.at[pl.ds(r * per_row, per_row)], block_sems.at[r])
        for r, a_ref in enumerate((own_ref, other_ref))
    ]
    for load in loads:
        load.start()
    between()
    for r in range(2):
        loads[r].wait()
        total = None
        for g in range(r * per_row, (r + 1) * per_row, GROUP):
            xs, group = [], []
            for k in range(g, g + GROUP):
                code = code_ref[level - 1, k]
                kept = (code >= 0).astype(jnp.float32)
                picked = picks(k, jnp.clip(code, 0, known - 1))
                if solved_ref is not None:
                    picked = jnp.where(code >= known, solved_ref[jnp.maximum(code - known, 0)], picked)
                xs.append((picked.astype(jnp.float32) * kept).astype(jnp.bfloat16))
                group.append(blocks[k])
            part = nt_dot(jnp.concatenate(xs, axis=1), jnp.concatenate(group, axis=1))
            total = part if total is None else total + part
        out_ref[r] = total


def first_kernel(code_ref, *refs):
    sources, refs = refs[:-7], refs[-7:]
    own_ref, other_ref, out_ref, store_ref, blocks, block_sems, store_sems = refs
    keeps, starts, known = [], [], 0
    for i, source in enumerate(sources):
        target = store_ref.at[pl.ds(known, source.shape[0])]
        keeps.append(pltpu.make_async_copy(source, target, store_sems.at[i]))
        starts.append(known)
        known += source.shape[0]

    def between():
        for keep in keeps:
            keep.start()

    def picks(k, code):
        value = None
        for start, source in zip(starts, sources):
            one = source[jnp.clip(code - start, 0, source.shape[0] - 1)]
            value = one if value is None else jnp.where(code >= start, one, value)
        return value

    gather_sum(1, code_ref, picks, known, None, own_ref, other_ref, out_ref, blocks, block_sems, between)
    for keep in keeps:
        keep.wait()


def old_kernel(level, known, code_ref, fresh_ref, store_ref, *refs):
    solved, refs = refs[: level - 2], refs[level - 2 :]
    own_ref, other_ref, out_ref, list_ref, near_ref, blocks, block_sems, picked, pick_sem = refs[:9]
    solved_ref = refs[9] if solved else None
    slots = code_ref.shape[1]

    def between():
        for k in range(slots):
            place = jnp.clip(code_ref[level - 1, k], 0, known - 1)
            pltpu.make_async_copy(store_ref.at[place], picked.at[k], pick_sem).start()
        for i, one in enumerate(solved):
            solved_ref[i * one.shape[0] : (i + 1) * one.shape[0]] = one[...]
        pltpu.make_async_copy(store_ref.at[pl.ds(0, slots)], picked, pick_sem).wait()

    picks = lambda k, code: picked[k]
    gather_sum(level, code_ref, picks, known, solved_ref, own_ref, other_ref, out_ref, blocks, block_sems, between)

    def note(slot, count):
        code = fresh_ref[level - 1, slot]

        @pl.when(code >= 0)
        def _():
            list_ref[1 + count] = code * 1024 + slot

        @pl.when((code >= 0) & (count < NEAR))
        def _():
            near_ref[count] = blocks[slot]

        return count + (code >= 0).astype(jnp.int32)

    list_ref[0] = lax.fori_loop(0, fresh_ref.shape[1], note, jnp.int32(0))


def sum_call(kernel, codes, sources, source_spaces, own, other, outs, out_spaces, extra, name, limit):
    slots, (rhs_cols, block) = codes[0].shape[1], sources[0].shape[-2:]
    return pl.pallas_call(
        kernel,
        out_shape=[jax.ShapeDtypeStruct((2, rhs_cols, block), jnp.float32)] + outs,
        in_specs=[pl.BlockSpec(memory_space=pltpu.SMEM)] * len(codes)
        + [pl.BlockSpec(memory_space=space) for space in source_spaces]
        + [pl.BlockSpec(memory_space=pltpu.HBM)] * 2,
        out_specs=[pl.BlockSpec(memory_space=space) for space in [pltpu.VMEM] + out_spaces],
        scratch_shapes=[pltpu.VMEM((slots, block, block), jnp.bfloat16), pltpu.SemaphoreType.DMA((2,))] + extra,
        compiler_params=pltpu.CompilerParams(vmem_limit_bytes=limit),
        cost_estimate=pl.CostEstimate(
            flops=2 * slots * rhs_cols * block * block,
            bytes_accessed=slots * block * (block + 2 * rhs_cols) * 4,
            transcendentals=0,
        ),
        name=name,
    )(*codes, *sources, own, other)


def first_sum(code, sources, own, other):
    store = jax.ShapeDtypeStruct((2048,) + sources[0].shape[1:], jnp.bfloat16)
    extra = [pltpu.SemaphoreType.DMA((len(sources),))]
    spaces = [pltpu.VMEM] * len(sources)
    return sum_call(first_kernel, [code], sources, spaces, own, other, [store], [pltpu.HBM], extra, "first_sum", VMEM_LIMIT)


def old_sum(level, known, code, fresh, store, solved, own, other):
    one = store.shape[1:]
    outs = [
        jax.ShapeDtypeStruct((code.shape[1] + 1,), jnp.int32),
        jax.ShapeDtypeStruct((NEAR, one[1], one[1]), jnp.bfloat16),
    ]
    kernel = functools.partial(old_kernel, level, known)
    extra = [pltpu.VMEM((code.shape[1],) + one, jnp.bfloat16), pltpu.SemaphoreType.DMA]
    if solved:
        extra.append(pltpu.VMEM((sum(v.shape[0] for v in solved),) + one, jnp.bfloat16))
    spaces = [pl.ANY] + [pltpu.VMEM] * len(solved)
    out_spaces = [pltpu.SMEM, pltpu.VMEM]
    return sum_call(kernel, [code, fresh], [store] + solved, spaces, own, other, outs, out_spaces, extra, "old_sum", VMEM_LIMIT)


def fresh_kernel(level, list_ref, old_ref, x_ref, near_ref, own_ref, other_ref, out_ref, far, sem):
    per_row = own_ref.shape[2]
    out_ref[...] = old_ref[...]
    count = list_ref[0]

    def add(block, entry):
        row = ((entry & 1023) >= per_row).astype(jnp.int32)
        out_ref[row] += nt_dot(x_ref[entry >> 10], block)

    def add_near(n, carry):
        add(near_ref[n], list_ref[1 + n])
        return carry

    def add_far(n, carry):
        slot = list_ref[1 + n] & 1023

        @pl.when(slot < per_row)
        def _():
            pltpu.make_async_copy(own_ref.at[level - 1, 0, slot], far, sem).start()

        @pl.when(slot >= per_row)
        def _():
            pltpu.make_async_copy(other_ref.at[level - 1, 0, slot - per_row], far, sem).start()

        pltpu.make_async_copy(own_ref.at[level - 1, 0, 0], far, sem).wait()
        add(far[...], list_ref[1 + n])
        return carry

    lax.fori_loop(0, jnp.minimum(count, NEAR), add_near, 0)
    lax.fori_loop(NEAR, count, add_far, 0)


def fresh_sum(level, listed, solved, old, near, own, other):
    block = solved.shape[-1]
    vmem = pl.BlockSpec(memory_space=pltpu.VMEM)
    return pl.pallas_call(
        functools.partial(fresh_kernel, level),
        out_shape=jax.ShapeDtypeStruct(old.shape, jnp.float32),
        in_specs=[pl.BlockSpec(memory_space=pltpu.SMEM)] + [vmem] * 3 + [pl.BlockSpec(memory_space=pltpu.HBM)] * 2,
        out_specs=vmem,
        scratch_shapes=[
            pltpu.VMEM((block, block), jnp.bfloat16),
            pltpu.SemaphoreType.DMA,
        ],
        compiler_params=pltpu.CompilerParams(vmem_limit_bytes=VMEM_LIMIT),
        name="fresh_sum",
    )(listed, old, solved, near, own, other)


def solve_kernel(level, p0, p1, p2, p3, rhs_ref, own_d_ref, other_d_ref, out_ref, *refs):
    core = lax.axis_index("core")
    for r, d_ref in enumerate((own_d_ref, other_d_ref)):
        coupled = (p0[r] + p1[r]) + (p2[r] + p3[r])
        reduced = (rhs_ref[level, r].astype(jnp.float32) - coupled).astype(jnp.bfloat16)
        solved = nt_dot(reduced, d_ref[level, 0]).astype(jnp.bfloat16)
        out_ref[r] = solved
        if refs:
            for i in range(refs[1].shape[0]):
                refs[1][i, core ^ r] = solved
    if refs:
        all_ref, copies, sem = refs
        send = pltpu.make_async_copy(copies, all_ref, sem)
        send.start()
        send.wait()


def solve_level(level, partials, rhs, own_d, other_d, copies):
    _, rhs_cols, block = partials[0].shape
    vmem = pl.BlockSpec(memory_space=pltpu.VMEM)
    out_shape, out_specs, scratch = [jax.ShapeDtypeStruct((2, rhs_cols, block), jnp.bfloat16)], [vmem], []
    if copies:
        out_shape.append(jax.ShapeDtypeStruct((copies, 2, rhs_cols, block), jnp.bfloat16))
        out_specs.append(pl.BlockSpec(memory_space=pltpu.HBM))
        scratch = [pltpu.VMEM((copies, 2, rhs_cols, block), jnp.bfloat16), pltpu.SemaphoreType.DMA]
    return pl.pallas_call(
        functools.partial(solve_kernel, level),
        out_shape=out_shape,
        in_specs=[vmem] * 7,
        out_specs=out_specs,
        scratch_shapes=scratch,
        compiler_params=pltpu.CompilerParams(vmem_limit_bytes=VMEM_LIMIT),
        name="solve_level",
    )(*partials, rhs, own_d, other_d)


def on_device(rhs, boundary, diag_inv, off_blocks, coupling, present):
    levels, _, rhs_cols, block = rhs.shape
    outer_each = boundary.shape[0]
    outer = outer_each * 32
    half = rhs_cols // 2
    z, y, core = lax.axis_index("z"), lax.axis_index("y"), lax.axis_index("core")

    def my_half(v, axis):
        return lax.dynamic_slice_in_dim(v, core * half, half, axis)

    def their_half(v, axis):
        return lax.dynamic_slice_in_dim(v, (1 - core) * half, half, axis)

    first = jnp.einsum("rb,ab->ra", rhs[0, 0], diag_inv[0, 0], preferred_element_type=jnp.float32).astype(jnp.bfloat16)
    known = jnp.concatenate([boundary, first[None]])
    known = jnp.stack([my_half(known, 1), their_half(known, 1)])
    code_own = (coupling + 1024 * present)[:, 0]
    code_both = jnp.stack([code_own, swap_cores(code_own)], axis=1)
    diag_other = swap_cores(diag_inv)
    off_sent, known = lax.optimization_barrier((off_blocks, known))
    off_other = swap_cores(off_sent)

    pieces = [piece.reshape((-1,) + piece.shape[2:]) for piece in gather_parts(known)]

    keep, index = code_both >= 1024, code_both % 1024
    in_outer = index < outer
    row = jnp.where(in_outer, index // outer_each, index - outer)
    member = jnp.where(in_outer, index % outer_each, outer_each)
    src_z, src_y, src_core = row // 8, (row // 2) % 4, row % 2
    each = outer_each + 1
    away = jnp.where(src_core == 0, src_y - y, src_z - z) % 4
    part = jnp.where(away == 3, 1, jnp.where(away == 1, 2, jnp.where(away == 2, 3, 0))) * 4
    apart = jnp.where(src_core == 0, src_z ^ z, src_y ^ y)
    part = part + jnp.where(apart == 0, 0, jnp.where(apart == 1, 3, apart - 1)) + jnp.where(src_core == core, 0, 16)
    known_place = part * each + member
    level_of = jnp.maximum(index - outer, 0) // 32
    this = jnp.arange(levels - 1)[:, None, None]
    is_fresh = (level_of == this) & (level_of > 0)
    place_level = (index - outer) % 32
    old_code = jnp.where(level_of == 0, known_place, 32 * each + (level_of - 1) * 32 + place_level)
    old_code = jnp.where(keep & ~is_fresh, old_code, -1).reshape(levels - 1, -1)
    fresh_code = jnp.where(keep & is_fresh, place_level, -1).reshape(levels - 1, -1)

    own_rows, other_rows = [], []
    value, store = first_sum(old_code, pieces, off_blocks, off_other)
    solved_levels = []
    rhs_late, value = lax.optimization_barrier((rhs, value))
    rhs_both = jnp.concatenate([my_half(rhs_late, 2), swap_cores(their_half(rhs_late, 2))], axis=1)
    for level in range(1, levels):
        partials = [value] + [lax.ppermute(value, "x", xor_pairs(4, k)) for k in (1, 2, 3)]
        last = level == levels - 1
        outs = solve_level(level, partials, rhs_both, diag_inv, diag_other, 0 if last else 16)
        own_rows.append(outs[0][0])
        other_rows.append(outs[0][1])
        if not last:
            next_fresh, sent = lax.optimization_barrier((fresh_code, outs[1]))
            solved = lax.all_to_all(sent, ("z", "y"), 0, 0).reshape(32, half, block)
            old, listed, near = old_sum(
                level + 1, 32 * each, old_code, next_fresh, store, solved_levels, off_blocks, off_other
            )
            value = fresh_sum(level + 1, listed, solved, old, near, off_blocks, off_other)
            solved_levels = solved_levels + [solved]

    mine = jnp.stack(own_rows)
    theirs = swap_cores(jnp.stack(other_rows))
    low = jnp.where(core == 0, mine, theirs)
    high = jnp.where(core == 0, theirs, mine)
    rest = jnp.concatenate([low, high], axis=1)
    return jnp.concatenate([first[None], rest])[:, None]


def solution(mesh):
    split = Mesh(mesh.devices.reshape(4, 4, 2, 4), ("z", "y", "core", "x"))
    in_specs = (
        P(None, ROWS, None, None),
        P(ROWS, None, None),
        P(None, ROWS, None, None),
        P(None, ROWS, "x", None, None),
        P(None, ROWS, "x"),
        P(None, ROWS, "x"),
    )
    return jax.shard_map(
        on_device, mesh=split, in_specs=in_specs, out_specs=P(None, ROWS, None, None), check_vma=False
    )
```

```python
import functools

import jax
import jax.numpy as jnp
from jax import lax
from jax.experimental import pallas as pl
from jax.experimental.pallas import tpu as pltpu
from jax.sharding import Mesh, PartitionSpec as P

ROWS = ("z", "y", "core")
VMEM_LIMIT = 48 * 1024 * 1024


def xor_pairs(n, k):
    return [(i, i ^ k) for i in range(n)]


def shift_pairs(n, k):
    return [(i, (i + k) % n) for i in range(n)]


def swap_cores(v):
    return lax.ppermute(v, "core", xor_pairs(2, 1))


def pairs(stage, move, cross=False):
    result = []
    for z in range(4):
        for y in range(4):
            for core in range(2):
                to_z, to_y = (move(z), y) if core + 1 == stage else (z, move(y))
                to_core = 1 - core if cross else core
                result.append(((z * 4 + y) * 2 + core, (to_z * 4 + to_y) * 2 + to_core))
    return result


def gather_parts(v):
    after_one, before_one = lambda i: (i + 1) % 4, lambda i: (i + 3) % 4
    near = [v] + [lax.ppermute(v, ROWS, pairs(1, lambda i, k=k: i ^ k)) for k in (2, 3, 1)]
    mine, theirs = jnp.stack([one[0] for one in near]), jnp.stack([one[1] for one in near])

    def spread(part, cross):
        again = 1 if cross else 2
        before = lax.ppermute(part, ROWS, pairs(2, after_one, cross))
        after = lax.ppermute(part, ROWS, pairs(2, before_one, cross))
        far_low = lax.ppermute(before[:2], ROWS, pairs(again, after_one))
        far_high = lax.ppermute(after[2:], ROWS, pairs(again, before_one))
        return [before, after, far_low, far_high]

    return [mine, *spread(mine, False), swap_cores(theirs), *spread(theirs, True)]


def nt_dot(x, a):
    return lax.dot_general(x, a, (((1,), (1,)), ((), ())), preferred_element_type=jnp.float32)


GROUP = 8
NEAR = 16


def gather_sum(level, code_ref, picks, known, solved_ref, own_ref, other_ref, out_ref, blocks, block_sems, between):
    slots = code_ref.shape[1]
    per_row = slots // 2
    loads = [
        pltpu.make_async_copy(a_ref.at[level - 1, 0], blocks.at[pl.ds(r * per_row, per_row)], block_sems.at[r])
        for r, a_ref in enumerate((own_ref, other_ref))
    ]
    for load in loads:
        load.start()
    between()
    for r in range(2):
        loads[r].wait()
        total = None
        for g in range(r * per_row, (r + 1) * per_row, GROUP):
            xs, group = [], []
            for k in range(g, g + GROUP):
                code = code_ref[level - 1, k]
                kept = (code >= 0).astype(jnp.float32)
                picked = picks(k, jnp.clip(code, 0, known - 1))
                if solved_ref is not None:
                    picked = jnp.where(code >= known, solved_ref[jnp.maximum(code - known, 0)], picked)
                xs.append((picked.astype(jnp.float32) * kept).astype(jnp.bfloat16))
                group.append(blocks[k])
            part = nt_dot(jnp.concatenate(xs, axis=1), jnp.concatenate(group, axis=1))
            total = part if total is None else total + part
        out_ref[r] = total


def first_kernel(code_ref, *refs):
    sources, refs = refs[:-7], refs[-7:]
    own_ref, other_ref, out_ref, store_ref, blocks, block_sems, store_sems = refs
    keeps, starts, known = [], [], 0
    for i, source in enumerate(sources):
        target = store_ref.at[pl.ds(known, source.shape[0])]
        keeps.append(pltpu.make_async_copy(source, target, store_sems.at[i]))
        starts.append(known)
        known += source.shape[0]

    def between():
        for keep in keeps:
            keep.start()

    def picks(k, code):
        value = None
        for start, source in zip(starts, sources):
            one = source[jnp.clip(code - start, 0, source.shape[0] - 1)]
            value = one if value is None else jnp.where(code >= start, one, value)
        return value

    gather_sum(1, code_ref, picks, known, None, own_ref, other_ref, out_ref, blocks, block_sems, between)
    for keep in keeps:
        keep.wait()


def old_kernel(level, known, code_ref, fresh_ref, store_ref, *refs):
    solved, refs = refs[: level - 2], refs[level - 2 :]
    own_ref, other_ref, out_ref, list_ref, near_ref, blocks, block_sems, picked, pick_sem = refs[:9]
    solved_ref = refs[9] if solved else None
    slots = code_ref.shape[1]

    def between():
        for k in range(slots):
            place = jnp.clip(code_ref[level - 1, k], 0, known - 1)
            pltpu.make_async_copy(store_ref.at[place], picked.at[k], pick_sem).start()
        for i, one in enumerate(solved):
            solved_ref[i * one.shape[0] : (i + 1) * one.shape[0]] = one[...]
        pltpu.make_async_copy(store_ref.at[pl.ds(0, slots)], picked, pick_sem).wait()

    picks = lambda k, code: picked[k]
    gather_sum(level, code_ref, picks, known, solved_ref, own_ref, other_ref, out_ref, blocks, block_sems, between)

    def note(slot, count):
        code = fresh_ref[level - 1, slot]

        @pl.when(code >= 0)
        def _():
            list_ref[1 + count] = code * 1024 + slot

        @pl.when((code >= 0) & (count < NEAR))
        def _():
            near_ref[count] = blocks[slot]

        return count + (code >= 0).astype(jnp.int32)

    list_ref[0] = lax.fori_loop(0, fresh_ref.shape[1], note, jnp.int32(0))


def sum_call(kernel, codes, sources, source_spaces, own, other, outs, out_spaces, extra, name, limit):
    slots, (rhs_cols, block) = codes[0].shape[1], sources[0].shape[-2:]
    return pl.pallas_call(
        kernel,
        out_shape=[jax.ShapeDtypeStruct((2, rhs_cols, block), jnp.float32)] + outs,
        in_specs=[pl.BlockSpec(memory_space=pltpu.SMEM)] * len(codes)
        + [pl.BlockSpec(memory_space=space) for space in source_spaces]
        + [pl.BlockSpec(memory_space=pltpu.HBM)] * 2,
        out_specs=[pl.BlockSpec(memory_space=space) for space in [pltpu.VMEM] + out_spaces],
        scratch_shapes=[pltpu.VMEM((slots, block, block), jnp.bfloat16), pltpu.SemaphoreType.DMA((2,))] + extra,
        compiler_params=pltpu.CompilerParams(vmem_limit_bytes=limit),
        cost_estimate=pl.CostEstimate(
            flops=2 * slots * rhs_cols * block * block,
            bytes_accessed=slots * block * (block + 2 * rhs_cols) * 4,
            transcendentals=0,
        ),
        name=name,
    )(*codes, *sources, own, other)


def first_sum(code, sources, own, other):
    store = jax.ShapeDtypeStruct((2048,) + sources[0].shape[1:], jnp.bfloat16)
    extra = [pltpu.SemaphoreType.DMA((len(sources),))]
    spaces = [pltpu.VMEM] * len(sources)
    return sum_call(first_kernel, [code], sources, spaces, own, other, [store], [pltpu.HBM], extra, "first_sum", 54 * 1024 * 1024)


def old_sum(level, known, code, fresh, store, solved, own, other):
    one = store.shape[1:]
    outs = [
        jax.ShapeDtypeStruct((code.shape[1] + 1,), jnp.int32),
        jax.ShapeDtypeStruct((NEAR, one[1], one[1]), jnp.bfloat16),
    ]
    kernel = functools.partial(old_kernel, level, known)
    extra = [pltpu.VMEM((code.shape[1],) + one, jnp.bfloat16), pltpu.SemaphoreType.DMA]
    if solved:
        extra.append(pltpu.VMEM((sum(v.shape[0] for v in solved),) + one, jnp.bfloat16))
    spaces = [pl.ANY] + [pltpu.VMEM] * len(solved)
    out_spaces = [pltpu.SMEM, pltpu.VMEM]
    return sum_call(kernel, [code, fresh], [store] + solved, spaces, own, other, outs, out_spaces, extra, "old_sum", VMEM_LIMIT)


def fresh_kernel(level, list_ref, old_ref, x_ref, near_ref, own_ref, other_ref, out_ref, far, sem):
    per_row = own_ref.shape[2]
    out_ref[...] = old_ref[...]
    count = list_ref[0]

    def add(block, entry):
        row = ((entry & 1023) >= per_row).astype(jnp.int32)
        out_ref[row] += nt_dot(x_ref[entry >> 10], block)

    def add_near(n, carry):
        add(near_ref[n], list_ref[1 + n])
        return carry

    def add_far(n, carry):
        slot = list_ref[1 + n] & 1023

        @pl.when(slot < per_row)
        def _():
            pltpu.make_async_copy(own_ref.at[level - 1, 0, slot], far, sem).start()

        @pl.when(slot >= per_row)
        def _():
            pltpu.make_async_copy(other_ref.at[level - 1, 0, slot - per_row], far, sem).start()

        pltpu.make_async_copy(own_ref.at[level - 1, 0, 0], far, sem).wait()
        add(far[...], list_ref[1 + n])
        return carry

    lax.fori_loop(0, jnp.minimum(count, NEAR), add_near, 0)
    lax.fori_loop(NEAR, count, add_far, 0)


def fresh_sum(level, listed, solved, old, near, own, other):
    block = solved.shape[-1]
    vmem = pl.BlockSpec(memory_space=pltpu.VMEM)
    return pl.pallas_call(
        functools.partial(fresh_kernel, level),
        out_shape=jax.ShapeDtypeStruct(old.shape, jnp.float32),
        in_specs=[pl.BlockSpec(memory_space=pltpu.SMEM)] + [vmem] * 3 + [pl.BlockSpec(memory_space=pltpu.HBM)] * 2,
        out_specs=vmem,
        scratch_shapes=[
            pltpu.VMEM((block, block), jnp.bfloat16),
            pltpu.SemaphoreType.DMA,
        ],
        compiler_params=pltpu.CompilerParams(vmem_limit_bytes=VMEM_LIMIT),
        name="fresh_sum",
    )(listed, old, solved, near, own, other)


def solve_kernel(level, p0, p1, p2, p3, rhs_ref, own_d_ref, other_d_ref, out_ref, *refs):
    core = lax.axis_index("core")
    for r, d_ref in enumerate((own_d_ref, other_d_ref)):
        coupled = (p0[r] + p1[r]) + (p2[r] + p3[r])
        reduced = (rhs_ref[level, r].astype(jnp.float32) - coupled).astype(jnp.bfloat16)
        solved = nt_dot(reduced, d_ref[level, 0]).astype(jnp.bfloat16)
        out_ref[r] = solved
        if refs:
            for i in range(refs[1].shape[0]):
                refs[1][i, core ^ r] = solved
    if refs:
        all_ref, copies, sem = refs
        send = pltpu.make_async_copy(copies, all_ref, sem)
        send.start()
        send.wait()


def solve_level(level, partials, rhs, own_d, other_d, copies):
    _, rhs_cols, block = partials[0].shape
    vmem = pl.BlockSpec(memory_space=pltpu.VMEM)
    out_shape, out_specs, scratch = [jax.ShapeDtypeStruct((2, rhs_cols, block), jnp.bfloat16)], [vmem], []
    if copies:
        out_shape.append(jax.ShapeDtypeStruct((copies, 2, rhs_cols, block), jnp.bfloat16))
        out_specs.append(pl.BlockSpec(memory_space=pltpu.HBM))
        scratch = [pltpu.VMEM((copies, 2, rhs_cols, block), jnp.bfloat16), pltpu.SemaphoreType.DMA]
    return pl.pallas_call(
        functools.partial(solve_kernel, level),
        out_shape=out_shape,
        in_specs=[vmem] * 7,
        out_specs=out_specs,
        scratch_shapes=scratch,
        compiler_params=pltpu.CompilerParams(vmem_limit_bytes=VMEM_LIMIT),
        name="solve_level",
    )(*partials, rhs, own_d, other_d)


def on_device(rhs, boundary, diag_inv, off_blocks, coupling, present):
    levels, _, rhs_cols, block = rhs.shape
    outer_each = boundary.shape[0]
    outer = outer_each * 32
    half = rhs_cols // 2
    z, y, core = lax.axis_index("z"), lax.axis_index("y"), lax.axis_index("core")

    def my_half(v, axis):
        return lax.dynamic_slice_in_dim(v, core * half, half, axis)

    def their_half(v, axis):
        return lax.dynamic_slice_in_dim(v, (1 - core) * half, half, axis)

    first = jnp.einsum("rb,ab->ra", rhs[0, 0], diag_inv[0, 0], preferred_element_type=jnp.float32).astype(jnp.bfloat16)
    known = jnp.concatenate([boundary, first[None]])
    known = jnp.stack([my_half(known, 1), their_half(known, 1)])
    code_own = (coupling + 1024 * present)[:, 0]
    code_both = jnp.stack([code_own, swap_cores(code_own)], axis=1)
    diag_other = swap_cores(diag_inv)
    off_sent, known = lax.optimization_barrier((off_blocks, known))
    off_other = swap_cores(off_sent)

    pieces = [piece.reshape((-1,) + piece.shape[2:]) for piece in gather_parts(known)]

    keep, index = code_both >= 1024, code_both % 1024
    in_outer = index < outer
    row = jnp.where(in_outer, index // outer_each, index - outer)
    member = jnp.where(in_outer, index % outer_each, outer_each)
    src_z, src_y, src_core = row // 8, (row // 2) % 4, row % 2
    each = outer_each + 1
    away = jnp.where(src_core == 0, src_y - y, src_z - z) % 4
    part = jnp.where(away == 3, 1, jnp.where(away == 1, 2, jnp.where(away == 2, 3, 0))) * 4
    apart = jnp.where(src_core == 0, src_z ^ z, src_y ^ y)
    part = part + jnp.where(apart == 0, 0, jnp.where(apart == 1, 3, apart - 1)) + jnp.where(src_core == core, 0, 16)
    known_place = part * each + member
    level_of = jnp.maximum(index - outer, 0) // 32
    this = jnp.arange(levels - 1)[:, None, None]
    is_fresh = (level_of == this) & (level_of > 0)
    place_level = (index - outer) % 32
    old_code = jnp.where(level_of == 0, known_place, 32 * each + (level_of - 1) * 32 + place_level)
    old_code = jnp.where(keep & ~is_fresh, old_code, -1).reshape(levels - 1, -1)
    fresh_code = jnp.where(keep & is_fresh, place_level, -1).reshape(levels - 1, -1)

    own_rows, other_rows = [], []
    value, store = first_sum(old_code, pieces, off_blocks, off_other)
    solved_levels = []
    rhs_late, value = lax.optimization_barrier((rhs, value))
    rhs_both = jnp.concatenate([my_half(rhs_late, 2), swap_cores(their_half(rhs_late, 2))], axis=1)
    for level in range(1, levels):
        partials = [value] + [lax.ppermute(value, "x", xor_pairs(4, k)) for k in (1, 2, 3)]
        last = level == levels - 1
        outs = solve_level(level, partials, rhs_both, diag_inv, diag_other, 0 if last else 16)
        own_rows.append(outs[0][0])
        other_rows.append(outs[0][1])
        if not last:
            next_fresh, sent = lax.optimization_barrier((fresh_code, outs[1]))
            solved = lax.all_to_all(sent, ("z", "y"), 0, 0).reshape(32, half, block)
            old, listed, near = old_sum(
                level + 1, 32 * each, old_code, next_fresh, store, solved_levels, off_blocks, off_other
            )
            value = fresh_sum(level + 1, listed, solved, old, near, off_blocks, off_other)
            solved_levels = solved_levels + [solved]

    mine = jnp.stack(own_rows)
    theirs = swap_cores(jnp.stack(other_rows))
    low = jnp.where(core == 0, mine, theirs)
    high = jnp.where(core == 0, theirs, mine)
    rest = jnp.concatenate([low, high], axis=1)
    return jnp.concatenate([first[None], rest])[:, None]


def solution(mesh):
    split = Mesh(mesh.devices.reshape(4, 4, 2, 4), ("z", "y", "core", "x"))
    in_specs = (
        P(None, ROWS, None, None),
        P(ROWS, None, None),
        P(None, ROWS, None, None),
        P(None, ROWS, "x", None, None),
        P(None, ROWS, "x"),
        P(None, ROWS, "x"),
    )
    return jax.shard_map(
        on_device, mesh=split, in_specs=in_specs, out_specs=P(None, ROWS, None, None), check_vma=False
    )
```
